512 devices in a mesh: gx: 8 (over y, core), gy: 4 (over x), gz: 16 (over z).
Axes of the slice: x: 4, y: 4, z: 16, core: 2. Of those that a mesh axis runs over, the one named last changes fastest.
Arguments:
- sph_pos: float32 [3, 8, 16, 8, 2048], P(None, None, 'gx', 'gy', 'gz'), may hold values from 0 to 1
- sph_vel: float32 [3, 8, 16, 8, 2048], P(None, None, 'gx', 'gy', 'gz'), may hold values from -4 to 4
- sph_mass: float32 [8, 16, 8, 2048], P(None, 'gx', 'gy', 'gz'), may hold values from 0.5 to 2
- cell_count: int32 [16, 8, 2048], P('gx', 'gy', 'gz'), may hold values from 1 to 8
- grain_pos: float32 [3, 2, 16, 8, 2048], P(None, None, 'gx', 'gy', 'gz'), may hold values from 0 to 1
- grain_vel: float32 [3, 2, 16, 8, 2048], P(None, None, 'gx', 'gy', 'gz'), may hold values from -3 to 3
- grain_radius: float32 [2, 16, 8, 2048], P(None, 'gx', 'gy', 'gz'), may hold values from 0.3 to 0.6
- contact_pairs: int32 [2, 8, 4, 98304], P(None, 'gx', 'gy', 'gz'), may hold values from 0 to 4159, as said below
- contact_count: int32 [8, 4, 16], P('gx', 'gy', 'gz'), may hold values from 3072 to 6144, as said below
- iface_grain: int32 [8, 4, 256, 128], P('gx', 'gy', 'gz'), may hold values from 0 to 1023
- iface_offset: float32 [3, 8, 4, 256, 128], P(None, 'gx', 'gy', 'gz'), may hold values from -0.25 to 1.25
- pair_count: int32 [8, 4, 256], P('gx', 'gy', 'gz'), may hold values from 0 to 128, as said below
- iface_cell: int32 [8, 4, 256, 128], P('gx', 'gy', 'gz'), may hold values from 0 to 511
Outputs:
- sph_accel: float32 [3, 8, 16, 8, 2048], P(None, None, 'gx', 'gy', 'gz')
- grain_force: float32 [3, 2, 16, 8, 2048], P(None, None, 'gx', 'gy', 'gz')
- grain_stress: float32 [6, 2, 16, 8, 2048], P(None, None, 'gx', 'gy', 'gz')
The draws below stay inside these ranges and needn't reach their ends.
Inputs may be any that keep to these rules, and one draw needn't show every extreme that they name: `contact_pairs`: row 0 names any grain of the brick; row 1 names a grain of the same or an adjacent grain cell in the extended brick, never grain i itself. `contact_count`: some brick is full in every draw. `pair_count`: in every brick column one water brick layer receives 128 live pairs from every grain brick layer.
All inputs are finite; a program needn't handle non-finite values.
Results may differ from the reference program's by a relative error of at most 0.0003.
Values sent between devices are 32-bit elements; how exact they have to be, the bound alone decides.
No kernel may reach another device: no remote copies, remote signals or barrier semaphores. Data moves between devices by JAX's collectives and lax.ppermute only.
A program may use at most 128 MiB of HBM per device.

```python
import math
import jax
import jax.numpy as jnp
from jax import lax

CAP = 8
CX = 2
CY = 2
CZ = 128
GCAP = 2
EX = 2
EY = 2
EZ = 128
CON_DEV = 6144
CAPX = 128
NX = 16
NY = 8
NZ = 2048
MX = 16
MY = 8
MZ = 2048
BX = 8
BY = 4
PEERS = 16
GRAINS = 1024
CELLS = 512


def draw_pair_count(key, part):
    key = jax.random.fold_in(key, 11)
    hot_key, base_key = jax.random.split(key)
    hottest = jax.random.randint(hot_key, (BX, BY, 1, 1), 0, PEERS)
    baseline = jax.random.randint(base_key, (BX, BY, PEERS, PEERS), 0, CAPX // 2 + 1)
    target = jnp.arange(PEERS, dtype=jnp.int32)[None, None, None, :]
    counts = jnp.where(target == hottest, CAPX, baseline)
    return counts.reshape(BX, BY, PEERS * PEERS).astype(jnp.int32)


def draw_contact_count(key, part):
    key = jax.random.fold_in(key, 12)
    counts = jax.random.randint(key, (BX, BY, PEERS), CON_DEV // 2, CON_DEV + 1)
    return counts.at[0, 0, 0].set(CON_DEV).astype(jnp.int32)


def draw_contact_pairs(key, part):
    key = jax.random.fold_in(key, 13)
    keys = jax.random.split(key, 5)
    shape = (BX, BY, PEERS * CON_DEV)
    first = jax.random.randint(keys[0], shape, 0, GRAINS)
    own_slot = first // (EX * EY * EZ)
    cell_a = first // (EY * EZ) % EX
    cell_b = first // EZ % EY
    cell_c = first % EZ
    step_a = jax.random.randint(keys[1], shape, -1, 2)
    step_b = jax.random.randint(keys[2], shape, -1, 2)
    step_c = jax.random.randint(keys[3], shape, -1, 2)
    other_slot = jax.random.randint(keys[4], shape, 0, GCAP)
    itself = (step_a == 0) & (step_b == 0) & (step_c == 0) & (other_slot == own_slot)
    other_slot = jnp.where(itself, (own_slot + 1) % GCAP, other_slot)
    second = ((other_slot * (EX + 2) + cell_a + 1 + step_a) * (EY + 2) + cell_b + 1 + step_b) * (EZ + 2) + cell_c + 1 + step_c
    return jnp.stack([first, second]).astype(jnp.int32)


def touch_ends(values, own_key, low, largest):
    shape = values.shape
    place = [jax.random.randint(jax.random.fold_in(own_key, axis), (), 0, shape[axis]) for axis in range(len(shape))]
    values = values.at[tuple(place)].set(low)
    longest = shape.index(max(shape))
    place[longest] = (place[longest] + 1) % shape[longest]
    return values.at[tuple(place)].set(largest)


def block_levels(key, dims, pieces, low, top_value):
    def one(position, blocks):
        steps = jax.random.uniform(jax.random.fold_in(jax.random.fold_in(key, 6), position), (blocks,), jnp.float32, low / len(pieces), top_value / len(pieces))
        return jnp.repeat(jnp.exp(steps), dims[position] // blocks).reshape((-1,) + (1,) * (len(dims) - position - 1))

    loudness = one(*pieces[0])
    for cut in pieces[1:]:
        loudness = loudness * one(*cut)
    return loudness


def gaussian(stream_key, extent, spread, limit, pieces=(), held_as=jnp.bfloat16):
    result = jax.random.normal(stream_key, extent, jnp.float32) * spread
    if len(pieces) > 0:
        result = block_levels(stream_key, extent, pieces, -0.22, 0.18) * result
    return jnp.clip(result, min=-limit, max=limit).astype(held_as)


def setup_inputs(seed: int = 0) -> dict:
    streams_of = jax.random.split(jax.random.key(seed), 14)
    sph_pos = jnp.clip(1.0 * jax.random.uniform(streams_of[0], (3, CAP, NX, NY, NZ), jnp.float32) ** block_levels(streams_of[0], (3, CAP, NX, NY, NZ), ((2, 8), (3, 4), (4, 16)), -0.2, 0.2), 0.0, 1.0)
    sph_vel = gaussian(streams_of[1], (3, CAP, NX, NY, NZ), 1.0, 4.0, ((2, 8), (3, 4), (4, 16)), jnp.float32)
    sph_mass = jnp.clip(jnp.exp(math.log(2.0) - 1.3862944 * jax.random.uniform(streams_of[2], (CAP, NX, NY, NZ), jnp.float32) ** block_levels(streams_of[2], (CAP, NX, NY, NZ), ((1, 8), (2, 4), (3, 16)), -0.2, 0.2)), 0.5, 2.0)
    cell_count = touch_ends(jax.random.randint(streams_of[3], (NX, NY, NZ), 1, CAP + 1), jax.random.fold_in(streams_of[3], 1), 1, CAP).astype(jnp.int32)
    grain_pos = jnp.clip(1.0 * jax.random.uniform(streams_of[4], (3, GCAP, MX, MY, MZ), jnp.float32) ** block_levels(streams_of[4], (3, GCAP, MX, MY, MZ), ((2, 8), (3, 4), (4, 16)), -0.2, 0.2), 0.0, 1.0)
    grain_vel = gaussian(streams_of[5], (3, GCAP, MX, MY, MZ), 0.5, 3.0, ((2, 8), (3, 4), (4, 16)), jnp.float32)
    grain_radius = jnp.clip(jnp.exp(math.log(0.6) - 0.6931472 * jax.random.uniform(streams_of[6], (GCAP, MX, MY, MZ), jnp.float32) ** block_levels(streams_of[6], (GCAP, MX, MY, MZ), ((1, 8), (2, 4), (3, 16)), -0.2, 0.2)), 0.3, 0.6)
    contact_pairs = draw_contact_pairs(jax.random.fold_in(streams_of[13], 71), 0)
    contact_count = draw_contact_count(jax.random.fold_in(streams_of[13], 71), 0)
    iface_grain = touch_ends(jax.random.randint(streams_of[9], (BX, BY, PEERS * PEERS, CAPX), 0, GRAINS), jax.random.fold_in(streams_of[9], 1), 0, GRAINS - 1).astype(jnp.int32)
    iface_offset = jnp.clip(-0.25 + 1.5 * jax.random.uniform(streams_of[10], (3, BX, BY, PEERS * PEERS, CAPX), jnp.float32) ** block_levels(streams_of[10], (3, BX, BY, PEERS * PEERS, CAPX), ((1, 8), (2, 4), (3, 16)), -0.2, 0.2), -0.25, 1.25)
    pair_count = draw_pair_count(jax.random.fold_in(streams_of[13], 71), 0)
    iface_cell = touch_ends(jax.random.randint(streams_of[12], (BX, BY, PEERS * PEERS, CAPX), 0, CELLS), jax.random.fold_in(streams_of[12], 1), 0, CELLS - 1).astype(jnp.int32)
    return {"sph_pos": sph_pos, "sph_vel": sph_vel, "sph_mass": sph_mass, "cell_count": cell_count, "grain_pos": grain_pos, "grain_vel": grain_vel, "grain_radius": grain_radius, "contact_pairs": contact_pairs, "contact_count": contact_count, "iface_grain": iface_grain, "iface_offset": iface_offset, "pair_count": pair_count, "iface_cell": iface_cell}


NORMING = 21.0 / (2.0 * math.pi)
STIFFNESS = 1.0
REST_DENSITY = 6.0
VISCOSITY = 0.5
GRAVITY = 1.0
DRAG_RATE = 2.0
SPRING = 20.0
SOFT_WIDTH = 0.2
DAMPING = 0.5
SOFTENING = 0.01
GRAIN_WEIGHT = 2.0
VOLUME_FACTOR = 4.0 * math.pi / 3.0

def kernel_terms(delta_x, delta_y, delta_z):
    square = delta_x * delta_x + delta_y * delta_y + delta_z * delta_z
    radius = jnp.sqrt(square)
    reach = jnp.maximum(1.0 - radius, 0.0)
    cubed = reach * reach * reach
    weight = NORMING * cubed * reach * (4.0 * radius + 1.0)
    slope = -20.0 * NORMING * cubed
    return (square, weight, slope)

def density_on(center_pos, source):
    size_a, size_b, size_c = center_pos.shape[2:]
    total = jnp.zeros(center_pos.shape[1:], center_pos.dtype)
    for step_a in range(3):
        for step_b in range(3):
            for step_c in range(3):
                near = source[:, :, step_a:step_a + size_a, step_b:step_b + size_b, step_c:step_c + size_c]
                delta_x = center_pos[0][:, None] - near[0][None, :] - float(step_a - 1)
                delta_y = center_pos[1][:, None] - near[1][None, :] - float(step_b - 1)
                delta_z = center_pos[2][:, None] - near[2][None, :] - float(step_c - 1)
                _, weight, _ = kernel_terms(delta_x, delta_y, delta_z)
                total = total + lax.optimization_barrier(jnp.sum(near[3][None, :] * weight, axis=1))
    return total

def force_on(center_pos, center_vel, center_press, center_inverse, source):
    size_a, size_b, size_c = center_pos.shape[2:]
    accel = jnp.zeros(center_pos.shape, center_pos.dtype)
    for step_a in range(3):
        for step_b in range(3):
            for step_c in range(3):
                near = source[:, :, step_a:step_a + size_a, step_b:step_b + size_b, step_c:step_c + size_c]
                delta = jnp.stack([center_pos[0][:, None] - near[0][None, :] - float(step_a - 1), center_pos[1][:, None] - near[1][None, :] - float(step_b - 1), center_pos[2][:, None] - near[2][None, :] - float(step_c - 1)])
                square, weight, slope = kernel_terms(delta[0], delta[1], delta[2])
                near_mass = near[3][None, :]
                press_coef = -near_mass * (center_press[:, None] + near[7][None, :]) * slope
                visc_coef = 2.0 * VISCOSITY * near_mass * center_inverse[:, None] * near[8][None, :] * slope * square / (square + SOFTENING)
                vel_gap = center_vel[:, :, None] - near[4:7][:, None]
                accel = accel + lax.optimization_barrier(jnp.sum(press_coef[None] * delta + visc_coef[None] * vel_gap, axis=2))
    return accel

def pressure_fields(density, mass_live):
    alive = mass_live > 0.0
    live = jnp.where(alive, 1.0, 0.0).astype(density.dtype)
    safe = jnp.where(alive, density, 1.0)
    pressure = STIFFNESS * (density - REST_DENSITY) * live
    return (live, pressure, pressure / (safe * safe), live / safe)

def pair_terms(cell_data, offset, grain_velocity, grain_volume):
    delta = offset[:, None] - cell_data[0:3]
    square, weight, slope = kernel_terms(delta[0], delta[1], delta[2])
    bracket = -cell_data[7][None] * slope[None] * delta + DRAG_RATE * weight[None] * (cell_data[3:6] - grain_velocity[:, None])
    scaled = grain_volume[None, None] * bracket
    pair_force = lax.optimization_barrier(jnp.sum(cell_data[6][None] * scaled, axis=1))
    reaction = -cell_data[8][None] * scaled
    return (pair_force, reaction)

def cell_shift(first, second, size_a, size_b, size_c):
    own_c = first % size_c
    own_b = first // size_c % size_b
    own_a = first // (size_c * size_b) % size_a
    wide_c = size_c + 2
    wide_b = size_b + 2
    wide_a = size_a + 2
    far_c = second % wide_c
    far_b = second // wide_c % wide_b
    far_a = second // (wide_c * wide_b) % wide_a
    return jnp.stack([own_a - far_a + 1, own_b - far_b + 1, own_c - far_c + 1]).astype(jnp.float32)

def contact_terms(own, other, shift, live):
    delta = own[0:3] - other[0:3] + shift
    distance = jnp.sqrt(lax.optimization_barrier(jnp.sum(delta * delta, axis=0)) + SOFTENING)
    normal = delta / distance
    intersection = own[6] + other[6] - distance
    stiff = SPRING * own[6] * other[6] / (own[6] + other[6])
    closing = lax.optimization_barrier(jnp.sum((own[3:6] - other[3:6]) * normal, axis=0))
    magnitude = live * stiff * (SOFT_WIDTH * jax.nn.softplus(intersection / SOFT_WIDTH) - DAMPING * closing)
    force = magnitude[None] * normal
    parts = jnp.stack([magnitude * normal[0] * normal[0], magnitude * normal[1] * normal[1], magnitude * normal[2] * normal[2], magnitude * normal[0] * normal[1], magnitude * normal[0] * normal[2], magnitude * normal[1] * normal[2]])
    return (force, parts)

def reference(sph_pos, sph_vel, sph_mass, cell_count, grain_pos, grain_vel, grain_radius, contact_pairs, contact_count, iface_grain, iface_offset, pair_count, iface_cell):
    slot_ids = jnp.arange(CAP, dtype=jnp.int32)[:, None, None, None]
    mass_live = jnp.where(slot_ids < cell_count[None], sph_mass, 0.0)
    spatial_pad = ((0, 0), (0, 0), (1, 1), (1, 1), (1, 1))
    first_source = jnp.pad(jnp.concatenate([sph_pos, mass_live[None]], axis=0), spatial_pad)
    layers = jnp.arange(PEERS, dtype=jnp.int32)

    def slab_density(layer):
        center = lax.dynamic_slice_in_dim(sph_pos, layer * CZ, CZ, axis=4)
        source = lax.dynamic_slice_in_dim(first_source, layer * CZ, CZ + 2, axis=4)
        return density_on(center, source)
    density = jnp.moveaxis(lax.map(slab_density, layers), 0, 3).reshape(CAP, NX, NY, NZ)
    live, pressure, press_term, inverse = pressure_fields(density, mass_live)
    second_source = jnp.pad(jnp.concatenate([sph_pos, mass_live[None], sph_vel, press_term[None], inverse[None]], axis=0), spatial_pad)

    def slab_force(layer):
        start = layer * CZ

        def layer_of(array):
            return lax.dynamic_slice_in_dim(array, start, CZ, axis=array.ndim - 1)
        source = lax.dynamic_slice_in_dim(second_source, start, CZ + 2, axis=4)
        return force_on(layer_of(sph_pos), layer_of(sph_vel), layer_of(press_term), layer_of(inverse), source)
    water_force = jnp.moveaxis(lax.map(slab_force, layers), 0, 4).reshape(3, CAP, NX, NY, NZ)
    cell_fields = jnp.concatenate([sph_pos, sph_vel, (mass_live * inverse)[None], pressure[None], inverse[None]], axis=0)
    grain_volume = VOLUME_FACTOR * grain_radius * grain_radius * grain_radius
    route_grain = iface_grain.reshape(BX, BY, PEERS, PEERS, CAPX)
    route_cell = jnp.swapaxes(iface_cell.reshape(BX, BY, PEERS, PEERS, CAPX), 2, 3)
    route_offset = iface_offset.reshape(3, BX, BY, PEERS, PEERS, CAPX)
    route_count = pair_count.reshape(BX, BY, PEERS, PEERS)
    column_x = jnp.arange(BX, dtype=jnp.int32)[:, None, None, None]
    column_y = jnp.arange(BY, dtype=jnp.int32)[None, :, None, None]
    target = jnp.arange(PEERS, dtype=jnp.int32)[None, None, :, None]
    slot_range = jnp.arange(CAPX, dtype=jnp.int32)[None, None, None, :]

    def couple(carry, source_layer):
        reactions, extra = carry
        grains = route_grain[:, :, source_layer]
        cells = route_cell[:, :, source_layer]
        offsets = route_offset[:, :, :, source_layer]
        alive = jnp.where(slot_range < route_count[:, :, source_layer][..., None], 1.0, 0.0)
        grain_slot = grains // (EX * EY * EZ)
        grain_x = column_x * EX + grains // (EY * EZ) % EX
        grain_y = column_y * EY + grains // EZ % EY
        grain_z = source_layer * EZ + grains % EZ
        velocity = grain_vel[:, grain_slot, grain_x, grain_y, grain_z]
        volume = grain_volume[grain_slot, grain_x, grain_y, grain_z] * alive
        cell_x = column_x * CX + cells // (CY * CZ)
        cell_y = column_y * CY + cells // CZ % CY
        cell_z = target * CZ + cells % CZ
        gathered = cell_fields[:, :, cell_x, cell_y, cell_z]
        pair_force, reaction = pair_terms(gathered, offsets, velocity, volume)
        reactions = reactions.at[:, :, cell_x, cell_y, cell_z].add(reaction)
        extra = extra.at[:, grain_slot, grain_x, grain_y, grain_z].add(pair_force)
        return ((reactions, extra), None)
    start_couple = (jnp.zeros((3, CAP, NX, NY, NZ), jnp.float32), jnp.zeros((3, GCAP, MX, MY, MZ), jnp.float32))
    (reactions, iface_force), _ = lax.scan(couple, start_couple, layers)
    gravity = jnp.array([0.0, 0.0, -GRAVITY], dtype=jnp.float32).reshape(3, 1, 1, 1, 1)
    sph_accel = live[None] * (water_force + gravity) + reactions
    grain_pack = jnp.concatenate([grain_pos, grain_vel, grain_radius[None]], axis=0)
    padded_pack = jnp.pad(grain_pack, spatial_pad)
    pairs = contact_pairs.reshape(2, BX, BY, PEERS, CON_DEV)
    brick_x = jnp.arange(BX, dtype=jnp.int32)[:, None, None]
    brick_y = jnp.arange(BY, dtype=jnp.int32)[None, :, None]
    contact_range = jnp.arange(CON_DEV, dtype=jnp.int32)[None, None, :]
    wide_cells = (EX + 2) * (EY + 2) * (EZ + 2)

    def collide(carry, layer):
        force_total, stress_total = carry
        first = pairs[0, :, :, layer]
        second = pairs[1, :, :, layer]
        alive = jnp.where(contact_range < contact_count[:, :, layer][..., None], 1.0, 0.0)
        own_slot = first // (EX * EY * EZ)
        own_x = brick_x * EX + first // (EY * EZ) % EX
        own_y = brick_y * EY + first // EZ % EY
        own_z = layer * EZ + first % EZ
        far_slot = second // wide_cells
        far_x = brick_x * EX + second // ((EY + 2) * (EZ + 2)) % (EX + 2)
        far_y = brick_y * EY + second // (EZ + 2) % (EY + 2)
        far_z = layer * EZ + second % (EZ + 2)
        own = grain_pack[:, own_slot, own_x, own_y, own_z]
        other = padded_pack[:, far_slot, far_x, far_y, far_z]
        shift = cell_shift(first, second, EX, EY, EZ)
        force, parts = contact_terms(own, other, shift, alive)
        force_total = force_total.at[:, own_slot, own_x, own_y, own_z].add(force)
        stress_total = stress_total.at[:, own_slot, own_x, own_y, own_z].add(parts)
        return ((force_total, stress_total), None)
    start_collide = (jnp.zeros((3, GCAP, MX, MY, MZ), jnp.float32), jnp.zeros((6, GCAP, MX, MY, MZ), jnp.float32))
    (force_total, stress_total), _ = lax.scan(collide, start_collide, layers)
    blank = jnp.zeros_like(grain_volume)
    weight_term = jnp.stack([blank, blank, -GRAIN_WEIGHT * grain_volume])
    grain_force = force_total + iface_force + weight_term
    grain_stress = -stress_total * (grain_radius / grain_volume)[None]
    return (sph_accel, grain_force, grain_stress)
```

```python
import math

import jax
import jax.numpy as jnp
from jax import lax
from jax.experimental import pallas as pl
from jax.experimental.pallas import tpu as pltpu
from jax.sharding import PartitionSpec as P

NORMING = 21.0 / (2.0 * math.pi)
REST_DENSITY = 6.0
GRAVITY = 1.0
DRAG_RATE = 2.0
SPRING = 20.0
SOFT_WIDTH = 0.2
DAMPING = 0.5
SOFTENING = 0.01
GRAIN_WEIGHT = 2.0
VOLUME_FACTOR = 4.0 * math.pi / 3.0
TINY = 1e-30

F32 = jnp.float32
BF16 = jnp.bfloat16
VM = pltpu.VMEM
SM = pltpu.SMEM

Y_GRAIN = 28
Y_RIM = 35
Y_TILES = 37
X_VEL = 24
X_GRAIN = 36
X_RIM = 43
X_TILES = 49
GRAIN_LANE = 56


def call(kernel, outs, scratch=(), ins=(), cost=None, alias=None, grid=None, out_specs=None):
    single = not isinstance(outs, (list, tuple))
    count = 1 if single else len(outs)
    if out_specs is None:
        out_specs = [pl.BlockSpec(memory_space=VM)] * count
    extra = {}
    if grid is not None:
        extra["grid"] = grid
    return pl.pallas_call(
        kernel,
        out_shape=outs,
        in_specs=list(ins),
        out_specs=out_specs[0] if single else out_specs,
        scratch_shapes=list(scratch),
        input_output_aliases=alias or {},
        compiler_params=pltpu.CompilerParams(vmem_limit_bytes=24 * 1024 * 1024),
        cost_estimate=cost,
        **extra,
    )


def cost(micros):
    return pl.CostEstimate(flops=int(micros * 4e6), bytes_accessed=int(micros * 2e6), transcendentals=0)


V = pl.BlockSpec(memory_space=VM)
S = pl.BlockSpec(memory_space=SM)


def shape(*dims):
    return jax.ShapeDtypeStruct(dims, F32)


def lanes():
    return lax.broadcasted_iota(jnp.int32, (8, 128), 1)


def subs():
    return lax.broadcasted_iota(jnp.int32, (8, 128), 0)


def roll(value, amount):
    amount = amount % 128
    return value if amount == 0 else pltpu.roll(value, amount, 1)


def spread(row):
    return jnp.broadcast_to(row, (8, 128))


def lane_gather(table, index):
    numbers = lax.GatherDimensionNumbers(
        offset_dims=(),
        collapsed_slice_dims=(1,),
        start_index_map=(1,),
        operand_batching_dims=(0,),
        start_indices_batching_dims=(0,),
    )
    return lax.gather(
        table,
        index[..., None],
        numbers,
        slice_sizes=(1, 1),
        mode=lax.GatherScatterMode.PROMISE_IN_BOUNDS,
    )


def rim_lane(field, layer, col):
    return (field * 2 + layer) * 4 + col


def split_rows(value):
    high = value.astype(BF16).astype(F32)
    return jnp.concatenate([high, value - high], axis=0)


def scatter_dot(left, hot):
    return lax.dot_general(
        left, hot, (((1,), (1,)), ((), ())), preferred_element_type=F32
    )


def hot_rows(row):
    ids = lax.broadcasted_iota(jnp.int32, (128, 128), 0)
    return jnp.where(ids == jnp.broadcast_to(row, (128, 128)), 1.0, 0.0).astype(BF16)


def pack_kernel(place, counts, pos, vel, mass, count, gpos, gvel, grad, grain, offset, send, own):
    lane = lanes()
    sub = subs()
    low = jnp.zeros((8, 128), F32)
    high = jnp.zeros((8, 128), F32)
    for col in range(4):
        for field in range(7):
            if field < 3:
                value = pos[pl.ds(field * 32 + col, 8, stride=4), :]
            elif field == 3:
                value = mass[pl.ds(col, 8, stride=4), :]
                value = jnp.where(sub < spread(count[pl.ds(col, 1), :]), value, 0.0)
            else:
                value = vel[pl.ds((field - 4) * 32 + col, 8, stride=4), :]
            own[col * 7 + field] = value
            for layer in range(2):
                at = rim_lane(field, layer, col)
                low = jnp.where(lane == at, roll(value, at - layer), low)
                high = jnp.where(lane == at, roll(value, at - 126 - layer), high)
    for field in range(7):
        if field < 3:
            value = gpos[pl.ds(field * 8, 8), :]
        elif field < 6:
            value = gvel[pl.ds((field - 3) * 8, 8), :]
        else:
            value = grad[...]
        own[Y_GRAIN + field] = value
        at = GRAIN_LANE + field
        low = jnp.where(lane == at, roll(value, at), low)
        high = jnp.where(lane == at, roll(value, at - 127), high)
    radius = grad[...]
    volume = VOLUME_FACTOR * radius * radius * radius
    tables = [gvel[pl.ds(field * 8, 8), :] for field in range(3)] + [volume]
    for group in range(2):
        index = grain[pl.ds(group * 8, 8), :]
        row = index >> 7
        at = index & 127
        found = [jnp.zeros((8, 128), F32) for _ in range(4)]
        for place_row in range(8):
            here = row == place_row
            for field in range(4):
                got = lane_gather(spread(tables[field][place_row : place_row + 1]), at)
                found[field] = jnp.where(here, got, found[field])
        alive = jnp.zeros((8, 128), jnp.int32)
        for peer in range(8):
            alive = jnp.where(sub == peer, counts[group * 8 + peer], alive)
        found[3] = jnp.where(lane < alive, found[3], 0.0)
        for field in range(3):
            send[pl.ds(group * 128 + field, 8, stride=16), :] = offset[
                pl.ds(field * 16 + group * 8, 8), :
            ]
        for field in range(4):
            send[pl.ds(group * 128 + 3 + field, 8, stride=16), :] = found[field]
        send[pl.ds(group * 128 + 7, 8, stride=16), :] = jnp.zeros((8, 128), F32)
    for peer in range(16):
        send[pl.ds(peer * 16 + 8, 8), :] = jnp.where(peer < place[2], low, high)


def rim_kernel(place, arrived, own_in, own):
    step = pl.program_id(0)
    layer = place[2]
    other = jnp.where(step == 0, layer - 1, layer + 1)
    inside = jnp.logical_and(other >= 0, other <= 15)
    start = pl.multiple_of(jnp.clip(other, 0, 15) * 16 + 8, 8)
    own[0] = jnp.where(inside, arrived[pl.ds(start, 8), :], 0.0)


def widen_kernel(own, ahead, behind, up, down):
    for send, a in ((up, 1), (down, 0)):
        for y in range(6):
            source = (ahead, own, behind)[y // 2]
            col = a * 2 + y % 2
            for field in range(4):
                send[y * 4 + field] = source[col * 7 + field]
        for y in range(4):
            source = (ahead, own, own, behind)[y]
            col = a * 2 + (1, 0, 1, 0)[y]
            for field in range(3):
                send[X_VEL + y * 3 + field] = source[col * 7 + 4 + field]
            for field in range(7):
                for slot in range(2):
                    send[X_GRAIN + field, pl.ds(slot * 4 + y, 1), :] = source[
                        Y_GRAIN + field, pl.ds(slot * 4 + col, 1), :
                    ]
        for part, source in enumerate((own, ahead, behind)):
            for side in range(2):
                send[X_RIM + part * 2 + side] = source[Y_RIM + side]


class Near:
    def __init__(self, own, ahead, behind, left, right):
        self.own, self.ahead, self.behind = own, ahead, behind
        self.left, self.right = left, right

    def part(self, y):
        return (1, 0, 2)[y // 2] if y // 2 != 1 else 0

    def main(self, field, x, y):
        if x in (1, 2):
            source = (self.ahead, self.own, self.behind)[y // 2]
            return source[((x - 1) * 2 + y % 2) * 7 + field]
        source = self.left if x == 0 else self.right
        if field < 4:
            return source[y * 4 + field]
        return source[X_VEL + (y - 1) * 3 + field - 4]

    def rim(self, side, x, y):
        part = (1, 0, 2)[y // 2]
        if x in (1, 2):
            return (self.own, self.ahead, self.behind)[part][Y_RIM + side]
        source = self.left if x == 0 else self.right
        return source[X_RIM + part * 2 + side]

    def rim_col(self, x, y):
        return (1, 0, 1, 0)[x] * 2 + y % 2


def density_kernel(place, own, ahead, behind, left, right, out, near, table):
    lane = lanes()
    first = lane == 0
    last = lane == 127
    data = Near(own, ahead, behind, left, right)
    has_left = place[0] > 0
    has_right = place[0] < 7
    sign = jnp.where(lane < 64, -1.0, 1.0)
    packed = [[jnp.zeros((8, 128), F32) for _ in range(4)] for _ in range(3)]
    for x in range(4):
        for y in range(6):
            col = data.rim_col(x, y)
            rims = [data.rim(side, x, y) for side in range(2)]
            for field in range(4):
                value = data.main(field, x, y)
                edge = [rims[0], rims[1]]
                if field == 3 and x in (0, 3):
                    there = has_left if x == 0 else has_right
                    value = jnp.where(there, value, 0.0)
                    edge = [jnp.where(there, one, 0.0) for one in edge]
                shift = float(x - 1) if field == 0 else float(y - 2) if field == 1 else 0.0
                if shift:
                    value = value + shift
                    edge = [one + shift for one in edge]
                back = jnp.where(first, roll(edge[0], -rim_lane(field, 1, col)), roll(value, 1))
                fore = jnp.where(last, roll(edge[1], 127 - rim_lane(field, 0, col)), roll(value, 127))
                if field == 2:
                    back = back - 1.0
                    fore = fore + 1.0
                at = (x * 6 + y) * 12 + field
                near[at] = back
                near[at + 4] = value
                near[at + 8] = fore
                for side in range(2):
                    spot = side * 64 + x * 8 + y
                    here = lane == spot
                    outer = rim_lane(field, 0 if side == 0 else 1, col)
                    inner = rim_lane(field, 1 if side == 0 else 0, col)
                    packed[0][field] = jnp.where(here, roll(edge[side], spot - outer), packed[0][field])
                    packed[1][field] = jnp.where(here, roll(edge[side], spot - inner), packed[1][field])
                    packed[2][field] = jnp.where(
                        here, roll(value, spot - (0 if side == 0 else 127)), packed[2][field]
                    )
    packed[0][2] = packed[0][2] + sign
    packed[2][2] = packed[2][2] - sign
    for step_x in range(3):
        for step_y in range(3):
            for level in range(3):
                for field in range(4):
                    at = (24 + step_x * 3 + step_y) * 12 + level * 4 + field
                    near[at] = roll(packed[level][field], -((step_x - 1) * 8 + step_y - 1))
    for x in range(2):
        for y in range(4):
            for step in range(9):
                table[(x * 4 + y) * 9 + step] = (x + step // 3) * 6 + y + step % 3
    for step in range(9):
        table[72 + step] = 24 + step

    def one_column(target, carry):
        middle = table[target * 9 + 4] * 12
        center = [near[middle + 4 + field] for field in range(4)]

        def one_neighbour(step, total):
            base = table[target * 9 + step] * 12
            for level in range(3):
                for slot in range(8):
                    row = [
                        spread(near[base + level * 4 + field, pl.ds(slot, 1), :])
                        for field in range(4)
                    ]
                    dx = center[0] - row[0]
                    dy = center[1] - row[1]
                    dz = center[2] - row[2]
                    square = jnp.maximum(dx * dx + dy * dy + dz * dz, TINY)
                    radius = square * lax.rsqrt(square)
                    reach = jnp.maximum(1.0 - radius, 0.0)
                    reach = reach * reach
                    total = total + (reach * reach) * (4.0 * radius + 1.0) * row[3]
            return total

        total = lax.fori_loop(0, 9, one_neighbour, jnp.zeros((8, 128), F32))
        density = NORMING * total
        alive = center[3] > 0.0
        live = jnp.where(alive, 1.0, 0.0)
        safe = jnp.where(alive, density, 1.0)
        pressure = (density - REST_DENSITY) * live
        out[target * 3] = pressure / (safe * safe)
        out[target * 3 + 1] = live / safe
        out[target * 3 + 2] = pressure
        return carry

    lax.fori_loop(0, 9, one_column, 0)


def force_kernel(place, own, ahead, behind, left, right, fields, fleft, fright, reaction, out, near):
    lane = lanes()
    first = lane == 0
    last = lane == 127
    data = Near(own, ahead, behind, left, right)
    has_left = place[0] > 0
    has_right = place[0] < 7
    for x in range(4):
        for y in range(1, 5):
            col = data.rim_col(x, y)
            rims = [data.rim(side, x, y) for side in range(2)]
            source = fields if x in (1, 2) else fleft if x == 0 else fright
            far_x = (1, 0, 1, 0)[x]
            target = far_x * 4 + y - 1
            extra = []
            for which in range(2):
                value = source[target * 3 + which]
                halo = source[24 + which]
                extra.append((value, halo))
            levels = [[], [], []]
            for field in range(7):
                value = data.main(field, x, y)
                edge = [rims[0], rims[1]]
                if field == 3 and x in (0, 3):
                    there = has_left if x == 0 else has_right
                    value = jnp.where(there, value, 0.0)
                    edge = [jnp.where(there, one, 0.0) for one in edge]
                back = jnp.where(first, roll(edge[0], -rim_lane(field, 1, col)), roll(value, 1))
                fore = jnp.where(last, roll(edge[1], 127 - rim_lane(field, 0, col)), roll(value, 127))
                shift = float(x - 1) if field == 0 else float(y - 2) if field == 1 else 0.0
                if shift:
                    value, back, fore = value + shift, back + shift, fore + shift
                if field == 2:
                    back = back - 1.0
                    fore = fore + 1.0
                for level, one in enumerate((back, value, fore)):
                    levels[level].append(one)
            spot = (far_x + 1) * 8 + y
            for value, halo in extra:
                back = jnp.where(first, roll(halo, -spot), roll(value, 1))
                fore = jnp.where(last, roll(halo, 127 - 64 - spot), roll(value, 127))
                for level, one in enumerate((back, value, fore)):
                    levels[level].append(one)
            for level in range(3):
                px, py, pz, m, vx, vy, vz, press, inverse = levels[level]
                at = ((x * 4 + y - 1) * 3 + level) * 9
                for k, one in enumerate((px, py, pz, m, m * press, m * inverse, vx, vy, vz)):
                    near[at + k] = one

    def one_column(target, carry):
        a = target // 2
        b = target % 2
        middle = (((a + 1) * 4 + b + 1) * 3 + 1) * 9
        center = [near[middle + k] for k in range(3)]
        press = fields[(a * 4 + b + 1) * 3]
        inverse = fields[(a * 4 + b + 1) * 3 + 1]

        def one_neighbour(step, total):
            base = (((a + step // 3) * 4 + b + step % 3) * 3) * 9
            total = list(total)
            for level in range(3):
                for slot in range(8):
                    row = [
                        spread(near[base + level * 9 + k, pl.ds(slot, 1), :]) for k in range(9)
                    ]
                    dx = center[0] - row[0]
                    dy = center[1] - row[1]
                    dz = center[2] - row[2]
                    square = dx * dx + dy * dy + dz * dz
                    guarded = jnp.maximum(square, TINY)
                    radius = guarded * lax.rsqrt(guarded)
                    reach = jnp.maximum(1.0 - radius, 0.0)
                    cubed = reach * reach * reach
                    push = cubed * (row[3] * press + row[4])
                    soft = lax.rsqrt(square + SOFTENING)
                    drag = (cubed * row[5]) * (square * soft * soft)
                    total[0] = total[0] + push * dx
                    total[1] = total[1] + push * dy
                    total[2] = total[2] + push * dz
                    total[3] = total[3] + drag
                    total[4] = total[4] + drag * row[6]
                    total[5] = total[5] + drag * row[7]
                    total[6] = total[6] + drag * row[8]
            return tuple(total)

        zero = jnp.zeros((8, 128), F32)
        total = lax.fori_loop(0, 9, one_neighbour, (zero,) * 7)
        live = jnp.where(near[middle + 3] > 0.0, 1.0, 0.0)
        for d in range(3):
            slow = inverse * (near[middle + 6 + d] * total[3] - total[4 + d])
            force = 20.0 * NORMING * (total[d] - slow)
            if d == 2:
                force = force - GRAVITY
            out[pl.ds(d * 32 + target, 8, stride=4), :] = live * force + reaction[d * 4 + target]
        return carry

    lax.fori_loop(0, 4, one_column, 0)


def pair_kernel(own, fields, arrived, cells, send, reaction, left, hot):
    for peer in range(16):
        index = cells[pl.ds(peer, 1), :]
        at_row = index & 127
        at = spread(at_row)
        col_of = spread(index >> 7)
        found = None
        for col in range(4):
            mid = ((col // 2) * 4 + col % 2 + 1) * 3
            inverse = fields[mid + 1]
            tables = [own[col * 7 + k] for k in (0, 1, 2, 4, 5, 6)]
            tables += [own[col * 7 + 3] * inverse, fields[mid + 2], inverse]
            got = [lane_gather(one, at) for one in tables]
            if found is None:
                found = got
            else:
                here = col_of == col
                found = [jnp.where(here, new, old) for new, old in zip(got, found)]
        row = [spread(arrived[pl.ds(peer * 16 + k, 1), :]) for k in range(7)]
        delta = [row[d] - found[d] for d in range(3)]
        square = jnp.maximum(delta[0] * delta[0] + delta[1] * delta[1] + delta[2] * delta[2], TINY)
        radius = square * lax.rsqrt(square)
        reach = jnp.maximum(1.0 - radius, 0.0)
        cubed = reach * reach * reach
        weight = (DRAG_RATE * NORMING) * cubed * reach * (4.0 * radius + 1.0)
        push = (20.0 * NORMING) * found[7] * cubed
        hot[:, peer * 128 : peer * 128 + 128] = hot_rows(at_row)
        for d in range(3):
            bracket = row[6] * (push * delta[d] + weight * (found[3 + d] - row[3 + d]))
            send[peer, pl.ds(d, 1), :] = jnp.sum(found[6] * bracket, axis=0, keepdims=True)
            both = split_rows(-found[8] * bracket)
            col_both = jnp.concatenate([col_of, col_of], axis=0)
            for col in range(4):
                at16 = (d * 4 + col) * 16
                left[at16 : at16 + 16, peer * 128 : peer * 128 + 128] = jnp.where(
                    col_both == col, both, 0.0
                ).astype(BF16)
        send[peer, pl.ds(3, 1), :] = jnp.zeros((1, 128), F32)
    sums = scatter_dot(left[...], hot[...])
    for k in range(12):
        reaction[k] = sums[k * 16 : k * 16 + 8] + sums[k * 16 + 8 : k * 16 + 16]


def contact_kernel(place, live_count, own, ahead, behind, left, right, first, second, out, table, rims, turned, rows, lhs, hot):
    lane = lanes()
    sub = subs()
    has_left = place[0] > 0
    has_right = place[0] < 7
    for field in range(7):
        for slot in range(2):
            for x in range(4):
                for y in range(4):
                    if x in (1, 2):
                        source = (ahead, own, own, behind)[y]
                        value = source[
                            Y_GRAIN + field,
                            pl.ds(slot * 4 + (x - 1) * 2 + (1, 0, 1, 0)[y], 1),
                            :,
                        ]
                    else:
                        source, there = (left, has_left) if x == 0 else (right, has_right)
                        value = source[X_GRAIN + field, pl.ds(slot * 4 + y, 1), :]
                        value = jnp.where(there, value, 0.0)
                    table[pl.ds(field * 32 + slot * 16 + x * 4 + y, 1), :] = value
    for side in range(2):
        rims[...] = jnp.zeros((128, 128), F32)
        for part, source in enumerate((own, ahead, behind)):
            rims[pl.ds(part * 8, 8), :] = source[Y_RIM + side]
            rims[pl.ds((3 + part) * 8, 8), :] = jnp.where(
                has_left, left[X_RIM + part * 2 + side], 0.0
            )
            rims[pl.ds((6 + part) * 8, 8), :] = jnp.where(
                has_right, right[X_RIM + part * 2 + side], 0.0
            )
        turned[side] = jnp.transpose(rims[...])

    def one_group(group, carry):
        start = pl.multiple_of(group * 8, 8)
        one = first[pl.ds(start, 8), :]
        two = second[pl.ds(start, 8), :]
        own_row = one >> 7
        own_c = one & 127
        far_row = (two * 4033) >> 19
        far_c = two - far_row * 130
        far_slot = far_row >> 4
        far_x = (far_row >> 2) & 3
        far_y = far_row & 3
        far_at = jnp.clip(far_c - 1, 0, 127)
        x_part = jnp.where(far_x == 0, 1, jnp.where(far_x == 3, 2, 0))
        y_part = jnp.where(far_y == 0, 1, jnp.where(far_y == 3, 2, 0))
        rim_a = jnp.where(far_x == 0, 1, jnp.where(far_x == 3, 0, far_x - 1))
        rim_b = jnp.where(far_y == 0, 1, jnp.where(far_y == 3, 0, far_y - 1))
        rim_at = (x_part * 3 + y_part) * 8 + far_slot * 4 + rim_a * 2 + rim_b
        own_found = [jnp.zeros((8, 128), F32) for _ in range(7)]
        for row in range(8):
            here = own_row == row
            for field in range(7):
                got = lane_gather(spread(own[Y_GRAIN + field, pl.ds(row, 1), :]), own_c)
                own_found[field] = jnp.where(here, got, own_found[field])
        far_found = [jnp.zeros((8, 128), F32) for _ in range(7)]
        for row in range(32):
            here = far_row == row
            for field in range(7):
                got = lane_gather(spread(table[pl.ds(field * 32 + row, 1), :]), far_at)
                far_found[field] = jnp.where(here, got, far_found[field])
        for side, edge in ((0, 0), (1, 129)):
            here = far_c == edge
            for field in range(7):
                got = lane_gather(
                    spread(turned[side, pl.ds(GRAIN_LANE + field, 1), :]), rim_at
                )
                far_found[field] = jnp.where(here, got, far_found[field])
        shift = [
            (((own_row >> 1) & 1) - far_x + 1).astype(F32),
            ((own_row & 1) - far_y + 1).astype(F32),
            (own_c - far_c + 1).astype(F32),
        ]
        delta = [own_found[d] - far_found[d] + shift[d] for d in range(3)]
        distance = jnp.sqrt(
            delta[0] * delta[0] + delta[1] * delta[1] + delta[2] * delta[2] + SOFTENING
        )
        normal = [one_delta / distance for one_delta in delta]
        both = own_found[6] + far_found[6]
        overlap = (both - distance) / SOFT_WIDTH
        stiff = SPRING * own_found[6] * far_found[6] / both
        closing = sum((own_found[3 + d] - far_found[3 + d]) * normal[d] for d in range(3))
        soft = jnp.maximum(overlap, 0.0) + jnp.log1p(jnp.exp(-jnp.abs(overlap)))
        number = group * 1024 + sub * 128 + lane
        magnitude = jnp.where(
            number < live_count[0], stiff * (SOFT_WIDTH * soft - DAMPING * closing), 0.0
        )
        force = [magnitude * normal[d] for d in range(3)]
        values = force + [
            force[0] * normal[0],
            force[1] * normal[1],
            force[2] * normal[2],
            force[0] * normal[1],
            force[0] * normal[2],
            force[1] * normal[2],
        ]
        for k in range(9):
            high = values[k].astype(BF16).astype(F32)
            rows[pl.ds(k * 16, 8), :] = high
            rows[pl.ds(k * 16 + 8, 8), :] = values[k] - high
        for s in range(8):
            at = pl.ds(pl.multiple_of((group * 8 + s) * 128, 128), 128)
            mine = spread(own_row[s : s + 1]) == sub
            mine2 = jnp.concatenate([mine, mine], axis=0)
            hot[:, at] = hot_rows(own_c[s : s + 1])
            for k in range(9):
                high = spread(rows[pl.ds(k * 16 + s, 1), :])
                low = spread(rows[pl.ds(k * 16 + 8 + s, 1), :])
                pair = jnp.concatenate(
                    [jnp.where(mine, high, 0.0), jnp.where(mine, low, 0.0)], axis=0
                )
                lhs[k * 16 : k * 16 + 16, at] = pair.astype(BF16)
        return carry

    lax.fori_loop(0, 6, one_group, 0)
    sums = scatter_dot(lhs[...], hot[...])
    for k in range(9):
        out[k] = sums[k * 16 : k * 16 + 8] + sums[k * 16 + 8 : k * 16 + 16]


def grain_kernel(back, grain, contact, radius_ref, force_out, stress_out, lhs, hot):
    sub = subs()
    for peer in range(16):
        index = grain[pl.ds(peer, 1), :]
        mine = spread(index >> 7) == sub
        hot[:, peer * 128 : peer * 128 + 128] = hot_rows(index & 127)
        for d in range(3):
            value = jnp.where(mine, spread(back[peer, pl.ds(d, 1), :]), 0.0)
            lhs[d * 16 : d * 16 + 16, peer * 128 : peer * 128 + 128] = split_rows(value).astype(BF16)
    sums = scatter_dot(lhs[...], hot[...])
    radius = radius_ref[...]
    volume = VOLUME_FACTOR * radius * radius * radius
    for d in range(3):
        value = contact[d] + (sums[d * 16 : d * 16 + 8] + sums[d * 16 + 8 : d * 16 + 16])
        if d == 2:
            value = value - GRAIN_WEIGHT * volume
        force_out[pl.ds(d * 8, 8), :] = value
    scale = radius / volume
    for k in range(6):
        stress_out[pl.ds(k * 8, 8), :] = -contact[3 + k] * scale


def along_y(value, step):
    count = lax.axis_size("gy")
    pairs = [(i, i + step) for i in range(count) if 0 <= i + step < count]
    return lax.ppermute(value, "gy", pairs)


def along_x(value, step):
    count = lax.axis_size("gx")
    return lax.ppermute(value, "gx", [(i, (i + step) % count) for i in range(count)])


def body(
    sph_pos,
    sph_vel,
    sph_mass,
    cell_count,
    grain_pos,
    grain_vel,
    grain_radius,
    contact_pairs,
    contact_count,
    iface_grain,
    iface_offset,
    pair_count,
    iface_cell,
):
    place = jnp.stack(
        [lax.axis_index("gx"), lax.axis_index("gy"), lax.axis_index("gz")]
    ).astype(jnp.int32)
    radius = grain_radius.reshape(8, 128)
    route_grain = iface_grain.reshape(16, 128)
    send, own = call(
        pack_kernel,
        [shape(256, 128), shape(Y_TILES, 8, 128)],
        ins=[S, S] + [V] * 9,
        cost=cost(3),
    )(
        place,
        pair_count.reshape(16),
        sph_pos.reshape(96, 128),
        sph_vel.reshape(96, 128),
        sph_mass.reshape(32, 128),
        cell_count.reshape(4, 128),
        grain_pos.reshape(24, 128),
        grain_vel.reshape(24, 128),
        radius,
        route_grain,
        iface_offset.reshape(48, 128),
    )
    arrived = lax.all_to_all(
        send.reshape(16, 16, 128), "gz", split_axis=0, concat_axis=0, tiled=True
    ).reshape(256, 128)
    own = call(
        rim_kernel,
        shape(Y_TILES, 8, 128),
        ins=[S, V, pl.BlockSpec(memory_space=pl.ANY)],
        alias={2: 0},
        grid=(2,),
        out_specs=[pl.BlockSpec((1, 8, 128), lambda i: (Y_RIM + i, 0, 0))],
        cost=cost(1),
    )(place, arrived, own)
    ahead = along_y(own, 1)
    behind = along_y(own, -1)
    up, down = call(
        widen_kernel,
        [shape(X_TILES, 8, 128)] * 2,
        ins=[V] * 3,
        cost=cost(1),
    )(own, ahead, behind)
    left = along_x(up, 1)
    right = along_x(down, -1)
    fields = call(
        density_kernel,
        shape(27, 8, 128),
        ins=[S] + [V] * 5,
        scratch=[pltpu.VMEM((33 * 12, 8, 128), F32), pltpu.SMEM((81,), jnp.int32)],
        cost=cost(6),
    )(place, own, ahead, behind, left, right)
    fields_left = along_x(fields, 1)
    fields_right = along_x(fields, -1)
    send_back, reaction = call(
        pair_kernel,
        [shape(16, 4, 128), shape(12, 8, 128)],
        ins=[V] * 4,
        scratch=[pltpu.VMEM((192, 2048), BF16), pltpu.VMEM((128, 2048), BF16)],
        cost=cost(3),
    )(own, fields, arrived, iface_cell.reshape(16, 128))
    back = lax.all_to_all(send_back, "gz", split_axis=0, concat_axis=0, tiled=True)
    contact = call(
        contact_kernel,
        shape(9, 8, 128),
        ins=[S, S] + [V] * 7,
        scratch=[
            pltpu.VMEM((224, 128), F32),
            pltpu.VMEM((128, 128), F32),
            pltpu.VMEM((2, 128, 128), F32),
            pltpu.VMEM((144, 128), F32),
            pltpu.VMEM((144, 6144), BF16),
            pltpu.VMEM((128, 6144), BF16),
        ],
        cost=cost(6),
    )(
        place,
        contact_count.reshape(1),
        own,
        ahead,
        behind,
        left,
        right,
        contact_pairs[0].reshape(48, 128),
        contact_pairs[1].reshape(48, 128),
    )
    accel = call(
        force_kernel,
        shape(96, 128),
        ins=[S] + [V] * 9,
        scratch=[pltpu.VMEM((16 * 27, 8, 128), F32)],
        cost=cost(6),
    )(place, own, ahead, behind, left, right, fields, fields_left, fields_right, reaction)
    grain_force, grain_stress = call(
        grain_kernel,
        [shape(24, 128), shape(48, 128)],
        ins=[V] * 4,
        scratch=[pltpu.VMEM((48, 2048), BF16), pltpu.VMEM((128, 2048), BF16)],
        cost=cost(2),
    )(back, route_grain, contact, radius)
    return (
        accel.reshape(sph_pos.shape),
        grain_force.reshape(grain_pos.shape),
        grain_stress.reshape((6,) + grain_radius.shape),
    )


def solution(mesh):
    return jax.shard_map(
        body,
        mesh=mesh,
        in_specs=(
            P(None, None, "gx", "gy", "gz"),
            P(None, None, "gx", "gy", "gz"),
            P(None, "gx", "gy", "gz"),
            P("gx", "gy", "gz"),
            P(None, None, "gx", "gy", "gz"),
            P(None, None, "gx", "gy", "gz"),
            P(None, "gx", "gy", "gz"),
            P(None, "gx", "gy", "gz"),
            P("gx", "gy", "gz"),
            P("gx", "gy", "gz", None),
            P(None, "gx", "gy", "gz", None),
            P("gx", "gy", "gz"),
            P("gx", "gy", "gz", None),
        ),
        out_specs=(
            P(None, None, "gx", "gy", "gz"),
            P(None, None, "gx", "gy", "gz"),
            P(None, None, "gx", "gy", "gz"),
        ),
        check_vma=False,
    )
```

```python
import math

import jax
import jax.numpy as jnp
from jax import lax
from jax.experimental import pallas as pl
from jax.experimental.pallas import tpu as pltpu
from jax.sharding import PartitionSpec as P

NORMING = 21.0 / (2.0 * math.pi)
REST_DENSITY = 6.0
GRAVITY = 1.0
DRAG_RATE = 2.0
SPRING = 20.0
SOFT_WIDTH = 0.2
DAMPING = 0.5
SOFTENING = 0.01
GRAIN_WEIGHT = 2.0
VOLUME_FACTOR = 4.0 * math.pi / 3.0
TINY = 1e-30

F32 = jnp.float32
BF16 = jnp.bfloat16
VM = pltpu.VMEM
SM = pltpu.SMEM

Y_GRAIN = 28
Y_RIM = 35
Y_TILES = 37
X_VEL = 24
X_GRAIN = 36
X_RIM = 43
X_TILES = 49
GRAIN_LANE = 56


def call(kernel, outs, scratch=(), ins=(), cost=None, alias=None, grid=None, out_specs=None, limit=24):
    single = not isinstance(outs, (list, tuple))
    count = 1 if single else len(outs)
    if out_specs is None:
        out_specs = [pl.BlockSpec(memory_space=VM)] * count
    extra = {}
    if grid is not None:
        extra["grid"] = grid
    if limit is not None:
        extra["compiler_params"] = pltpu.CompilerParams(vmem_limit_bytes=limit * 1024 * 1024)
    return pl.pallas_call(
        kernel,
        out_shape=outs,
        in_specs=list(ins),
        out_specs=out_specs[0] if single else out_specs,
        scratch_shapes=list(scratch),
        input_output_aliases=alias or {},
        cost_estimate=cost,
        **extra,
    )


def cost(micros):
    return pl.CostEstimate(flops=int(micros * 4e6), bytes_accessed=int(micros * 2e6), transcendentals=0)


V = pl.BlockSpec(memory_space=VM)
S = pl.BlockSpec(memory_space=SM)


def shape(*dims):
    return jax.ShapeDtypeStruct(dims, F32)


def lanes():
    return lax.broadcasted_iota(jnp.int32, (8, 128), 1)


def subs():
    return lax.broadcasted_iota(jnp.int32, (8, 128), 0)


def roll(value, amount):
    amount = amount % 128
    return value if amount == 0 else pltpu.roll(value, amount, 1)


def spread(row):
    return jnp.broadcast_to(row, (8, 128))


def lane_gather(table, index):
    numbers = lax.GatherDimensionNumbers(
        offset_dims=(),
        collapsed_slice_dims=(1,),
        start_index_map=(1,),
        operand_batching_dims=(0,),
        start_indices_batching_dims=(0,),
    )
    return lax.gather(
        table,
        index[..., None],
        numbers,
        slice_sizes=(1, 1),
        mode=lax.GatherScatterMode.PROMISE_IN_BOUNDS,
    )


def rim_lane(field, layer, col):
    return (field * 2 + layer) * 4 + col


def split_rows(value):
    high = value.astype(BF16).astype(F32)
    return jnp.concatenate([high, value - high], axis=0)


def scatter_dot(left, hot):
    return lax.dot_general(
        left, hot, (((1,), (1,)), ((), ())), preferred_element_type=F32
    )


def hot_rows(row):
    ids = lax.broadcasted_iota(jnp.int32, (128, 128), 0)
    return jnp.where(ids == jnp.broadcast_to(row, (128, 128)), 1.0, 0.0).astype(BF16)


def pack_kernel(place, counts, *refs):
    sources, (send, own), buffers, sems = refs[:9], refs[9:11], refs[11:20], refs[20]
    copies = [
        pltpu.make_async_copy(source, buffer, sems.at[k])
        for k, (source, buffer) in enumerate(zip(sources, buffers))
    ]
    for one in copies:
        one.start()
    for one in copies:
        one.wait()
    pos, vel, mass, count, gpos, gvel, grad, grain, offset = buffers
    lane = lanes()
    sub = subs()
    low = jnp.zeros((8, 128), F32)
    high = jnp.zeros((8, 128), F32)
    for col in range(4):
        for field in range(7):
            if field < 3:
                value = pos[pl.ds(field * 32 + col, 8, stride=4), :]
            elif field == 3:
                value = mass[pl.ds(col, 8, stride=4), :]
                value = jnp.where(sub < spread(count[pl.ds(col, 1), :]), value, 0.0)
            else:
                value = vel[pl.ds((field - 4) * 32 + col, 8, stride=4), :]
            own[col * 7 + field] = value
            for layer in range(2):
                at = rim_lane(field, layer, col)
                low = jnp.where(lane == at, roll(value, at - layer), low)
                high = jnp.where(lane == at, roll(value, at - 126 - layer), high)
    for field in range(7):
        if field < 3:
            value = gpos[pl.ds(field * 8, 8), :]
        elif field < 6:
            value = gvel[pl.ds((field - 3) * 8, 8), :]
        else:
            value = grad[...]
        own[Y_GRAIN + field] = value
        at = GRAIN_LANE + field
        low = jnp.where(lane == at, roll(value, at), low)
        high = jnp.where(lane == at, roll(value, at - 127), high)
    radius = grad[...]
    volume = VOLUME_FACTOR * radius * radius * radius
    tables = [gvel[pl.ds(field * 8, 8), :] for field in range(3)] + [volume]
    for group in range(2):
        index = grain[pl.ds(group * 8, 8), :]
        row = index >> 7
        at = index & 127
        found = [jnp.zeros((8, 128), F32) for _ in range(4)]
        for place_row in range(8):
            here = row == place_row
            for field in range(4):
                got = lane_gather(spread(tables[field][place_row : place_row + 1]), at)
                found[field] = jnp.where(here, got, found[field])
        alive = jnp.zeros((8, 128), jnp.int32)
        for peer in range(8):
            alive = jnp.where(sub == peer, counts[group * 8 + peer], alive)
        found[3] = jnp.where(lane < alive, found[3], 0.0)
        for field in range(3):
            send[pl.ds(group * 96 + field, 8, stride=12), :] = offset[
                pl.ds(field * 16 + group * 8, 8), :
            ]
        for field in range(4):
            send[pl.ds(group * 96 + 3 + field, 8, stride=12), :] = found[field]
        send[pl.ds(group * 96 + 7, 8, stride=12), :] = jnp.zeros((8, 128), F32)
    low, high = [
        jnp.where(lane < 64, one, pltpu.roll(roll(one, 64), 4, 0))[0:4] for one in (low, high)
    ]
    for peer in range(16):
        send[pl.ds(peer * 12 + 8, 4), :] = jnp.where(peer < place[2], low, high)


def rim_kernel(place, arrived, own_in, own):
    step = pl.program_id(0)
    layer = place[2]
    other = jnp.where(step == 0, layer - 1, layer + 1)
    inside = jnp.logical_and(other >= 0, other <= 15)
    rows = jnp.where(inside, arrived[jnp.clip(other, 0, 15) * 3 + 2], 0.0)
    own[0] = jnp.concatenate([rows, pltpu.roll(rows, 64, 1)], axis=0)


def widen_kernel(own, ahead, behind, up, down):
    for send, a in ((up, 1), (down, 0)):
        for y in range(6):
            source = (ahead, own, behind)[y // 2]
            col = a * 2 + y % 2
            for field in range(4):
                send[y * 4 + field] = source[col * 7 + field]
        for y in range(4):
            source = (ahead, own, own, behind)[y]
            col = a * 2 + (1, 0, 1, 0)[y]
            for field in range(3):
                send[X_VEL + y * 3 + field] = source[col * 7 + 4 + field]
            for field in range(7):
                for slot in range(2):
                    send[X_GRAIN + field, pl.ds(slot * 4 + y, 1), :] = source[
                        Y_GRAIN + field, pl.ds(slot * 4 + col, 1), :
                    ]
        for part, source in enumerate((own, ahead, behind)):
            for side in range(2):
                send[X_RIM + part * 2 + side] = source[Y_RIM + side]


class Near:
    def __init__(self, own, ahead, behind, left, right):
        self.own, self.ahead, self.behind = own, ahead, behind
        self.left, self.right = left, right

    def main(self, field, x, y):
        if x in (1, 2):
            source = (self.ahead, self.own, self.behind)[y // 2]
            return source[((x - 1) * 2 + y % 2) * 7 + field]
        source = self.left if x == 0 else self.right
        if field < 4:
            return source[y * 4 + field]
        return source[X_VEL + (y - 1) * 3 + field - 4]

    def rim(self, side, x, y):
        part = (1, 0, 2)[y // 2]
        if x in (1, 2):
            return (self.own, self.ahead, self.behind)[part][Y_RIM + side]
        source = self.left if x == 0 else self.right
        return source[X_RIM + part * 2 + side]

    def rim_col(self, x, y):
        return (1, 0, 1, 0)[x] * 2 + y % 2


class Columns:
    def __init__(self, data, near, has_left=None, has_right=None):
        self.data, self.near = data, near
        self.there = {0: has_left, 3: has_right}
        self.lane = lanes()
        self.packed = None

    def open_rim(self):
        self.packed = [[jnp.zeros((8, 128), F32) for _ in range(4)] for _ in range(3)]

    def put(self, at, x, y, rim):
        data, lane, packed = self.data, self.lane, self.packed
        col = data.rim_col(x, y)
        rims = [data.rim(side, x, y) for side in range(2)]
        for field in range(4):
            value = data.main(field, x, y)
            edge = [rims[0], rims[1]]
            if field == 3 and x in (0, 3):
                value = jnp.where(self.there[x], value, 0.0)
                edge = [jnp.where(self.there[x], one, 0.0) for one in edge]
            shift = float(x - 1) if field == 0 else float(y - 2) if field == 1 else 0.0
            if shift:
                value = value + shift
                edge = [one + shift for one in edge]
            back = jnp.where(
                lane == 0, roll(edge[0], -rim_lane(field, 1, col)), roll(value, 1)
            )
            fore = jnp.where(
                lane == 127, roll(edge[1], 127 - rim_lane(field, 0, col)), roll(value, 127)
            )
            if field == 2:
                back = back - 1.0
                fore = fore + 1.0
            self.near[at * 12 + field] = back
            self.near[at * 12 + 4 + field] = value
            self.near[at * 12 + 8 + field] = fore
            if not rim:
                continue
            for side in range(2):
                spot = side * 64 + x * 8 + y
                here = lane == spot
                outer = rim_lane(field, 0 if side == 0 else 1, col)
                inner = rim_lane(field, 1 if side == 0 else 0, col)
                packed[0][field] = jnp.where(here, roll(edge[side], spot - outer), packed[0][field])
                packed[1][field] = jnp.where(here, roll(edge[side], spot - inner), packed[1][field])
                packed[2][field] = jnp.where(
                    here, roll(value, spot - (0 if side == 0 else 127)), packed[2][field]
                )

    def close_rim(self):
        sign = jnp.where(self.lane < 64, -1.0, 1.0)
        self.packed[0][2] = self.packed[0][2] + sign
        self.packed[2][2] = self.packed[2][2] - sign

    def put_rim(self, at, moved):
        for level in range(3):
            for field in range(4):
                self.near[at * 12 + level * 4 + field] = moved(self.packed[level][field])


def place_of(data, x, y):
    value = [data.main(field, x, y) for field in range(4)]
    if x != 1:
        value[0] = value[0] + float(x - 1)
    if y != 2:
        value[1] = value[1] + float(y - 2)
    return value


def add_columns(near, table, start, targets, width, center_ref, total_ref):
    def one_column(number, carry):
        target = table[start + number * (width + 1)]
        center = [center_ref[target * 4 + field] for field in range(3)]

        def one_neighbour(step, total):
            base = table[start + number * (width + 1) + 1 + step] * 12
            for level in range(3):
                for slot in range(8):
                    row = [
                        spread(near[base + level * 4 + field, pl.ds(slot, 1), :])
                        for field in range(4)
                    ]
                    dx = center[0] - row[0]
                    dy = center[1] - row[1]
                    dz = center[2] - row[2]
                    square = jnp.maximum(dx * dx + dy * dy + dz * dz, TINY)
                    radius = square * lax.rsqrt(square)
                    reach = jnp.maximum(1.0 - radius, 0.0)
                    squared = reach * reach
                    total = total + (squared * squared) * ((1.25 - reach) * row[3])
            return total

        total_ref[target] = lax.fori_loop(0, width, one_neighbour, total_ref[target])
        return carry

    lax.fori_loop(0, targets, one_column, 0)


def fill(table, start, rows):
    at = start
    for row in rows:
        for value in row:
            table[at] = value
            at += 1
    return at


def own_density_kernel(own, total, near, center, table):
    data = Near(own, own, own, own, own)
    cols = Columns(data, near)
    rows = []
    for x in range(2):
        for y in range(2):
            cols.put(x * 2 + y, x + 1, y + 2, False)
            target = x * 4 + y + 1
            rows.append([target, 0, 1, 2, 3])
            for field, value in enumerate(place_of(data, x + 1, y + 2)):
                center[target * 4 + field] = value
    fill(table, 0, rows)
    total[...] = jnp.zeros((9, 8, 128), F32)
    add_columns(near, table, 0, 4, 4, center, total)


def mid_density_kernel(own, ahead, behind, start, total, rim_center, near, center, table):
    data = Near(own, ahead, behind, own, own)
    cols = Columns(data, near)
    cols.open_rim()
    for x in range(2):
        for y in range(6):
            cols.put(x * 6 + y, x + 1, y, True)
    cols.close_rim()
    lane = lanes()
    in_first = (lane & 63) < 16
    for step in range(3):
        cols.put_rim(12 + step, lambda v: roll(v, 1 - step))
        cols.put_rim(
            15 + step,
            lambda v: jnp.where(in_first, roll(v, 1 - step - 8), roll(v, 1 - step + 8)),
        )
    for field in range(4):
        center[8 * 4 + field] = cols.packed[1][field]
        rim_center[field] = cols.packed[1][field]
    outer, inner = [], []
    for x in range(2):
        for y in range(4):
            target = x * 4 + y
            for field, value in enumerate(place_of(data, x + 1, y + 1)):
                center[target * 4 + field] = value
            if y in (0, 3):
                outer.append([target] + [sx * 6 + y + dy for sx in range(2) for dy in range(3)])
            else:
                far = 1 if y == 1 else 4
                inner.append([target] + [sx * 6 + far for sx in range(2)])
    outer.append([8] + [12 + k for k in range(6)])
    total[...] = start[...]
    at = fill(table, 0, outer)
    fill(table, at, inner)
    add_columns(near, table, 0, 5, 6, center, total)
    add_columns(near, table, at, 4, 2, center, total)


def far_own_kernel(place, own, ahead, behind, left, right, start, out, near, center, table, total):
    data = Near(own, ahead, behind, left, right)
    cols = Columns(data, near, place[0] > 0, place[0] < 7)
    for x in range(2):
        for y in range(4):
            cols.put(x * 4 + y, x * 3, y + 1, False)
    rows = []
    for x in range(2):
        for y in (1, 2):
            target = x * 4 + y
            for field, value in enumerate(place_of(data, x + 1, y + 1)):
                center[target * 4 + field] = value
            rows.append([target] + [x * 4 + y - 1 + dy for dy in range(3)])
            total[target] = start[target]
    fill(table, 0, rows)
    add_columns(near, table, 0, 4, 3, center, total)
    for x in range(2):
        for y in (1, 2):
            press, inverse, pressure = finish(total[x * 4 + y], center[(x * 4 + y) * 4 + 3])
            at = (x * 2 + y - 1) * 3
            out[at] = press
            out[at + 1] = inverse
            out[at + 2] = pressure


def far_rest_kernel(
    place, own, ahead, behind, left, right, start, rim_center, own_fields, out, near, center, table, total
):
    data = Near(own, ahead, behind, left, right)
    cols = Columns(data, near, place[0] > 0, place[0] < 7)
    cols.open_rim()
    for x in range(2):
        for y in range(6):
            cols.put(x * 6 + y, x * 3, y, True)
    cols.close_rim()
    in_first = (lanes() & 63) < 16
    for step in range(3):
        cols.put_rim(
            12 + step,
            lambda v: jnp.where(in_first, roll(v, 1 - step + 8), roll(v, 1 - step - 8)),
        )
    rows = []
    for x in range(2):
        for y in (0, 3):
            target = x * 4 + y
            for field, value in enumerate(place_of(data, x + 1, y + 1)):
                center[target * 4 + field] = value
            rows.append([target] + [x * 6 + y + dy for dy in range(3)])
            total[target] = start[target]
    for field in range(4):
        center[8 * 4 + field] = rim_center[field]
    total[8] = start[8]
    rows.append([8, 12, 13, 14])
    fill(table, 0, rows)
    add_columns(near, table, 0, 5, 3, center, total)
    for target in (0, 3, 4, 7, 8):
        press, inverse, _ = finish(total[target], center[target * 4 + 3])
        out[target * 2] = press
        out[target * 2 + 1] = inverse
    for x in range(2):
        for y in range(2):
            for k in range(2):
                out[(x * 4 + y + 1) * 2 + k] = own_fields[(x * 2 + y) * 3 + k]


def finish(total, mass):
    density = (4.0 * NORMING) * total
    alive = mass > 0.0
    live = jnp.where(alive, 1.0, 0.0)
    safe = jnp.where(alive, density, 1.0)
    pressure = (density - REST_DENSITY) * live
    return pressure / (safe * safe), live / safe, pressure


def force_kernel(place, own, ahead, behind, left, right, fields, fleft, fright, reaction, out, near):
    lane = lanes()
    first = lane == 0
    last = lane == 127
    data = Near(own, ahead, behind, left, right)
    has_left = place[0] > 0
    has_right = place[0] < 7
    for x in range(4):
        for y in range(1, 5):
            col = data.rim_col(x, y)
            rims = [data.rim(side, x, y) for side in range(2)]
            source = fields if x in (1, 2) else fleft if x == 0 else fright
            far_x = (1, 0, 1, 0)[x]
            target = far_x * 4 + y - 1
            extra = []
            for which in range(2):
                value = source[target * 2 + which]
                halo = source[16 + which]
                extra.append((value, halo))
            levels = [[], [], []]
            for field in range(7):
                value = data.main(field, x, y)
                edge = [rims[0], rims[1]]
                if field == 3 and x in (0, 3):
                    there = has_left if x == 0 else has_right
                    value = jnp.where(there, value, 0.0)
                    edge = [jnp.where(there, one, 0.0) for one in edge]
                back = jnp.where(first, roll(edge[0], -rim_lane(field, 1, col)), roll(value, 1))
                fore = jnp.where(last, roll(edge[1], 127 - rim_lane(field, 0, col)), roll(value, 127))
                shift = float(x - 1) if field == 0 else float(y - 2) if field == 1 else 0.0
                if shift:
                    value, back, fore = value + shift, back + shift, fore + shift
                if field == 2:
                    back = back - 1.0
                    fore = fore + 1.0
                for level, one in enumerate((back, value, fore)):
                    levels[level].append(one)
            spot = (far_x + 1) * 8 + y
            for value, halo in extra:
                back = jnp.where(first, roll(halo, -spot), roll(value, 1))
                fore = jnp.where(last, roll(halo, 127 - 64 - spot), roll(value, 127))
                for level, one in enumerate((back, value, fore)):
                    levels[level].append(one)
            for level in range(3):
                px, py, pz, m, vx, vy, vz, press, inverse = levels[level]
                at = ((x * 4 + y - 1) * 3 + level) * 9
                for k, one in enumerate((px, py, pz, m, m * press, m * inverse, vx, vy, vz)):
                    near[at + k] = one

    def one_column(target, carry):
        a = target // 2
        b = target % 2
        middle = (((a + 1) * 4 + b + 1) * 3 + 1) * 9
        center = [near[middle + k] for k in range(3)]
        press = fields[(a * 4 + b + 1) * 2]
        inverse = fields[(a * 4 + b + 1) * 2 + 1]

        def one_neighbour(step, total):
            base = (((a + step // 3) * 4 + b + step % 3) * 3) * 9
            total = list(total)
            for level in range(3):
                for slot in range(8):
                    row = [
                        spread(near[base + level * 9 + k, pl.ds(slot, 1), :]) for k in range(9)
                    ]
                    dx = center[0] - row[0]
                    dy = center[1] - row[1]
                    dz = center[2] - row[2]
                    square = dx * dx + dy * dy + dz * dz
                    guarded = jnp.maximum(square, TINY)
                    radius = guarded * lax.rsqrt(guarded)
                    reach = jnp.maximum(1.0 - radius, 0.0)
                    cubed = reach * reach * reach
                    push = cubed * (row[3] * press + row[4])
                    soft = pltpu.reciprocal(square + SOFTENING, approx=True)
                    drag = (cubed * row[5]) * (square * soft)
                    total[0] = total[0] + push * dx
                    total[1] = total[1] + push * dy
                    total[2] = total[2] + push * dz
                    total[3] = total[3] + drag
                    total[4] = total[4] + drag * row[6]
                    total[5] = total[5] + drag * row[7]
                    total[6] = total[6] + drag * row[8]
            return tuple(total)

        zero = jnp.zeros((8, 128), F32)
        total = lax.fori_loop(0, 9, one_neighbour, (zero,) * 7)
        live = jnp.where(near[middle + 3] > 0.0, 1.0, 0.0)
        for d in range(3):
            slow = inverse * (near[middle + 6 + d] * total[3] - total[4 + d])
            force = 20.0 * NORMING * (total[d] - slow)
            if d == 2:
                force = force - GRAVITY
            out[pl.ds(d * 32 + target, 8, stride=4), :] = live * force + reaction[d * 4 + target]
        return carry

    lax.fori_loop(0, 4, one_column, 0)


def pair_kernel(own, fields, arrived, cells, send, reaction, left, hot):
    for peer in range(16):
        index = cells[pl.ds(peer, 1), :]
        at_row = index & 127
        at = spread(at_row)
        col_of = spread(index >> 7)
        found = None
        for col in range(4):
            mid = col * 3
            inverse = fields[mid + 1]
            tables = [own[col * 7 + k] for k in (0, 1, 2, 4, 5, 6)]
            tables += [own[col * 7 + 3] * inverse, fields[mid + 2], inverse]
            got = [lane_gather(one, at) for one in tables]
            if found is None:
                found = got
            else:
                here = col_of == col
                found = [jnp.where(here, new, old) for new, old in zip(got, found)]
        row = [spread(arrived[peer * 3 + k // 4, pl.ds(k % 4, 1), :]) for k in range(7)]
        delta = [row[d] - found[d] for d in range(3)]
        square = jnp.maximum(delta[0] * delta[0] + delta[1] * delta[1] + delta[2] * delta[2], TINY)
        radius = square * lax.rsqrt(square)
        reach = jnp.maximum(1.0 - radius, 0.0)
        cubed = reach * reach * reach
        weight = (DRAG_RATE * NORMING) * cubed * reach * (4.0 * radius + 1.0)
        push = (20.0 * NORMING) * found[7] * cubed
        hot[:, peer * 128 : peer * 128 + 128] = hot_rows(at_row)
        for d in range(3):
            bracket = row[6] * (push * delta[d] + weight * (found[3 + d] - row[3 + d]))
            send[peer, pl.ds(d, 1), :] = jnp.sum(found[6] * bracket, axis=0, keepdims=True)
            both = split_rows(-found[8] * bracket)
            col_both = jnp.concatenate([col_of, col_of], axis=0)
            for col in range(4):
                at16 = (d * 4 + col) * 16
                left[at16 : at16 + 16, peer * 128 : peer * 128 + 128] = jnp.where(
                    col_both == col, both, 0.0
                ).astype(BF16)
        send[peer, pl.ds(3, 1), :] = jnp.zeros((1, 128), F32)
    sums = scatter_dot(left[...], hot[...])
    for k in range(12):
        reaction[k] = sums[k * 16 : k * 16 + 8] + sums[k * 16 + 8 : k * 16 + 16]


def contact_kernel(place, live_count, own, ahead, behind, left, right, listed, out, rims, turned, rows, lhs, hot):
    lane = lanes()
    sub = subs()
    has_left = place[0] > 0
    has_right = place[0] < 7
    def far_line(field, row):
        slot, x, y = row // 16, row // 4 % 4, row % 4
        if x in (1, 2):
            source = (ahead, own, own, behind)[y]
            at = slot * 4 + (x - 1) * 2 + (1, 0, 1, 0)[y]
            return source[Y_GRAIN + field, pl.ds(at, 1), :]
        source = left if x == 0 else right
        return source[X_GRAIN + field, pl.ds(slot * 4 + y, 1), :]

    for side in range(2):
        rims[...] = jnp.zeros((128, 128), F32)
        for part, source in enumerate((own, ahead, behind)):
            rims[pl.ds(part * 8, 8), :] = source[Y_RIM + side]
            rims[pl.ds((3 + part) * 8, 8), :] = jnp.where(
                has_left, left[X_RIM + part * 2 + side], 0.0
            )
            rims[pl.ds((6 + part) * 8, 8), :] = jnp.where(
                has_right, right[X_RIM + part * 2 + side], 0.0
            )
        turned[side] = jnp.transpose(rims[...])

    def one_group(group):
        start = group * 8
        one = listed[pl.ds(start, 8), :]
        two = listed[pl.ds(start + 48, 8), :]
        own_row = one >> 7
        own_c = one & 127
        far_row = (two * 4033) >> 19
        far_c = two - far_row * 130
        far_slot = far_row >> 4
        far_x = (far_row >> 2) & 3
        far_y = far_row & 3
        far_at = jnp.clip(far_c - 1, 0, 127)
        x_part = jnp.where(far_x == 0, 1, jnp.where(far_x == 3, 2, 0))
        y_part = jnp.where(far_y == 0, 1, jnp.where(far_y == 3, 2, 0))
        rim_a = jnp.where(far_x == 0, 1, jnp.where(far_x == 3, 0, far_x - 1))
        rim_b = jnp.where(far_y == 0, 1, jnp.where(far_y == 3, 0, far_y - 1))
        rim_at = (x_part * 3 + y_part) * 8 + far_slot * 4 + rim_a * 2 + rim_b
        own_found = [jnp.zeros((8, 128), F32) for _ in range(7)]
        for row in range(8):
            here = own_row == row
            for field in range(7):
                got = lane_gather(spread(own[Y_GRAIN + field, pl.ds(row, 1), :]), own_c)
                own_found[field] = jnp.where(here, got, own_found[field])
        far_found = [jnp.zeros((8, 128), F32) for _ in range(7)]
        for row in range(32):
            here = far_row == row
            if row // 4 % 4 in (0, 3):
                here = jnp.logical_and(here, has_left if row // 4 % 4 == 0 else has_right)
            for field in range(7):
                got = lane_gather(spread(far_line(field, row)), far_at)
                far_found[field] = jnp.where(here, got, far_found[field])
        for side, edge in ((0, 0), (1, 129)):
            here = far_c == edge
            for field in range(7):
                got = lane_gather(
                    spread(turned[side, pl.ds(GRAIN_LANE + field, 1), :]), rim_at
                )
                far_found[field] = jnp.where(here, got, far_found[field])
        shift = [
            (((own_row >> 1) & 1) - far_x + 1).astype(F32),
            ((own_row & 1) - far_y + 1).astype(F32),
            (own_c - far_c + 1).astype(F32),
        ]
        delta = [own_found[d] - far_found[d] + shift[d] for d in range(3)]
        distance = jnp.sqrt(
            delta[0] * delta[0] + delta[1] * delta[1] + delta[2] * delta[2] + SOFTENING
        )
        normal = [one_delta / distance for one_delta in delta]
        both = own_found[6] + far_found[6]
        overlap = (both - distance) / SOFT_WIDTH
        stiff = SPRING * own_found[6] * far_found[6] / both
        closing = sum((own_found[3 + d] - far_found[3 + d]) * normal[d] for d in range(3))
        soft = jnp.maximum(overlap, 0.0) + jnp.log1p(jnp.exp(-jnp.abs(overlap)))
        number = group * 1024 + sub * 128 + lane
        magnitude = jnp.where(
            number < live_count[0], stiff * (SOFT_WIDTH * soft - DAMPING * closing), 0.0
        )
        force = [magnitude * normal[d] for d in range(3)]
        values = force + [
            force[0] * normal[0],
            force[1] * normal[1],
            force[2] * normal[2],
            force[0] * normal[1],
            force[0] * normal[2],
            force[1] * normal[2],
        ]
        for k in range(9):
            high = values[k].astype(BF16).astype(F32)
            rows[group, pl.ds(k * 16, 8), :] = high
            rows[group, pl.ds(k * 16 + 8, 8), :] = values[k] - high
        for s in range(8):
            at = pl.ds((group * 8 + s) * 128, 128)
            mine = spread(own_row[s : s + 1]) == sub
            hot[:, at] = hot_rows(own_c[s : s + 1])
            for k in range(9):
                high = spread(rows[group, pl.ds(k * 16 + s, 1), :])
                low = spread(rows[group, pl.ds(k * 16 + 8 + s, 1), :])
                pair = jnp.concatenate(
                    [jnp.where(mine, high, 0.0), jnp.where(mine, low, 0.0)], axis=0
                )
                lhs[k * 16 : k * 16 + 16, at] = pair.astype(BF16)

    for group in range(6):
        one_group(group)
    sums = scatter_dot(lhs[...], hot[...])
    for k in range(9):
        out[k] = sums[k * 16 : k * 16 + 8] + sums[k * 16 + 8 : k * 16 + 16]


def grain_kernel(back, grain, contact, radius_ref, force_out, stress_out, lhs, hot):
    sub = subs()
    for peer in range(16):
        index = grain[pl.ds(peer, 1), :]
        mine = spread(index >> 7) == sub
        hot[:, peer * 128 : peer * 128 + 128] = hot_rows(index & 127)
        for d in range(3):
            value = jnp.where(mine, spread(back[peer, pl.ds(d, 1), :]), 0.0)
            lhs[d * 16 : d * 16 + 16, peer * 128 : peer * 128 + 128] = split_rows(value).astype(BF16)
    sums = scatter_dot(lhs[...], hot[...])
    radius = radius_ref[...]
    volume = VOLUME_FACTOR * radius * radius * radius
    for d in range(3):
        value = contact[d] + (sums[d * 16 : d * 16 + 8] + sums[d * 16 + 8 : d * 16 + 16])
        if d == 2:
            value = value - GRAIN_WEIGHT * volume
        force_out[pl.ds(d * 8, 8), :] = value
    scale = radius / volume
    for k in range(6):
        stress_out[pl.ds(k * 8, 8), :] = -contact[3 + k] * scale


def density_scratch(columns):
    return [
        pltpu.VMEM((columns * 12, 8, 128), F32),
        pltpu.VMEM((36, 8, 128), F32),
        pltpu.SMEM((64,), jnp.int32),
    ]


def along_y(value, step):
    count = lax.axis_size("gy")
    pairs = [(i, i + step) for i in range(count) if 0 <= i + step < count]
    return lax.ppermute(value, "gy", pairs)


def along_x(value, step):
    count = lax.axis_size("gx")
    return lax.ppermute(value, "gx", [(i, (i + step) % count) for i in range(count)])


def body(
    sph_pos,
    sph_vel,
    sph_mass,
    cell_count,
    grain_pos,
    grain_vel,
    grain_radius,
    contact_pairs,
    contact_count,
    iface_grain,
    iface_offset,
    pair_count,
    iface_cell,
):
    place = jnp.stack(
        [lax.axis_index("gx"), lax.axis_index("gy"), lax.axis_index("gz")]
    ).astype(jnp.int32)
    radius = grain_radius.reshape(8, 128)
    route_grain = iface_grain.reshape(16, 128)
    send, own = call(
        pack_kernel,
        [shape(192, 128), shape(Y_TILES, 8, 128)],
        ins=[S, S] + [pl.BlockSpec(memory_space=pltpu.HBM)] * 9,
        scratch=[pltpu.VMEM((rows, 128), F32) for rows in (96, 96, 32)]
        + [pltpu.VMEM((4, 128), jnp.int32)]
        + [pltpu.VMEM((rows, 128), F32) for rows in (24, 24, 8)]
        + [pltpu.VMEM((16, 128), jnp.int32), pltpu.VMEM((48, 128), F32)]
        + [pltpu.SemaphoreType.DMA((9,))],
        cost=cost(3),
        limit=None,
    )(
        place,
        pair_count.reshape(16),
        sph_pos.reshape(96, 128),
        sph_vel.reshape(96, 128),
        sph_mass.reshape(32, 128),
        cell_count.reshape(4, 128),
        grain_pos.reshape(24, 128),
        grain_vel.reshape(24, 128),
        radius,
        route_grain,
        iface_offset.reshape(48, 128),
    )
    arrived = lax.all_to_all(
        send.reshape(16, 3, 4, 128), "gz", split_axis=0, concat_axis=0, tiled=True
    ).reshape(48, 4, 128)
    own = call(
        rim_kernel,
        shape(Y_TILES, 8, 128),
        ins=[S, V, pl.BlockSpec(memory_space=pl.ANY)],
        alias={2: 0},
        grid=(2,),
        out_specs=[pl.BlockSpec((1, 8, 128), lambda i: (Y_RIM + i, 0, 0))],
        cost=cost(1),
    )(place, arrived, own)
    ahead = along_y(own, 1)
    behind = along_y(own, -1)
    own_total = call(
        own_density_kernel,
        shape(9, 8, 128),
        ins=[V],
        scratch=density_scratch(4),
        cost=cost(3),
    )(own)
    ahead, behind, own_total = lax.optimization_barrier((ahead, behind, own_total))
    up, down = call(
        widen_kernel,
        [shape(X_TILES, 8, 128)] * 2,
        ins=[V] * 3,
        cost=cost(1),
    )(own, ahead, behind)
    left = along_x(up, 1)
    right = along_x(down, -1)
    mid_total, rim_center = call(
        mid_density_kernel,
        [shape(9, 8, 128), shape(4, 8, 128)],
        ins=[V] * 4,
        scratch=density_scratch(18),
        cost=cost(6),
    )(own, ahead, behind, own_total)
    own_fields = call(
        far_own_kernel,
        shape(12, 8, 128),
        ins=[S] + [V] * 6,
        scratch=density_scratch(8) + [pltpu.VMEM((9, 8, 128), F32)],
        cost=cost(2),
    )(place, own, ahead, behind, left, right, mid_total)
    send_back, reaction = call(
        pair_kernel,
        [shape(16, 4, 128), shape(12, 8, 128)],
        ins=[V] * 4,
        scratch=[pltpu.VMEM((192, 2048), BF16), pltpu.VMEM((128, 2048), BF16)],
        cost=cost(3),
    )(own, own_fields, arrived, iface_cell.reshape(16, 128))
    fields = call(
        far_rest_kernel,
        shape(18, 8, 128),
        ins=[S] + [V] * 8,
        scratch=density_scratch(15) + [pltpu.VMEM((9, 8, 128), F32)],
        cost=cost(3),
    )(place, own, ahead, behind, left, right, mid_total, rim_center, own_fields)
    fields_left = along_x(fields, 1)
    fields_right = along_x(fields, -1)
    back = lax.all_to_all(send_back, "gz", split_axis=0, concat_axis=0, tiled=True)
    contact = call(
        contact_kernel,
        shape(9, 8, 128),
        ins=[S, S] + [V] * 6,
        scratch=[
            pltpu.VMEM((128, 128), F32),
            pltpu.VMEM((2, 128, 128), F32),
            pltpu.VMEM((6, 144, 128), F32),
            pltpu.VMEM((144, 6144), BF16),
            pltpu.VMEM((128, 6144), BF16),
        ],
        cost=cost(6),
    )(
        place,
        contact_count.reshape(1),
        own,
        ahead,
        behind,
        left,
        right,
        contact_pairs.reshape(96, 128),
    )
    accel = call(
        force_kernel,
        shape(96, 128),
        ins=[S] + [V] * 9,
        scratch=[pltpu.VMEM((16 * 27, 8, 128), F32)],
        cost=cost(6),
    )(place, own, ahead, behind, left, right, fields, fields_left, fields_right, reaction)
    grain_force, grain_stress = call(
        grain_kernel,
        [shape(24, 128), shape(48, 128)],
        ins=[V] * 4,
        scratch=[pltpu.VMEM((48, 2048), BF16), pltpu.VMEM((128, 2048), BF16)],
        cost=cost(2),
    )(back, route_grain, contact, radius)
    return (
        accel.reshape(sph_pos.shape),
        grain_force.reshape(grain_pos.shape),
        grain_stress.reshape((6,) + grain_radius.shape),
    )


def solution(mesh):
    return jax.shard_map(
        body,
        mesh=mesh,
        in_specs=(
            P(None, None, "gx", "gy", "gz"),
            P(None, None, "gx", "gy", "gz"),
            P(None, "gx", "gy", "gz"),
            P("gx", "gy", "gz"),
            P(None, None, "gx", "gy", "gz"),
            P(None, None, "gx", "gy", "gz"),
            P(None, "gx", "gy", "gz"),
            P(None, "gx", "gy", "gz"),
            P("gx", "gy", "gz"),
            P("gx", "gy", "gz", None),
            P(None, "gx", "gy", "gz", None),
            P("gx", "gy", "gz"),
            P("gx", "gy", "gz", None),
        ),
        out_specs=(
            P(None, None, "gx", "gy", "gz"),
            P(None, None, "gx", "gy", "gz"),
            P(None, None, "gx", "gy", "gz"),
        ),
        check_vma=False,
    )
```

```python
import math

import jax
import jax.numpy as jnp
from jax import lax
from jax.experimental import pallas as pl
from jax.experimental.pallas import tpu as pltpu
from jax.sharding import PartitionSpec as P

NORMING = 21.0 / (2.0 * math.pi)
REST_DENSITY = 6.0
GRAVITY = 1.0
DRAG_RATE = 2.0
SPRING = 20.0
SOFT_WIDTH = 0.2
DAMPING = 0.5
SOFTENING = 0.01
GRAIN_WEIGHT = 2.0
VOLUME_FACTOR = 4.0 * math.pi / 3.0
TINY = 1e-30

F32 = jnp.float32
BF16 = jnp.bfloat16
VM = pltpu.VMEM
SM = pltpu.SMEM

Y_GRAIN = 28
Y_RIM = 35
Y_TILES = 37
X_VEL = 24
X_GRAIN = 36
X_RIM = 43
X_TILES = 49
GRAIN_LANE = 56


def call(kernel, outs, scratch=(), ins=(), cost=None, alias=None, grid=None, out_specs=None, limit=24):
    single = not isinstance(outs, (list, tuple))
    count = 1 if single else len(outs)
    if out_specs is None:
        out_specs = [pl.BlockSpec(memory_space=VM)] * count
    extra = {}
    if grid is not None:
        extra["grid"] = grid
    if limit is not None:
        extra["compiler_params"] = pltpu.CompilerParams(vmem_limit_bytes=limit * 1024 * 1024)
    return pl.pallas_call(
        kernel,
        out_shape=outs,
        in_specs=list(ins),
        out_specs=out_specs[0] if single else out_specs,
        scratch_shapes=list(scratch),
        input_output_aliases=alias or {},
        cost_estimate=cost,
        **extra,
    )


def cost(micros):
    return pl.CostEstimate(flops=int(micros * 4e6), bytes_accessed=int(micros * 2e6), transcendentals=0)


V = pl.BlockSpec(memory_space=VM)
S = pl.BlockSpec(memory_space=SM)


def shape(*dims):
    return jax.ShapeDtypeStruct(dims, F32)


def lanes():
    return lax.broadcasted_iota(jnp.int32, (8, 128), 1)


def subs():
    return lax.broadcasted_iota(jnp.int32, (8, 128), 0)


def roll(value, amount):
    amount = amount % 128
    return value if amount == 0 else pltpu.roll(value, amount, 1)


def spread(row):
    return jnp.broadcast_to(row, (8, 128))


def lane_gather(table, index):
    numbers = lax.GatherDimensionNumbers(
        offset_dims=(),
        collapsed_slice_dims=(1,),
        start_index_map=(1,),
        operand_batching_dims=(0,),
        start_indices_batching_dims=(0,),
    )
    return lax.gather(
        table,
        index[..., None],
        numbers,
        slice_sizes=(1, 1),
        mode=lax.GatherScatterMode.PROMISE_IN_BOUNDS,
    )


def rim_lane(field, layer, col):
    return (field * 2 + layer) * 4 + col


def split_rows(value):
    high = value.astype(BF16).astype(F32)
    return jnp.concatenate([high, value - high], axis=0)


def scatter_dot(left, hot):
    return lax.dot_general(
        left, hot, (((1,), (1,)), ((), ())), preferred_element_type=F32
    )


def hot_rows(row):
    ids = lax.broadcasted_iota(jnp.int32, (128, 128), 0)
    return jnp.where(ids == jnp.broadcast_to(row, (128, 128)), 1.0, 0.0).astype(BF16)


def water_tile(pos, vel, mass, count, col, field):
    if field < 3:
        return pos[pl.ds(field * 32 + col, 8, stride=4), :]
    if field > 3:
        return vel[pl.ds((field - 4) * 32 + col, 8, stride=4), :]
    value = mass[pl.ds(col, 8, stride=4), :]
    return jnp.where(subs() < spread(count[pl.ds(col, 1), :]), value, 0.0)


def grain_tile(gpos, gvel, grad, field):
    if field < 3:
        return gpos[pl.ds(field * 8, 8), :]
    if field < 6:
        return gvel[pl.ds((field - 3) * 8, 8), :]
    return grad[...]


def gather_kernel(pos, vel, mass, count, gpos, gvel, grad, own):
    for col in range(4):
        for field in range(7):
            own[col * 7 + field] = water_tile(pos, vel, mass, count, col, field)
    for field in range(7):
        own[Y_GRAIN + field] = grain_tile(gpos, gvel, grad, field)
    for side in range(2):
        own[Y_RIM + side] = jnp.zeros((8, 128), F32)


def pack_kernel(counts, *refs):
    sources, send, buffers, sems = refs[:9], refs[9], refs[10:19], refs[19]
    layer_here = lax.axis_index("gz")
    copies = [
        pltpu.make_async_copy(source, buffer, sems.at[k])
        for k, (source, buffer) in enumerate(zip(sources, buffers))
    ]
    for one in copies:
        one.start()
    for one in copies:
        one.wait()
    pos, vel, mass, count, gpos, gvel, grad, grain, offset = buffers
    lane = lanes()
    sub = subs()
    low = jnp.zeros((8, 128), F32)
    high = jnp.zeros((8, 128), F32)
    for col in range(4):
        for field in range(7):
            value = water_tile(pos, vel, mass, count, col, field)
            for layer in range(2):
                at = rim_lane(field, layer, col)
                low = jnp.where(lane == at, roll(value, at - layer), low)
                high = jnp.where(lane == at, roll(value, at - 126 - layer), high)
    for field in range(7):
        value = grain_tile(gpos, gvel, grad, field)
        at = GRAIN_LANE + field
        low = jnp.where(lane == at, roll(value, at), low)
        high = jnp.where(lane == at, roll(value, at - 127), high)
    radius = grad[...]
    volume = VOLUME_FACTOR * radius * radius * radius
    tables = [gvel[pl.ds(field * 8, 8), :] for field in range(3)] + [volume]
    for group in range(2):
        index = grain[pl.ds(group * 8, 8), :]
        row = index >> 7
        at = index & 127
        found = [jnp.zeros((8, 128), F32) for _ in range(4)]
        for place_row in range(8):
            here = row == place_row
            for field in range(4):
                got = lane_gather(spread(tables[field][place_row : place_row + 1]), at)
                found[field] = jnp.where(here, got, found[field])
        alive = jnp.zeros((8, 128), jnp.int32)
        for peer in range(8):
            alive = jnp.where(sub == peer, counts[group * 8 + peer], alive)
        found[3] = jnp.where(lane < alive, found[3], 0.0)
        for field in range(3):
            send[pl.ds(group * 96 + field, 8, stride=12), :] = offset[
                pl.ds(field * 16 + group * 8, 8), :
            ]
        for field in range(4):
            send[pl.ds(group * 96 + 3 + field, 8, stride=12), :] = found[field]
        send[pl.ds(group * 96 + 7, 8, stride=12), :] = jnp.zeros((8, 128), F32)
    low, high = [
        jnp.where(lane < 64, one, pltpu.roll(roll(one, 64), 4, 0))[0:4] for one in (low, high)
    ]
    for peer in range(16):
        send[pl.ds(peer * 12 + 8, 4), :] = jnp.where(peer < layer_here, low, high)


def rim_kernel(place, arrived, own_in, own):
    step = pl.program_id(0)
    layer = place[2]
    other = jnp.where(step == 0, layer - 1, layer + 1)
    inside = jnp.logical_and(other >= 0, other <= 15)
    rows = jnp.where(inside, arrived[jnp.clip(other, 0, 15) * 3 + 2], 0.0)
    own[0] = jnp.concatenate([rows, pltpu.roll(rows, 64, 1)], axis=0)


def widen_kernel(own, ahead, behind, up, down):
    for send, a in ((up, 1), (down, 0)):
        for y in range(6):
            source = (ahead, own, behind)[y // 2]
            col = a * 2 + y % 2
            for field in range(4):
                send[y * 4 + field] = source[col * 7 + field]
        for y in range(4):
            source = (ahead, own, own, behind)[y]
            col = a * 2 + (1, 0, 1, 0)[y]
            for field in range(3):
                send[X_VEL + y * 3 + field] = source[col * 7 + 4 + field]
            for field in range(7):
                for slot in range(2):
                    send[X_GRAIN + field, pl.ds(slot * 4 + y, 1), :] = source[
                        Y_GRAIN + field, pl.ds(slot * 4 + col, 1), :
                    ]
        for part, source in enumerate((own, ahead, behind)):
            for side in range(2):
                send[X_RIM + part * 2 + side] = source[Y_RIM + side]


class Near:
    def __init__(self, own, ahead, behind, left, right):
        self.own, self.ahead, self.behind = own, ahead, behind
        self.left, self.right = left, right

    def main(self, field, x, y):
        if x in (1, 2):
            source = (self.ahead, self.own, self.behind)[y // 2]
            return source[((x - 1) * 2 + y % 2) * 7 + field]
        source = self.left if x == 0 else self.right
        if field < 4:
            return source[y * 4 + field]
        return source[X_VEL + (y - 1) * 3 + field - 4]

    def rim(self, side, x, y):
        part = (1, 0, 2)[y // 2]
        if x in (1, 2):
            return (self.own, self.ahead, self.behind)[part][Y_RIM + side]
        source = self.left if x == 0 else self.right
        return source[X_RIM + part * 2 + side]

    def rim_col(self, x, y):
        return (1, 0, 1, 0)[x] * 2 + y % 2


class Columns:
    def __init__(self, data, near, has_left=None, has_right=None):
        self.data, self.near = data, near
        self.there = {0: has_left, 3: has_right}
        self.lane = lanes()
        self.packed = None

    def open_rim(self):
        self.packed = [[jnp.zeros((8, 128), F32) for _ in range(4)] for _ in range(3)]

    def put(self, at, x, y, rim):
        data, lane, packed = self.data, self.lane, self.packed
        col = data.rim_col(x, y)
        rims = [data.rim(side, x, y) for side in range(2)]
        for field in range(4):
            value = data.main(field, x, y)
            edge = [rims[0], rims[1]]
            if field == 3 and x in (0, 3):
                value = jnp.where(self.there[x], value, 0.0)
                edge = [jnp.where(self.there[x], one, 0.0) for one in edge]
            shift = float(x - 1) if field == 0 else float(y - 2) if field == 1 else 0.0
            if shift:
                value = value + shift
                edge = [one + shift for one in edge]
            back = jnp.where(
                lane == 0, roll(edge[0], -rim_lane(field, 1, col)), roll(value, 1)
            )
            fore = jnp.where(
                lane == 127, roll(edge[1], 127 - rim_lane(field, 0, col)), roll(value, 127)
            )
            if field == 2:
                back = back - 1.0
                fore = fore + 1.0
            self.near[at * 12 + field] = back
            self.near[at * 12 + 4 + field] = value
            self.near[at * 12 + 8 + field] = fore
            if not rim:
                continue
            for side in range(2):
                spot = side * 64 + x * 8 + y
                here = lane == spot
                outer = rim_lane(field, 0 if side == 0 else 1, col)
                inner = rim_lane(field, 1 if side == 0 else 0, col)
                packed[0][field] = jnp.where(here, roll(edge[side], spot - outer), packed[0][field])
                packed[1][field] = jnp.where(here, roll(edge[side], spot - inner), packed[1][field])
                packed[2][field] = jnp.where(
                    here, roll(value, spot - (0 if side == 0 else 127)), packed[2][field]
                )

    def close_rim(self):
        sign = jnp.where(self.lane < 64, -1.0, 1.0)
        self.packed[0][2] = self.packed[0][2] + sign
        self.packed[2][2] = self.packed[2][2] - sign

    def put_rim(self, at, moved):
        for level in range(3):
            for field in range(4):
                self.near[at * 12 + level * 4 + field] = moved(self.packed[level][field])


def place_of(data, x, y):
    value = [data.main(field, x, y) for field in range(4)]
    if x != 1:
        value[0] = value[0] + float(x - 1)
    if y != 2:
        value[1] = value[1] + float(y - 2)
    return value


def add_columns(near, table, start, targets, width, center_ref, total_ref):
    def one_column(number, carry):
        target = table[start + number * (width + 1)]
        center = [center_ref[target * 4 + field] for field in range(3)]

        def one_neighbour(step, total):
            base = table[start + number * (width + 1) + 1 + step] * 12
            for level in range(3):
                for slot in range(8):
                    row = [
                        spread(near[base + level * 4 + field, pl.ds(slot, 1), :])
                        for field in range(4)
                    ]
                    dx = center[0] - row[0]
                    dy = center[1] - row[1]
                    dz = center[2] - row[2]
                    square = jnp.maximum(dx * dx + dy * dy + dz * dz, TINY)
                    radius = square * lax.rsqrt(square)
                    reach = jnp.maximum(1.0 - radius, 0.0)
                    squared = reach * reach
                    total = total + (squared * squared) * ((1.25 - reach) * row[3])
            return total

        total_ref[target] = lax.fori_loop(0, width, one_neighbour, total_ref[target])
        return carry

    lax.fori_loop(0, targets, one_column, 0)


def fill(table, start, rows):
    at = start
    for row in rows:
        for value in row:
            table[at] = value
            at += 1
    return at


def own_density_kernel(own, total, near, center, table):
    data = Near(own, own, own, own, own)
    cols = Columns(data, near)
    rows = []
    for x in range(2):
        for y in range(2):
            cols.put(x * 2 + y, x + 1, y + 2, False)
            target = x * 4 + y + 1
            rows.append([target, 0, 1, 2, 3])
            for field, value in enumerate(place_of(data, x + 1, y + 2)):
                center[target * 4 + field] = value
    fill(table, 0, rows)
    total[...] = jnp.zeros((9, 8, 128), F32)
    add_columns(near, table, 0, 4, 4, center, total)


def mid_density_kernel(own, ahead, behind, start, total, rim_center, near, center, table):
    data = Near(own, ahead, behind, own, own)
    cols = Columns(data, near)
    cols.open_rim()
    for x in range(2):
        for y in range(6):
            cols.put(x * 6 + y, x + 1, y, True)
    cols.close_rim()
    lane = lanes()
    in_first = (lane & 63) < 16
    for step in range(3):
        cols.put_rim(12 + step, lambda v: roll(v, 1 - step))
        cols.put_rim(
            15 + step,
            lambda v: jnp.where(in_first, roll(v, 1 - step - 8), roll(v, 1 - step + 8)),
        )
    for field in range(4):
        center[8 * 4 + field] = cols.packed[1][field]
        rim_center[field] = cols.packed[1][field]
    outer, inner = [], []
    for x in range(2):
        for y in range(4):
            target = x * 4 + y
            for field, value in enumerate(place_of(data, x + 1, y + 1)):
                center[target * 4 + field] = value
            if y in (0, 3):
                outer.append([target] + [sx * 6 + y + dy for sx in range(2) for dy in range(3)])
            else:
                far = 1 if y == 1 else 4
                inner.append([target] + [sx * 6 + far for sx in range(2)])
    outer.append([8] + [12 + k for k in range(6)])
    total[...] = start[...]
    at = fill(table, 0, outer)
    fill(table, at, inner)
    add_columns(near, table, 0, 5, 6, center, total)
    add_columns(near, table, at, 4, 2, center, total)


def far_own_kernel(place, own, ahead, behind, left, right, start, out, near, center, table, total):
    data = Near(own, ahead, behind, left, right)
    cols = Columns(data, near, place[0] > 0, place[0] < 7)
    for x in range(2):
        for y in range(4):
            cols.put(x * 4 + y, x * 3, y + 1, False)
    rows = []
    for x in range(2):
        for y in (1, 2):
            target = x * 4 + y
            for field, value in enumerate(place_of(data, x + 1, y + 1)):
                center[target * 4 + field] = value
            rows.append([target] + [x * 4 + y - 1 + dy for dy in range(3)])
            total[target] = start[target]
    fill(table, 0, rows)
    add_columns(near, table, 0, 4, 3, center, total)
    for x in range(2):
        for y in (1, 2):
            press, inverse, pressure = finish(total[x * 4 + y], center[(x * 4 + y) * 4 + 3])
            at = (x * 2 + y - 1) * 3
            out[at] = press
            out[at + 1] = inverse
            out[at + 2] = pressure


def far_rest_kernel(
    place, own, ahead, behind, left, right, start, rim_center, own_fields, out, near, center, table, total
):
    data = Near(own, ahead, behind, left, right)
    cols = Columns(data, near, place[0] > 0, place[0] < 7)
    cols.open_rim()
    for x in range(2):
        for y in range(6):
            cols.put(x * 6 + y, x * 3, y, True)
    cols.close_rim()
    in_first = (lanes() & 63) < 16
    for step in range(3):
        cols.put_rim(
            12 + step,
            lambda v: jnp.where(in_first, roll(v, 1 - step + 8), roll(v, 1 - step - 8)),
        )
    rows = []
    for x in range(2):
        for y in (0, 3):
            target = x * 4 + y
            for field, value in enumerate(place_of(data, x + 1, y + 1)):
                center[target * 4 + field] = value
            rows.append([target] + [x * 6 + y + dy for dy in range(3)])
            total[target] = start[target]
    for field in range(4):
        center[8 * 4 + field] = rim_center[field]
    total[8] = start[8]
    rows.append([8, 12, 13, 14])
    fill(table, 0, rows)
    add_columns(near, table, 0, 5, 3, center, total)
    for target in (0, 3, 4, 7, 8):
        press, inverse, _ = finish(total[target], center[target * 4 + 3])
        out[target * 2] = press
        out[target * 2 + 1] = inverse
    for x in range(2):
        for y in range(2):
            for k in range(2):
                out[(x * 4 + y + 1) * 2 + k] = own_fields[(x * 2 + y) * 3 + k]


def finish(total, mass):
    density = (4.0 * NORMING) * total
    alive = mass > 0.0
    live = jnp.where(alive, 1.0, 0.0)
    safe = jnp.where(alive, density, 1.0)
    pressure = (density - REST_DENSITY) * live
    return pressure / (safe * safe), live / safe, pressure


def force_kernel(place, own, ahead, behind, left, right, fields, fleft, fright, reaction, out, near):
    lane = lanes()
    first = lane == 0
    last = lane == 127
    data = Near(own, ahead, behind, left, right)
    has_left = place[0] > 0
    has_right = place[0] < 7
    for x in range(4):
        for y in range(1, 5):
            col = data.rim_col(x, y)
            rims = [data.rim(side, x, y) for side in range(2)]
            source = fields if x in (1, 2) else fleft if x == 0 else fright
            far_x = (1, 0, 1, 0)[x]
            target = far_x * 4 + y - 1
            extra = []
            for which in range(2):
                value = source[target * 2 + which]
                halo = source[16 + which]
                extra.append((value, halo))
            levels = [[], [], []]
            for field in range(7):
                value = data.main(field, x, y)
                edge = [rims[0], rims[1]]
                if field == 3 and x in (0, 3):
                    there = has_left if x == 0 else has_right
                    value = jnp.where(there, value, 0.0)
                    edge = [jnp.where(there, one, 0.0) for one in edge]
                back = jnp.where(first, roll(edge[0], -rim_lane(field, 1, col)), roll(value, 1))
                fore = jnp.where(last, roll(edge[1], 127 - rim_lane(field, 0, col)), roll(value, 127))
                shift = float(x - 1) if field == 0 else float(y - 2) if field == 1 else 0.0
                if shift:
                    value, back, fore = value + shift, back + shift, fore + shift
                if field == 2:
                    back = back - 1.0
                    fore = fore + 1.0
                for level, one in enumerate((back, value, fore)):
                    levels[level].append(one)
            spot = (far_x + 1) * 8 + y
            for value, halo in extra:
                back = jnp.where(first, roll(halo, -spot), roll(value, 1))
                fore = jnp.where(last, roll(halo, 127 - 64 - spot), roll(value, 127))
                for level, one in enumerate((back, value, fore)):
                    levels[level].append(one)
            for level in range(3):
                px, py, pz, m, vx, vy, vz, press, inverse = levels[level]
                at = ((x * 4 + y - 1) * 3 + level) * 9
                for k, one in enumerate((px, py, pz, m, m * press, m * inverse, vx, vy, vz)):
                    near[at + k] = one

    def one_column(target, carry):
        a = target // 2
        b = target % 2
        middle = (((a + 1) * 4 + b + 1) * 3 + 1) * 9
        center = [near[middle + k] for k in range(3)]
        press = fields[(a * 4 + b + 1) * 2]
        inverse = fields[(a * 4 + b + 1) * 2 + 1]

        def one_neighbour(step, total):
            base = (((a + step // 3) * 4 + b + step % 3) * 3) * 9
            total = list(total)
            for level in range(3):
                for slot in range(8):
                    row = [
                        spread(near[base + level * 9 + k, pl.ds(slot, 1), :]) for k in range(9)
                    ]
                    dx = center[0] - row[0]
                    dy = center[1] - row[1]
                    dz = center[2] - row[2]
                    square = dx * dx + dy * dy + dz * dz
                    guarded = jnp.maximum(square, TINY)
                    radius = guarded * lax.rsqrt(guarded)
                    reach = jnp.maximum(1.0 - radius, 0.0)
                    cubed = reach * reach * reach
                    push = cubed * (row[3] * press + row[4])
                    soft = pltpu.reciprocal(square + SOFTENING, approx=True)
                    drag = (cubed * row[5]) * (square * soft)
                    total[0] = total[0] + push * dx
                    total[1] = total[1] + push * dy
                    total[2] = total[2] + push * dz
                    total[3] = total[3] + drag
                    total[4] = total[4] + drag * row[6]
                    total[5] = total[5] + drag * row[7]
                    total[6] = total[6] + drag * row[8]
            return tuple(total)

        zero = jnp.zeros((8, 128), F32)
        total = lax.fori_loop(0, 9, one_neighbour, (zero,) * 7)
        live = jnp.where(near[middle + 3] > 0.0, 1.0, 0.0)
        for d in range(3):
            slow = inverse * (near[middle + 6 + d] * total[3] - total[4 + d])
            force = 20.0 * NORMING * (total[d] - slow)
            if d == 2:
                force = force - GRAVITY
            out[pl.ds(d * 32 + target, 8, stride=4), :] = live * force + reaction[d * 4 + target]
        return carry

    lax.fori_loop(0, 4, one_column, 0)


def pair_kernel(own, fields, arrived, cells, send, reaction, left, hot):
    for peer in range(16):
        index = cells[pl.ds(peer, 1), :]
        at_row = index & 127
        at = spread(at_row)
        col_of = spread(index >> 7)
        found = None
        for col in range(4):
            mid = col * 3
            inverse = fields[mid + 1]
            tables = [own[col * 7 + k] for k in (0, 1, 2, 4, 5, 6)]
            tables += [own[col * 7 + 3] * inverse, fields[mid + 2], inverse]
            got = [lane_gather(one, at) for one in tables]
            if found is None:
                found = got
            else:
                here = col_of == col
                found = [jnp.where(here, new, old) for new, old in zip(got, found)]
        row = [spread(arrived[peer * 3 + k // 4, pl.ds(k % 4, 1), :]) for k in range(7)]
        delta = [row[d] - found[d] for d in range(3)]
        square = jnp.maximum(delta[0] * delta[0] + delta[1] * delta[1] + delta[2] * delta[2], TINY)
        radius = square * lax.rsqrt(square)
        reach = jnp.maximum(1.0 - radius, 0.0)
        cubed = reach * reach * reach
        weight = (DRAG_RATE * NORMING) * cubed * reach * (4.0 * radius + 1.0)
        push = (20.0 * NORMING) * found[7] * cubed
        hot[:, peer * 128 : peer * 128 + 128] = hot_rows(at_row)
        for d in range(3):
            bracket = row[6] * (push * delta[d] + weight * (found[3 + d] - row[3 + d]))
            send[peer, pl.ds(d, 1), :] = jnp.sum(found[6] * bracket, axis=0, keepdims=True)
            both = split_rows(-found[8] * bracket)
            col_both = jnp.concatenate([col_of, col_of], axis=0)
            for col in range(4):
                at16 = (d * 4 + col) * 16
                left[at16 : at16 + 16, peer * 128 : peer * 128 + 128] = jnp.where(
                    col_both == col, both, 0.0
                ).astype(BF16)
        send[peer, pl.ds(3, 1), :] = jnp.zeros((1, 128), F32)
    sums = scatter_dot(left[...], hot[...])
    for k in range(12):
        reaction[k] = sums[k * 16 : k * 16 + 8] + sums[k * 16 + 8 : k * 16 + 16]


def contact_kernel(place, live_count, own, ahead, behind, left, right, listed, out, rims, turned, rows, lhs, hot):
    lane = lanes()
    sub = subs()
    has_left = place[0] > 0
    has_right = place[0] < 7
    def far_line(field, row):
        slot, x, y = row // 16, row // 4 % 4, row % 4
        if x in (1, 2):
            source = (ahead, own, own, behind)[y]
            at = slot * 4 + (x - 1) * 2 + (1, 0, 1, 0)[y]
            return source[Y_GRAIN + field, pl.ds(at, 1), :]
        source = left if x == 0 else right
        return source[X_GRAIN + field, pl.ds(slot * 4 + y, 1), :]

    for side in range(2):
        rims[...] = jnp.zeros((128, 128), F32)
        for part, source in enumerate((own, ahead, behind)):
            rims[pl.ds(part * 8, 8), :] = source[Y_RIM + side]
            rims[pl.ds((3 + part) * 8, 8), :] = jnp.where(
                has_left, left[X_RIM + part * 2 + side], 0.0
            )
            rims[pl.ds((6 + part) * 8, 8), :] = jnp.where(
                has_right, right[X_RIM + part * 2 + side], 0.0
            )
        turned[side] = jnp.transpose(rims[...])

    def one_group(group):
        start = group * 8
        one = listed[pl.ds(start, 8), :]
        two = listed[pl.ds(start + 48, 8), :]
        own_row = one >> 7
        own_c = one & 127
        far_row = (two * 4033) >> 19
        far_c = two - far_row * 130
        far_slot = far_row >> 4
        far_x = (far_row >> 2) & 3
        far_y = far_row & 3
        far_at = jnp.clip(far_c - 1, 0, 127)
        x_part = jnp.where(far_x == 0, 1, jnp.where(far_x == 3, 2, 0))
        y_part = jnp.where(far_y == 0, 1, jnp.where(far_y == 3, 2, 0))
        rim_a = jnp.where(far_x == 0, 1, jnp.where(far_x == 3, 0, far_x - 1))
        rim_b = jnp.where(far_y == 0, 1, jnp.where(far_y == 3, 0, far_y - 1))
        rim_at = (x_part * 3 + y_part) * 8 + far_slot * 4 + rim_a * 2 + rim_b
        own_found = [jnp.zeros((8, 128), F32) for _ in range(7)]
        for row in range(8):
            here = own_row == row
            for field in range(7):
                got = lane_gather(spread(own[Y_GRAIN + field, pl.ds(row, 1), :]), own_c)
                own_found[field] = jnp.where(here, got, own_found[field])
        far_found = [jnp.zeros((8, 128), F32) for _ in range(7)]
        for row in range(32):
            here = far_row == row
            if row // 4 % 4 in (0, 3):
                here = jnp.logical_and(here, has_left if row // 4 % 4 == 0 else has_right)
            for field in range(7):
                got = lane_gather(spread(far_line(field, row)), far_at)
                far_found[field] = jnp.where(here, got, far_found[field])
        for side, edge in ((0, 0), (1, 129)):
            here = far_c == edge
            for field in range(7):
                got = lane_gather(
                    spread(turned[side, pl.ds(GRAIN_LANE + field, 1), :]), rim_at
                )
                far_found[field] = jnp.where(here, got, far_found[field])
        shift = [
            (((own_row >> 1) & 1) - far_x + 1).astype(F32),
            ((own_row & 1) - far_y + 1).astype(F32),
            (own_c - far_c + 1).astype(F32),
        ]
        delta = [own_found[d] - far_found[d] + shift[d] for d in range(3)]
        distance = jnp.sqrt(
            delta[0] * delta[0] + delta[1] * delta[1] + delta[2] * delta[2] + SOFTENING
        )
        normal = [one_delta / distance for one_delta in delta]
        both = own_found[6] + far_found[6]
        overlap = (both - distance) / SOFT_WIDTH
        stiff = SPRING * own_found[6] * far_found[6] / both
        closing = sum((own_found[3 + d] - far_found[3 + d]) * normal[d] for d in range(3))
        soft = jnp.maximum(overlap, 0.0) + jnp.log1p(jnp.exp(-jnp.abs(overlap)))
        number = group * 1024 + sub * 128 + lane
        magnitude = jnp.where(
            number < live_count[0], stiff * (SOFT_WIDTH * soft - DAMPING * closing), 0.0
        )
        force = [magnitude * normal[d] for d in range(3)]
        values = force + [
            force[0] * normal[0],
            force[1] * normal[1],
            force[2] * normal[2],
            force[0] * normal[1],
            force[0] * normal[2],
            force[1] * normal[2],
        ]
        for k in range(9):
            high = values[k].astype(BF16).astype(F32)
            rows[group, pl.ds(k * 16, 8), :] = high
            rows[group, pl.ds(k * 16 + 8, 8), :] = values[k] - high
        for s in range(8):
            at = pl.ds((group * 8 + s) * 128, 128)
            mine = spread(own_row[s : s + 1]) == sub
            hot[:, at] = hot_rows(own_c[s : s + 1])
            for k in range(9):
                high = spread(rows[group, pl.ds(k * 16 + s, 1), :])
                low = spread(rows[group, pl.ds(k * 16 + 8 + s, 1), :])
                pair = jnp.concatenate(
                    [jnp.where(mine, high, 0.0), jnp.where(mine, low, 0.0)], axis=0
                )
                lhs[k * 16 : k * 16 + 16, at] = pair.astype(BF16)

    for group in range(6):
        one_group(group)
    sums = scatter_dot(lhs[...], hot[...])
    for k in range(9):
        out[k] = sums[k * 16 : k * 16 + 8] + sums[k * 16 + 8 : k * 16 + 16]


def grain_kernel(back, grain, contact, radius_ref, force_out, stress_out, lhs, hot):
    sub = subs()
    for peer in range(16):
        index = grain[pl.ds(peer, 1), :]
        mine = spread(index >> 7) == sub
        hot[:, peer * 128 : peer * 128 + 128] = hot_rows(index & 127)
        for d in range(3):
            value = jnp.where(mine, spread(back[peer, pl.ds(d, 1), :]), 0.0)
            lhs[d * 16 : d * 16 + 16, peer * 128 : peer * 128 + 128] = split_rows(value).astype(BF16)
    sums = scatter_dot(lhs[...], hot[...])
    radius = radius_ref[...]
    volume = VOLUME_FACTOR * radius * radius * radius
    for d in range(3):
        value = contact[d] + (sums[d * 16 : d * 16 + 8] + sums[d * 16 + 8 : d * 16 + 16])
        if d == 2:
            value = value - GRAIN_WEIGHT * volume
        force_out[pl.ds(d * 8, 8), :] = value
    scale = radius / volume
    for k in range(6):
        stress_out[pl.ds(k * 8, 8), :] = -contact[3 + k] * scale


def density_scratch(columns):
    return [
        pltpu.VMEM((columns * 12, 8, 128), F32),
        pltpu.VMEM((36, 8, 128), F32),
        pltpu.SMEM((64,), jnp.int32),
    ]


def along_y(value, step):
    count = lax.axis_size("gy")
    pairs = [(i, i + step) for i in range(count) if 0 <= i + step < count]
    return lax.ppermute(value, "gy", pairs)


def along_x(value, step):
    count = lax.axis_size("gx")
    return lax.ppermute(value, "gx", [(i, (i + step) % count) for i in range(count)])


def body(
    sph_pos,
    sph_vel,
    sph_mass,
    cell_count,
    grain_pos,
    grain_vel,
    grain_radius,
    contact_pairs,
    contact_count,
    iface_grain,
    iface_offset,
    pair_count,
    iface_cell,
):
    place = jnp.stack(
        [lax.axis_index("gx"), lax.axis_index("gy"), lax.axis_index("gz")]
    ).astype(jnp.int32)
    radius = grain_radius.reshape(8, 128)
    route_grain = iface_grain.reshape(16, 128)
    bricks = (
        sph_pos.reshape(96, 128),
        sph_vel.reshape(96, 128),
        sph_mass.reshape(32, 128),
        cell_count.reshape(4, 128),
        grain_pos.reshape(24, 128),
        grain_vel.reshape(24, 128),
        radius,
    )
    send = call(
        pack_kernel,
        shape(192, 128),
        ins=[S] + [pl.BlockSpec(memory_space=pltpu.HBM)] * 9,
        scratch=[pltpu.VMEM((rows, 128), F32) for rows in (96, 96, 32)]
        + [pltpu.VMEM((4, 128), jnp.int32)]
        + [pltpu.VMEM((rows, 128), F32) for rows in (24, 24, 8)]
        + [pltpu.VMEM((16, 128), jnp.int32), pltpu.VMEM((48, 128), F32)]
        + [pltpu.SemaphoreType.DMA((9,))],
        cost=cost(3),
        limit=None,
    )(pair_count.reshape(16), *bricks, route_grain, iface_offset.reshape(48, 128))
    later = lax.optimization_barrier((send,) + bricks)
    send, bricks = later[0], later[1:]
    own = call(gather_kernel, shape(Y_TILES, 8, 128), ins=[V] * 7, cost=cost(1))(*bricks)
    arrived = lax.all_to_all(
        send.reshape(16, 3, 4, 128), "gz", split_axis=0, concat_axis=0, tiled=True
    ).reshape(48, 4, 128)
    own = call(
        rim_kernel,
        shape(Y_TILES, 8, 128),
        ins=[S, V, pl.BlockSpec(memory_space=pl.ANY)],
        alias={2: 0},
        grid=(2,),
        out_specs=[pl.BlockSpec((1, 8, 128), lambda i: (Y_RIM + i, 0, 0))],
        cost=cost(1),
    )(place, arrived, own)
    ahead = along_y(own, 1)
    behind = along_y(own, -1)
    own_total = call(
        own_density_kernel,
        shape(9, 8, 128),
        ins=[V],
        scratch=density_scratch(4),
        cost=cost(3),
    )(own)
    ahead, behind, own_total = lax.optimization_barrier((ahead, behind, own_total))
    up, down = call(
        widen_kernel,
        [shape(X_TILES, 8, 128)] * 2,
        ins=[V] * 3,
        cost=cost(1),
    )(own, ahead, behind)
    left = along_x(up, 1)
    right = along_x(down, -1)
    mid_total, rim_center = call(
        mid_density_kernel,
        [shape(9, 8, 128), shape(4, 8, 128)],
        ins=[V] * 4,
        scratch=density_scratch(18),
        cost=cost(6),
    )(own, ahead, behind, own_total)
    own_fields = call(
        far_own_kernel,
        shape(12, 8, 128),
        ins=[S] + [V] * 6,
        scratch=density_scratch(8) + [pltpu.VMEM((9, 8, 128), F32)],
        cost=cost(2),
    )(place, own, ahead, behind, left, right, mid_total)
    send_back, reaction = call(
        pair_kernel,
        [shape(16, 4, 128), shape(12, 8, 128)],
        ins=[V] * 4,
        scratch=[pltpu.VMEM((192, 2048), BF16), pltpu.VMEM((128, 2048), BF16)],
        cost=cost(3),
    )(own, own_fields, arrived, iface_cell.reshape(16, 128))
    fields = call(
        far_rest_kernel,
        shape(18, 8, 128),
        ins=[S] + [V] * 8,
        scratch=density_scratch(15) + [pltpu.VMEM((9, 8, 128), F32)],
        cost=cost(3),
    )(place, own, ahead, behind, left, right, mid_total, rim_center, own_fields)
    fields_left = along_x(fields, 1)
    fields_right = along_x(fields, -1)
    back = lax.all_to_all(send_back, "gz", split_axis=0, concat_axis=0, tiled=True)
    contact = call(
        contact_kernel,
        shape(9, 8, 128),
        ins=[S, S] + [V] * 6,
        scratch=[
            pltpu.VMEM((128, 128), F32),
            pltpu.VMEM((2, 128, 128), F32),
            pltpu.VMEM((6, 144, 128), F32),
            pltpu.VMEM((144, 6144), BF16),
            pltpu.VMEM((128, 6144), BF16),
        ],
        cost=cost(6),
    )(
        place,
        contact_count.reshape(1),
        own,
        ahead,
        behind,
        left,
        right,
        contact_pairs.reshape(96, 128),
    )
    accel = call(
        force_kernel,
        shape(96, 128),
        ins=[S] + [V] * 9,
        scratch=[pltpu.VMEM((16 * 27, 8, 128), F32)],
        cost=cost(6),
    )(place, own, ahead, behind, left, right, fields, fields_left, fields_right, reaction)
    grain_force, grain_stress = call(
        grain_kernel,
        [shape(24, 128), shape(48, 128)],
        ins=[V] * 4,
        scratch=[pltpu.VMEM((48, 2048), BF16), pltpu.VMEM((128, 2048), BF16)],
        cost=cost(2),
    )(back, route_grain, contact, radius)
    return (
        accel.reshape(sph_pos.shape),
        grain_force.reshape(grain_pos.shape),
        grain_stress.reshape((6,) + grain_radius.shape),
    )


def solution(mesh):
    return jax.shard_map(
        body,
        mesh=mesh,
        in_specs=(
            P(None, None, "gx", "gy", "gz"),
            P(None, None, "gx", "gy", "gz"),
            P(None, "gx", "gy", "gz"),
            P("gx", "gy", "gz"),
            P(None, None, "gx", "gy", "gz"),
            P(None, None, "gx", "gy", "gz"),
            P(None, "gx", "gy", "gz"),
            P(None, "gx", "gy", "gz"),
            P("gx", "gy", "gz"),
            P("gx", "gy", "gz", None),
            P(None, "gx", "gy", "gz", None),
            P("gx", "gy", "gz"),
            P("gx", "gy", "gz", None),
        ),
        out_specs=(
            P(None, None, "gx", "gy", "gz"),
            P(None, None, "gx", "gy", "gz"),
            P(None, None, "gx", "gy", "gz"),
        ),
        check_vma=False,
    )
```

```python
import math

import jax
import jax.numpy as jnp
from jax import lax
from jax.experimental import pallas as pl
from jax.experimental.pallas import tpu as pltpu
from jax.sharding import PartitionSpec as P

NORMING = 21.0 / (2.0 * math.pi)
REST_DENSITY = 6.0
GRAVITY = 1.0
DRAG_RATE = 2.0
SPRING = 20.0
SOFT_WIDTH = 0.2
DAMPING = 0.5
SOFTENING = 0.01
GRAIN_WEIGHT = 2.0
VOLUME_FACTOR = 4.0 * math.pi / 3.0
TINY = 1e-30

F32 = jnp.float32
BF16 = jnp.bfloat16
VM = pltpu.VMEM
SM = pltpu.SMEM

Y_GRAIN = 28
Y_RIM = 35
Y_TILES = 37
X_VEL = 24
X_GRAIN = 36
X_RIM = 43
X_TILES = 49
GRAIN_LANE = 56


def call(kernel, outs, scratch=(), ins=(), cost=None, alias=None, grid=None, out_specs=None, limit=24):
    single = not isinstance(outs, (list, tuple))
    count = 1 if single else len(outs)
    if out_specs is None:
        out_specs = [pl.BlockSpec(memory_space=VM)] * count
    extra = {}
    if grid is not None:
        extra["grid"] = grid
    if limit is not None:
        extra["compiler_params"] = pltpu.CompilerParams(vmem_limit_bytes=limit * 1024 * 1024)
    return pl.pallas_call(
        kernel,
        out_shape=outs,
        in_specs=list(ins),
        out_specs=out_specs[0] if single else out_specs,
        scratch_shapes=list(scratch),
        input_output_aliases=alias or {},
        cost_estimate=cost,
        **extra,
    )


def cost(micros):
    return pl.CostEstimate(flops=int(micros * 4e6), bytes_accessed=int(micros * 2e6), transcendentals=0)


V = pl.BlockSpec(memory_space=VM)
S = pl.BlockSpec(memory_space=SM)


def shape(*dims):
    return jax.ShapeDtypeStruct(dims, F32)


def lanes():
    return lax.broadcasted_iota(jnp.int32, (8, 128), 1)


def subs():
    return lax.broadcasted_iota(jnp.int32, (8, 128), 0)


def roll(value, amount):
    amount = amount % 128
    return value if amount == 0 else pltpu.roll(value, amount, 1)


def spread(row):
    return jnp.broadcast_to(row, (8, 128))


def lane_gather(table, index):
    numbers = lax.GatherDimensionNumbers(
        offset_dims=(),
        collapsed_slice_dims=(1,),
        start_index_map=(1,),
        operand_batching_dims=(0,),
        start_indices_batching_dims=(0,),
    )
    return lax.gather(
        table,
        index[..., None],
        numbers,
        slice_sizes=(1, 1),
        mode=lax.GatherScatterMode.PROMISE_IN_BOUNDS,
    )


def rim_lane(field, layer, col):
    return (field * 2 + layer) * 4 + col


def split_rows(value):
    high = value.astype(BF16).astype(F32)
    return jnp.concatenate([high, value - high], axis=0)


def scatter_dot(left, hot):
    return lax.dot_general(
        left, hot, (((1,), (1,)), ((), ())), preferred_element_type=F32
    )


def hot_rows(row):
    ids = lax.broadcasted_iota(jnp.int32, (128, 128), 0)
    return jnp.where(ids == jnp.broadcast_to(row, (128, 128)), 1.0, 0.0).astype(BF16)


def water_tile(pos, vel, mass, count, col, field):
    if field < 3:
        return pos[pl.ds(field * 32 + col, 8, stride=4), :]
    if field > 3:
        return vel[pl.ds((field - 4) * 32 + col, 8, stride=4), :]
    value = mass[pl.ds(col, 8, stride=4), :]
    return jnp.where(subs() < spread(count[pl.ds(col, 1), :]), value, 0.0)


def grain_tile(gpos, gvel, grad, field):
    if field < 3:
        return gpos[pl.ds(field * 8, 8), :]
    if field < 6:
        return gvel[pl.ds((field - 3) * 8, 8), :]
    return grad[...]


def gather_kernel(pos, vel, mass, count, gpos, gvel, grad, own):
    for col in range(4):
        for field in range(7):
            own[col * 7 + field] = water_tile(pos, vel, mass, count, col, field)
    for field in range(7):
        own[Y_GRAIN + field] = grain_tile(gpos, gvel, grad, field)
    for side in range(2):
        own[Y_RIM + side] = jnp.zeros((8, 128), F32)


def pack_kernel(counts, *refs):
    sources, send, buffers, sems = refs[:9], refs[9], refs[10:19], refs[19]
    layer_here = lax.axis_index("gz")
    copies = [
        pltpu.make_async_copy(source, buffer, sems.at[k])
        for k, (source, buffer) in enumerate(zip(sources, buffers))
    ]
    for one in copies:
        one.start()
    for one in copies:
        one.wait()
    pos, vel, mass, count, gpos, gvel, grad, grain, offset = buffers
    lane = lanes()
    sub = subs()
    low = jnp.zeros((8, 128), F32)
    high = jnp.zeros((8, 128), F32)
    for col in range(4):
        for field in range(7):
            value = water_tile(pos, vel, mass, count, col, field)
            for layer in range(2):
                at = rim_lane(field, layer, col)
                low = jnp.where(lane == at, roll(value, at - layer), low)
                high = jnp.where(lane == at, roll(value, at - 126 - layer), high)
    for field in range(7):
        value = grain_tile(gpos, gvel, grad, field)
        at = GRAIN_LANE + field
        low = jnp.where(lane == at, roll(value, at), low)
        high = jnp.where(lane == at, roll(value, at - 127), high)
    radius = grad[...]
    volume = VOLUME_FACTOR * radius * radius * radius
    tables = [gvel[pl.ds(field * 8, 8), :] for field in range(3)] + [volume]
    for group in range(2):
        index = grain[pl.ds(group * 8, 8), :]
        row = index >> 7
        at = index & 127
        found = [jnp.zeros((8, 128), F32) for _ in range(4)]
        for place_row in range(8):
            here = row == place_row
            for field in range(4):
                got = lane_gather(spread(tables[field][place_row : place_row + 1]), at)
                found[field] = jnp.where(here, got, found[field])
        alive = jnp.zeros((8, 128), jnp.int32)
        for peer in range(8):
            alive = jnp.where(sub == peer, counts[group * 8 + peer], alive)
        found[3] = jnp.where(lane < alive, found[3], 0.0)
        for field in range(3):
            send[pl.ds(group * 96 + field, 8, stride=12), :] = offset[
                pl.ds(field * 16 + group * 8, 8), :
            ]
        for field in range(4):
            send[pl.ds(group * 96 + 3 + field, 8, stride=12), :] = found[field]
        send[pl.ds(group * 96 + 7, 8, stride=12), :] = jnp.zeros((8, 128), F32)
    low, high = [
        jnp.where(lane < 64, one, pltpu.roll(roll(one, 64), 4, 0))[0:4] for one in (low, high)
    ]
    for peer in range(16):
        send[pl.ds(peer * 12 + 8, 4), :] = jnp.where(peer < layer_here, low, high)


def rim_kernel(place, arrived, own_in, own):
    step = pl.program_id(0)
    layer = place[2]
    other = jnp.where(step == 0, layer - 1, layer + 1)
    inside = jnp.logical_and(other >= 0, other <= 15)
    rows = jnp.where(inside, arrived[jnp.clip(other, 0, 15) * 3 + 2], 0.0)
    own[0] = jnp.concatenate([rows, pltpu.roll(rows, 64, 1)], axis=0)


def widen_kernel(own, ahead, behind, up, down):
    for send, a in ((up, 1), (down, 0)):
        for y in range(6):
            source = (ahead, own, behind)[y // 2]
            col = a * 2 + y % 2
            for field in range(4):
                send[y * 4 + field] = source[col * 7 + field]
        for y in range(4):
            source = (ahead, own, own, behind)[y]
            col = a * 2 + (1, 0, 1, 0)[y]
            for field in range(3):
                send[X_VEL + y * 3 + field] = source[col * 7 + 4 + field]
            for field in range(7):
                for slot in range(2):
                    send[X_GRAIN + field, pl.ds(slot * 4 + y, 1), :] = source[
                        Y_GRAIN + field, pl.ds(slot * 4 + col, 1), :
                    ]
        for part, source in enumerate((own, ahead, behind)):
            for side in range(2):
                send[X_RIM + part * 2 + side] = source[Y_RIM + side]


class Near:
    def __init__(self, own, ahead, behind, left, right):
        self.own, self.ahead, self.behind = own, ahead, behind
        self.left, self.right = left, right

    def main(self, field, x, y):
        if x in (1, 2):
            source = (self.ahead, self.own, self.behind)[y // 2]
            return source[((x - 1) * 2 + y % 2) * 7 + field]
        source = self.left if x == 0 else self.right
        if field < 4:
            return source[y * 4 + field]
        return source[X_VEL + (y - 1) * 3 + field - 4]

    def rim(self, side, x, y):
        part = (1, 0, 2)[y // 2]
        if x in (1, 2):
            return (self.own, self.ahead, self.behind)[part][Y_RIM + side]
        source = self.left if x == 0 else self.right
        return source[X_RIM + part * 2 + side]

    def rim_col(self, x, y):
        return (1, 0, 1, 0)[x] * 2 + y % 2


class Columns:
    def __init__(self, data, near, has_left=None, has_right=None):
        self.data, self.near = data, near
        self.there = {0: has_left, 3: has_right}
        self.lane = lanes()
        self.packed = None

    def open_rim(self):
        self.packed = [[jnp.zeros((8, 128), F32) for _ in range(4)] for _ in range(3)]

    def put(self, at, x, y, rim):
        data, lane, packed = self.data, self.lane, self.packed
        col = data.rim_col(x, y)
        rims = [data.rim(side, x, y) for side in range(2)]
        for field in range(4):
            value = data.main(field, x, y)
            edge = [rims[0], rims[1]]
            if field == 3 and x in (0, 3):
                value = jnp.where(self.there[x], value, 0.0)
                edge = [jnp.where(self.there[x], one, 0.0) for one in edge]
            shift = float(x - 1) if field == 0 else float(y - 2) if field == 1 else 0.0
            if shift:
                value = value + shift
                edge = [one + shift for one in edge]
            back = jnp.where(
                lane == 0, roll(edge[0], -rim_lane(field, 1, col)), roll(value, 1)
            )
            fore = jnp.where(
                lane == 127, roll(edge[1], 127 - rim_lane(field, 0, col)), roll(value, 127)
            )
            if field == 2:
                back = back - 1.0
                fore = fore + 1.0
            self.near[at * 12 + field] = back
            self.near[at * 12 + 4 + field] = value
            self.near[at * 12 + 8 + field] = fore
            if not rim:
                continue
            for side in range(2):
                spot = side * 64 + x * 8 + y
                here = lane == spot
                outer = rim_lane(field, 0 if side == 0 else 1, col)
                inner = rim_lane(field, 1 if side == 0 else 0, col)
                packed[0][field] = jnp.where(here, roll(edge[side], spot - outer), packed[0][field])
                packed[1][field] = jnp.where(here, roll(edge[side], spot - inner), packed[1][field])
                packed[2][field] = jnp.where(
                    here, roll(value, spot - (0 if side == 0 else 127)), packed[2][field]
                )

    def close_rim(self):
        sign = jnp.where(self.lane < 64, -1.0, 1.0)
        self.packed[0][2] = self.packed[0][2] + sign
        self.packed[2][2] = self.packed[2][2] - sign

    def put_rim(self, at, moved):
        for level in range(3):
            for field in range(4):
                self.near[at * 12 + level * 4 + field] = moved(self.packed[level][field])


def place_of(data, x, y):
    value = [data.main(field, x, y) for field in range(4)]
    if x != 1:
        value[0] = value[0] + float(x - 1)
    if y != 2:
        value[1] = value[1] + float(y - 2)
    return value


def add_columns(near, table, start, targets, width, center_ref, total_ref):
    def one_column(number, carry):
        target = table[start + number * (width + 1)]
        center = [center_ref[target * 4 + field] for field in range(3)]

        def one_neighbour(step, total):
            base = table[start + number * (width + 1) + 1 + step] * 12
            for level in range(3):
                for slot in range(8):
                    row = [
                        spread(near[base + level * 4 + field, pl.ds(slot, 1), :])
                        for field in range(4)
                    ]
                    dx = center[0] - row[0]
                    dy = center[1] - row[1]
                    dz = center[2] - row[2]
                    square = jnp.maximum(dx * dx + dy * dy + dz * dz, TINY)
                    radius = square * lax.rsqrt(square)
                    reach = jnp.maximum(1.0 - radius, 0.0)
                    squared = reach * reach
                    total = total + (squared * squared) * ((1.25 - reach) * row[3])
            return total

        total_ref[target] = lax.fori_loop(
            0, width, one_neighbour, total_ref[target], unroll=True
        )
        return carry

    lax.fori_loop(0, targets, one_column, 0)


def fill(table, start, rows):
    at = start
    for row in rows:
        for value in row:
            table[at] = value
            at += 1
    return at


def own_density_kernel(own, total, near, center, table):
    data = Near(own, own, own, own, own)
    cols = Columns(data, near)
    rows = []
    for x in range(2):
        for y in range(2):
            cols.put(x * 2 + y, x + 1, y + 2, False)
            target = x * 4 + y + 1
            rows.append([target, 0, 1, 2, 3])
            for field, value in enumerate(place_of(data, x + 1, y + 2)):
                center[target * 4 + field] = value
    fill(table, 0, rows)
    total[...] = jnp.zeros((9, 8, 128), F32)
    add_columns(near, table, 0, 4, 4, center, total)


def mid_density_kernel(own, ahead, behind, start, total, rim_center, near, center, table):
    data = Near(own, ahead, behind, own, own)
    cols = Columns(data, near)
    cols.open_rim()
    for x in range(2):
        for y in range(6):
            cols.put(x * 6 + y, x + 1, y, True)
    cols.close_rim()
    lane = lanes()
    in_first = (lane & 63) < 16
    for step in range(3):
        cols.put_rim(12 + step, lambda v: roll(v, 1 - step))
        cols.put_rim(
            15 + step,
            lambda v: jnp.where(in_first, roll(v, 1 - step - 8), roll(v, 1 - step + 8)),
        )
    for field in range(4):
        center[8 * 4 + field] = cols.packed[1][field]
        rim_center[field] = cols.packed[1][field]
    outer, inner = [], []
    for x in range(2):
        for y in range(4):
            target = x * 4 + y
            for field, value in enumerate(place_of(data, x + 1, y + 1)):
                center[target * 4 + field] = value
            if y in (0, 3):
                outer.append([target] + [sx * 6 + y + dy for sx in range(2) for dy in range(3)])
            else:
                far = 1 if y == 1 else 4
                inner.append([target] + [sx * 6 + far for sx in range(2)])
    outer.append([8] + [12 + k for k in range(6)])
    total[...] = start[...]
    at = fill(table, 0, outer)
    fill(table, at, inner)
    add_columns(near, table, 0, 5, 6, center, total)
    add_columns(near, table, at, 4, 2, center, total)


def far_own_kernel(place, own, ahead, behind, left, right, start, out, near, center, table, total):
    data = Near(own, ahead, behind, left, right)
    cols = Columns(data, near, place[0] > 0, place[0] < 7)
    for x in range(2):
        for y in range(4):
            cols.put(x * 4 + y, x * 3, y + 1, False)
    rows = []
    for x in range(2):
        for y in (1, 2):
            target = x * 4 + y
            for field, value in enumerate(place_of(data, x + 1, y + 1)):
                center[target * 4 + field] = value
            rows.append([target] + [x * 4 + y - 1 + dy for dy in range(3)])
            total[target] = start[target]
    fill(table, 0, rows)
    add_columns(near, table, 0, 4, 3, center, total)
    for x in range(2):
        for y in (1, 2):
            press, inverse, pressure = finish(total[x * 4 + y], center[(x * 4 + y) * 4 + 3])
            at = (x * 2 + y - 1) * 3
            out[at] = press
            out[at + 1] = inverse
            out[at + 2] = pressure


def far_rest_kernel(
    place, own, ahead, behind, left, right, start, rim_center, own_fields, out, near, center, table, total
):
    data = Near(own, ahead, behind, left, right)
    cols = Columns(data, near, place[0] > 0, place[0] < 7)
    cols.open_rim()
    for x in range(2):
        for y in range(6):
            cols.put(x * 6 + y, x * 3, y, True)
    cols.close_rim()
    in_first = (lanes() & 63) < 16
    for step in range(3):
        cols.put_rim(
            12 + step,
            lambda v: jnp.where(in_first, roll(v, 1 - step + 8), roll(v, 1 - step - 8)),
        )
    rows = []
    for x in range(2):
        for y in (0, 3):
            target = x * 4 + y
            for field, value in enumerate(place_of(data, x + 1, y + 1)):
                center[target * 4 + field] = value
            rows.append([target] + [x * 6 + y + dy for dy in range(3)])
            total[target] = start[target]
    for field in range(4):
        center[8 * 4 + field] = rim_center[field]
    total[8] = start[8]
    rows.append([8, 12, 13, 14])
    fill(table, 0, rows)
    add_columns(near, table, 0, 5, 3, center, total)
    for target in (0, 3, 4, 7, 8):
        press, inverse, _ = finish(total[target], center[target * 4 + 3])
        out[target * 2] = press
        out[target * 2 + 1] = inverse
    for x in range(2):
        for y in range(2):
            for k in range(2):
                out[(x * 4 + y + 1) * 2 + k] = own_fields[(x * 2 + y) * 3 + k]


def finish(total, mass):
    density = (4.0 * NORMING) * total
    alive = mass > 0.0
    live = jnp.where(alive, 1.0, 0.0)
    safe = jnp.where(alive, density, 1.0)
    pressure = (density - REST_DENSITY) * live
    return pressure / (safe * safe), live / safe, pressure


def force_kernel(place, own, ahead, behind, left, right, fields, fleft, fright, reaction, out, near):
    lane = lanes()
    first = lane == 0
    last = lane == 127
    data = Near(own, ahead, behind, left, right)
    has_left = place[0] > 0
    has_right = place[0] < 7
    for x in range(4):
        for y in range(1, 5):
            col = data.rim_col(x, y)
            rims = [data.rim(side, x, y) for side in range(2)]
            source = fields if x in (1, 2) else fleft if x == 0 else fright
            far_x = (1, 0, 1, 0)[x]
            target = far_x * 4 + y - 1
            extra = []
            for which in range(2):
                value = source[target * 2 + which]
                halo = source[16 + which]
                extra.append((value, halo))
            levels = [[], [], []]
            for field in range(7):
                value = data.main(field, x, y)
                edge = [rims[0], rims[1]]
                if field == 3 and x in (0, 3):
                    there = has_left if x == 0 else has_right
                    value = jnp.where(there, value, 0.0)
                    edge = [jnp.where(there, one, 0.0) for one in edge]
                back = jnp.where(first, roll(edge[0], -rim_lane(field, 1, col)), roll(value, 1))
                fore = jnp.where(last, roll(edge[1], 127 - rim_lane(field, 0, col)), roll(value, 127))
                shift = float(x - 1) if field == 0 else float(y - 2) if field == 1 else 0.0
                if shift:
                    value, back, fore = value + shift, back + shift, fore + shift
                if field == 2:
                    back = back - 1.0
                    fore = fore + 1.0
                for level, one in enumerate((back, value, fore)):
                    levels[level].append(one)
            spot = (far_x + 1) * 8 + y
            for value, halo in extra:
                back = jnp.where(first, roll(halo, -spot), roll(value, 1))
                fore = jnp.where(last, roll(halo, 127 - 64 - spot), roll(value, 127))
                for level, one in enumerate((back, value, fore)):
                    levels[level].append(one)
            for level in range(3):
                px, py, pz, m, vx, vy, vz, press, inverse = levels[level]
                at = ((x * 4 + y - 1) * 3 + level) * 9
                for k, one in enumerate((px, py, pz, m, m * press, m * inverse, vx, vy, vz)):
                    near[at + k] = one

    def one_column(target, carry):
        a = target // 2
        b = target % 2
        middle = (((a + 1) * 4 + b + 1) * 3 + 1) * 9
        center = [near[middle + k] for k in range(3)]
        press = fields[(a * 4 + b + 1) * 2]
        inverse = fields[(a * 4 + b + 1) * 2 + 1]

        def one_neighbour(step, total):
            base = (((a + step // 3) * 4 + b + step % 3) * 3) * 9
            total = list(total)
            for level in range(3):
                for slot in range(8):
                    row = [
                        spread(near[base + level * 9 + k, pl.ds(slot, 1), :]) for k in range(9)
                    ]
                    dx = center[0] - row[0]
                    dy = center[1] - row[1]
                    dz = center[2] - row[2]
                    square = dx * dx + dy * dy + dz * dz
                    guarded = jnp.maximum(square, TINY)
                    radius = guarded * lax.rsqrt(guarded)
                    reach = jnp.maximum(1.0 - radius, 0.0)
                    cubed = reach * reach * reach
                    push = cubed * (row[3] * press + row[4])
                    soft = pltpu.reciprocal(square + SOFTENING, approx=True)
                    drag = (cubed * row[5]) * (square * soft)
                    total[0] = total[0] + push * dx
                    total[1] = total[1] + push * dy
                    total[2] = total[2] + push * dz
                    total[3] = total[3] + drag
                    total[4] = total[4] + drag * row[6]
                    total[5] = total[5] + drag * row[7]
                    total[6] = total[6] + drag * row[8]
            return tuple(total)

        zero = jnp.zeros((8, 128), F32)
        total = lax.fori_loop(0, 9, one_neighbour, (zero,) * 7, unroll=3)
        live = jnp.where(near[middle + 3] > 0.0, 1.0, 0.0)
        for d in range(3):
            slow = inverse * (near[middle + 6 + d] * total[3] - total[4 + d])
            force = 20.0 * NORMING * (total[d] - slow)
            if d == 2:
                force = force - GRAVITY
            out[pl.ds(d * 32 + target, 8, stride=4), :] = live * force + reaction[d * 4 + target]
        return carry

    lax.fori_loop(0, 4, one_column, 0)


def pair_kernel(own, fields, arrived, cells, send, reaction, left, hot):
    for peer in range(16):
        index = cells[pl.ds(peer, 1), :]
        at_row = index & 127
        at = spread(at_row)
        col_of = spread(index >> 7)
        found = None
        for col in range(4):
            mid = col * 3
            inverse = fields[mid + 1]
            tables = [own[col * 7 + k] for k in (0, 1, 2, 4, 5, 6)]
            tables += [own[col * 7 + 3] * inverse, fields[mid + 2], inverse]
            got = [lane_gather(one, at) for one in tables]
            if found is None:
                found = got
            else:
                here = col_of == col
                found = [jnp.where(here, new, old) for new, old in zip(got, found)]
        row = [spread(arrived[peer * 3 + k // 4, pl.ds(k % 4, 1), :]) for k in range(7)]
        delta = [row[d] - found[d] for d in range(3)]
        square = jnp.maximum(delta[0] * delta[0] + delta[1] * delta[1] + delta[2] * delta[2], TINY)
        radius = square * lax.rsqrt(square)
        reach = jnp.maximum(1.0 - radius, 0.0)
        cubed = reach * reach * reach
        weight = (DRAG_RATE * NORMING) * cubed * reach * (4.0 * radius + 1.0)
        push = (20.0 * NORMING) * found[7] * cubed
        hot[:, peer * 128 : peer * 128 + 128] = hot_rows(at_row)
        for d in range(3):
            bracket = row[6] * (push * delta[d] + weight * (found[3 + d] - row[3 + d]))
            send[peer, pl.ds(d, 1), :] = jnp.sum(found[6] * bracket, axis=0, keepdims=True)
            both = split_rows(-found[8] * bracket)
            col_both = jnp.concatenate([col_of, col_of], axis=0)
            for col in range(4):
                at16 = (d * 4 + col) * 16
                left[at16 : at16 + 16, peer * 128 : peer * 128 + 128] = jnp.where(
                    col_both == col, both, 0.0
                ).astype(BF16)
        send[peer, pl.ds(3, 1), :] = jnp.zeros((1, 128), F32)
    sums = scatter_dot(left[...], hot[...])
    for k in range(12):
        reaction[k] = sums[k * 16 : k * 16 + 8] + sums[k * 16 + 8 : k * 16 + 16]


def contact_kernel(place, live_count, own, ahead, behind, left, right, listed, out, rims, turned, rows, lhs, hot):
    lane = lanes()
    sub = subs()
    has_left = place[0] > 0
    has_right = place[0] < 7
    def far_line(field, row):
        slot, x, y = row // 16, row // 4 % 4, row % 4
        if x in (1, 2):
            source = (ahead, own, own, behind)[y]
            at = slot * 4 + (x - 1) * 2 + (1, 0, 1, 0)[y]
            return source[Y_GRAIN + field, pl.ds(at, 1), :]
        source = left if x == 0 else right
        return source[X_GRAIN + field, pl.ds(slot * 4 + y, 1), :]

    for side in range(2):
        rims[...] = jnp.zeros((128, 128), F32)
        for part, source in enumerate((own, ahead, behind)):
            rims[pl.ds(part * 8, 8), :] = source[Y_RIM + side]
            rims[pl.ds((3 + part) * 8, 8), :] = jnp.where(
                has_left, left[X_RIM + part * 2 + side], 0.0
            )
            rims[pl.ds((6 + part) * 8, 8), :] = jnp.where(
                has_right, right[X_RIM + part * 2 + side], 0.0
            )
        turned[side] = jnp.transpose(rims[...])

    def one_group(group):
        start = group * 8
        one = listed[pl.ds(start, 8), :]
        two = listed[pl.ds(start + 48, 8), :]
        own_row = one >> 7
        own_c = one & 127
        far_row = (two * 4033) >> 19
        far_c = two - far_row * 130
        far_slot = far_row >> 4
        far_x = (far_row >> 2) & 3
        far_y = far_row & 3
        far_at = jnp.clip(far_c - 1, 0, 127)
        x_part = jnp.where(far_x == 0, 1, jnp.where(far_x == 3, 2, 0))
        y_part = jnp.where(far_y == 0, 1, jnp.where(far_y == 3, 2, 0))
        rim_a = jnp.where(far_x == 0, 1, jnp.where(far_x == 3, 0, far_x - 1))
        rim_b = jnp.where(far_y == 0, 1, jnp.where(far_y == 3, 0, far_y - 1))
        rim_at = (x_part * 3 + y_part) * 8 + far_slot * 4 + rim_a * 2 + rim_b
        own_found = [jnp.zeros((8, 128), F32) for _ in range(7)]
        for row in range(8):
            here = own_row == row
            for field in range(7):
                got = lane_gather(spread(own[Y_GRAIN + field, pl.ds(row, 1), :]), own_c)
                own_found[field] = jnp.where(here, got, own_found[field])
        far_found = [jnp.zeros((8, 128), F32) for _ in range(7)]
        for row in range(32):
            here = far_row == row
            if row // 4 % 4 in (0, 3):
                here = jnp.logical_and(here, has_left if row // 4 % 4 == 0 else has_right)
            for field in range(7):
                got = lane_gather(spread(far_line(field, row)), far_at)
                far_found[field] = jnp.where(here, got, far_found[field])
        for side, edge in ((0, 0), (1, 129)):
            here = far_c == edge
            for field in range(7):
                got = lane_gather(
                    spread(turned[side, pl.ds(GRAIN_LANE + field, 1), :]), rim_at
                )
                far_found[field] = jnp.where(here, got, far_found[field])
        shift = [
            (((own_row >> 1) & 1) - far_x + 1).astype(F32),
            ((own_row & 1) - far_y + 1).astype(F32),
            (own_c - far_c + 1).astype(F32),
        ]
        delta = [own_found[d] - far_found[d] + shift[d] for d in range(3)]
        distance = jnp.sqrt(
            delta[0] * delta[0] + delta[1] * delta[1] + delta[2] * delta[2] + SOFTENING
        )
        normal = [one_delta / distance for one_delta in delta]
        both = own_found[6] + far_found[6]
        overlap = (both - distance) / SOFT_WIDTH
        stiff = SPRING * own_found[6] * far_found[6] / both
        closing = sum((own_found[3 + d] - far_found[3 + d]) * normal[d] for d in range(3))
        soft = jnp.maximum(overlap, 0.0) + jnp.log1p(jnp.exp(-jnp.abs(overlap)))
        number = group * 1024 + sub * 128 + lane
        magnitude = jnp.where(
            number < live_count[0], stiff * (SOFT_WIDTH * soft - DAMPING * closing), 0.0
        )
        force = [magnitude * normal[d] for d in range(3)]
        values = force + [
            force[0] * normal[0],
            force[1] * normal[1],
            force[2] * normal[2],
            force[0] * normal[1],
            force[0] * normal[2],
            force[1] * normal[2],
        ]
        for k in range(9):
            high = values[k].astype(BF16).astype(F32)
            rows[group, pl.ds(k * 16, 8), :] = high
            rows[group, pl.ds(k * 16 + 8, 8), :] = values[k] - high
        for s in range(8):
            at = pl.ds((group * 8 + s) * 128, 128)
            mine = spread(own_row[s : s + 1]) == sub
            hot[:, at] = hot_rows(own_c[s : s + 1])
            for k in range(9):
                high = spread(rows[group, pl.ds(k * 16 + s, 1), :])
                low = spread(rows[group, pl.ds(k * 16 + 8 + s, 1), :])
                pair = jnp.concatenate(
                    [jnp.where(mine, high, 0.0), jnp.where(mine, low, 0.0)], axis=0
                )
                lhs[k * 16 : k * 16 + 16, at] = pair.astype(BF16)

    for group in range(6):
        one_group(group)
    sums = scatter_dot(lhs[...], hot[...])
    for k in range(9):
        out[k] = sums[k * 16 : k * 16 + 8] + sums[k * 16 + 8 : k * 16 + 16]


def grain_kernel(back, grain, contact, radius_ref, force_out, stress_out, lhs, hot):
    sub = subs()
    for peer in range(16):
        index = grain[pl.ds(peer, 1), :]
        mine = spread(index >> 7) == sub
        hot[:, peer * 128 : peer * 128 + 128] = hot_rows(index & 127)
        for d in range(3):
            value = jnp.where(mine, spread(back[peer, pl.ds(d, 1), :]), 0.0)
            lhs[d * 16 : d * 16 + 16, peer * 128 : peer * 128 + 128] = split_rows(value).astype(BF16)
    sums = scatter_dot(lhs[...], hot[...])
    radius = radius_ref[...]
    volume = VOLUME_FACTOR * radius * radius * radius
    for d in range(3):
        value = contact[d] + (sums[d * 16 : d * 16 + 8] + sums[d * 16 + 8 : d * 16 + 16])
        if d == 2:
            value = value - GRAIN_WEIGHT * volume
        force_out[pl.ds(d * 8, 8), :] = value
    scale = radius / volume
    for k in range(6):
        stress_out[pl.ds(k * 8, 8), :] = -contact[3 + k] * scale


def density_scratch(columns):
    return [
        pltpu.VMEM((columns * 12, 8, 128), F32),
        pltpu.VMEM((36, 8, 128), F32),
        pltpu.SMEM((64,), jnp.int32),
    ]


def along_y(value, step):
    count = lax.axis_size("gy")
    pairs = [(i, i + step) for i in range(count) if 0 <= i + step < count]
    return lax.ppermute(value, "gy", pairs)


def along_x(value, step):
    count = lax.axis_size("gx")
    return lax.ppermute(value, "gx", [(i, (i + step) % count) for i in range(count)])


def body(
    sph_pos,
    sph_vel,
    sph_mass,
    cell_count,
    grain_pos,
    grain_vel,
    grain_radius,
    contact_pairs,
    contact_count,
    iface_grain,
    iface_offset,
    pair_count,
    iface_cell,
):
    place = jnp.stack(
        [lax.axis_index("gx"), lax.axis_index("gy"), lax.axis_index("gz")]
    ).astype(jnp.int32)
    radius = grain_radius.reshape(8, 128)
    route_grain = iface_grain.reshape(16, 128)
    bricks = (
        sph_pos.reshape(96, 128),
        sph_vel.reshape(96, 128),
        sph_mass.reshape(32, 128),
        cell_count.reshape(4, 128),
        grain_pos.reshape(24, 128),
        grain_vel.reshape(24, 128),
        radius,
    )
    send = call(
        pack_kernel,
        shape(192, 128),
        ins=[S] + [pl.BlockSpec(memory_space=pltpu.HBM)] * 9,
        scratch=[pltpu.VMEM((rows, 128), F32) for rows in (96, 96, 32)]
        + [pltpu.VMEM((4, 128), jnp.int32)]
        + [pltpu.VMEM((rows, 128), F32) for rows in (24, 24, 8)]
        + [pltpu.VMEM((16, 128), jnp.int32), pltpu.VMEM((48, 128), F32)]
        + [pltpu.SemaphoreType.DMA((9,))],
        cost=cost(3),
        limit=None,
    )(pair_count.reshape(16), *bricks, route_grain, iface_offset.reshape(48, 128))
    later = lax.optimization_barrier((send,) + bricks)
    send, bricks = later[0], later[1:]
    own = call(gather_kernel, shape(Y_TILES, 8, 128), ins=[V] * 7, cost=cost(1))(*bricks)
    arrived = lax.all_to_all(
        send.reshape(16, 3, 4, 128), "gz", split_axis=0, concat_axis=0, tiled=True
    ).reshape(48, 4, 128)
    own = call(
        rim_kernel,
        shape(Y_TILES, 8, 128),
        ins=[S, V, pl.BlockSpec(memory_space=pl.ANY)],
        alias={2: 0},
        grid=(2,),
        out_specs=[pl.BlockSpec((1, 8, 128), lambda i: (Y_RIM + i, 0, 0))],
        cost=cost(1),
    )(place, arrived, own)
    ahead = along_y(own, 1)
    behind = along_y(own, -1)
    own_total = call(
        own_density_kernel,
        shape(9, 8, 128),
        ins=[V],
        scratch=density_scratch(4),
        cost=cost(3),
    )(own)
    ahead, behind, own_total = lax.optimization_barrier((ahead, behind, own_total))
    up, down = call(
        widen_kernel,
        [shape(X_TILES, 8, 128)] * 2,
        ins=[V] * 3,
        cost=cost(1),
    )(own, ahead, behind)
    left = along_x(up, 1)
    right = along_x(down, -1)
    mid_total, rim_center = call(
        mid_density_kernel,
        [shape(9, 8, 128), shape(4, 8, 128)],
        ins=[V] * 4,
        scratch=density_scratch(18),
        cost=cost(6),
    )(own, ahead, behind, own_total)
    own_fields = call(
        far_own_kernel,
        shape(12, 8, 128),
        ins=[S] + [V] * 6,
        scratch=density_scratch(8) + [pltpu.VMEM((9, 8, 128), F32)],
        cost=cost(2),
    )(place, own, ahead, behind, left, right, mid_total)
    send_back, reaction = call(
        pair_kernel,
        [shape(16, 4, 128), shape(12, 8, 128)],
        ins=[V] * 4,
        scratch=[pltpu.VMEM((192, 2048), BF16), pltpu.VMEM((128, 2048), BF16)],
        cost=cost(3),
    )(own, own_fields, arrived, iface_cell.reshape(16, 128))
    fields = call(
        far_rest_kernel,
        shape(18, 8, 128),
        ins=[S] + [V] * 8,
        scratch=density_scratch(15) + [pltpu.VMEM((9, 8, 128), F32)],
        cost=cost(3),
    )(place, own, ahead, behind, left, right, mid_total, rim_center, own_fields)
    fields_left = along_x(fields, 1)
    fields_right = along_x(fields, -1)
    back = lax.all_to_all(send_back, "gz", split_axis=0, concat_axis=0, tiled=True)
    contact = call(
        contact_kernel,
        shape(9, 8, 128),
        ins=[S, S] + [V] * 6,
        scratch=[
            pltpu.VMEM((128, 128), F32),
            pltpu.VMEM((2, 128, 128), F32),
            pltpu.VMEM((6, 144, 128), F32),
            pltpu.VMEM((144, 6144), BF16),
            pltpu.VMEM((128, 6144), BF16),
        ],
        cost=cost(6),
    )(
        place,
        contact_count.reshape(1),
        own,
        ahead,
        behind,
        left,
        right,
        contact_pairs.reshape(96, 128),
    )
    accel = call(
        force_kernel,
        shape(96, 128),
        ins=[S] + [V] * 9,
        scratch=[pltpu.VMEM((16 * 27, 8, 128), F32)],
        cost=cost(6),
    )(place, own, ahead, behind, left, right, fields, fields_left, fields_right, reaction)
    grain_force, grain_stress = call(
        grain_kernel,
        [shape(24, 128), shape(48, 128)],
        ins=[V] * 4,
        scratch=[pltpu.VMEM((48, 2048), BF16), pltpu.VMEM((128, 2048), BF16)],
        cost=cost(2),
    )(back, route_grain, contact, radius)
    return (
        accel.reshape(sph_pos.shape),
        grain_force.reshape(grain_pos.shape),
        grain_stress.reshape((6,) + grain_radius.shape),
    )


def solution(mesh):
    return jax.shard_map(
        body,
        mesh=mesh,
        in_specs=(
            P(None, None, "gx", "gy", "gz"),
            P(None, None, "gx", "gy", "gz"),
            P(None, "gx", "gy", "gz"),
            P("gx", "gy", "gz"),
            P(None, None, "gx", "gy", "gz"),
            P(None, None, "gx", "gy", "gz"),
            P(None, "gx", "gy", "gz"),
            P(None, "gx", "gy", "gz"),
            P("gx", "gy", "gz"),
            P("gx", "gy", "gz", None),
            P(None, "gx", "gy", "gz", None),
            P("gx", "gy", "gz"),
            P("gx", "gy", "gz", None),
        ),
        out_specs=(
            P(None, None, "gx", "gy", "gz"),
            P(None, None, "gx", "gy", "gz"),
            P(None, None, "gx", "gy", "gz"),
        ),
        check_vma=False,
    )
```

```python
import math

import jax
import jax.numpy as jnp
from jax import lax
from jax.experimental import pallas as pl
from jax.experimental.pallas import tpu as pltpu
from jax.sharding import PartitionSpec as P

NORMING = 21.0 / (2.0 * math.pi)
REST_DENSITY = 6.0
GRAVITY = 1.0
DRAG_RATE = 2.0
SPRING = 20.0
SOFT_WIDTH = 0.2
DAMPING = 0.5
SOFTENING = 0.01
GRAIN_WEIGHT = 2.0
VOLUME_FACTOR = 4.0 * math.pi / 3.0
TINY = 1e-30

F32 = jnp.float32
BF16 = jnp.bfloat16
VM = pltpu.VMEM
SM = pltpu.SMEM

Y_GRAIN = 28
Y_RIM = 35
Y_TILES = 37
X_VEL = 24
X_GRAIN = 36
X_RIM = 43
X_TILES = 49
GRAIN_LANE = 56


def call(kernel, outs, scratch=(), ins=(), cost=None, alias=None, grid=None, out_specs=None, limit=24):
    single = not isinstance(outs, (list, tuple))
    count = 1 if single else len(outs)
    if out_specs is None:
        out_specs = [pl.BlockSpec(memory_space=VM)] * count
    extra = {}
    if grid is not None:
        extra["grid"] = grid
    if limit is not None:
        extra["compiler_params"] = pltpu.CompilerParams(vmem_limit_bytes=limit * 1024 * 1024)
    return pl.pallas_call(
        kernel,
        out_shape=outs,
        in_specs=list(ins),
        out_specs=out_specs[0] if single else out_specs,
        scratch_shapes=list(scratch),
        input_output_aliases=alias or {},
        cost_estimate=cost,
        **extra,
    )


def cost(micros):
    return pl.CostEstimate(flops=int(micros * 4e6), bytes_accessed=int(micros * 2e6), transcendentals=0)


V = pl.BlockSpec(memory_space=VM)
S = pl.BlockSpec(memory_space=SM)


def shape(*dims):
    return jax.ShapeDtypeStruct(dims, F32)


def lanes():
    return lax.broadcasted_iota(jnp.int32, (8, 128), 1)


def subs():
    return lax.broadcasted_iota(jnp.int32, (8, 128), 0)


def roll(value, amount):
    amount = amount % 128
    return value if amount == 0 else pltpu.roll(value, amount, 1)


def spread(row):
    return jnp.broadcast_to(row, (8, 128))


def lane_gather(table, index):
    numbers = lax.GatherDimensionNumbers(
        offset_dims=(),
        collapsed_slice_dims=(1,),
        start_index_map=(1,),
        operand_batching_dims=(0,),
        start_indices_batching_dims=(0,),
    )
    return lax.gather(
        table,
        index[..., None],
        numbers,
        slice_sizes=(1, 1),
        mode=lax.GatherScatterMode.PROMISE_IN_BOUNDS,
    )


def rim_lane(field, layer, col):
    return (field * 2 + layer) * 4 + col


def split_rows(value):
    high = value.astype(BF16).astype(F32)
    return jnp.concatenate([high, value - high], axis=0)


def scatter_dot(left, hot):
    return lax.dot_general(
        left, hot, (((1,), (1,)), ((), ())), preferred_element_type=F32
    )


def hot_rows(row):
    ids = lax.broadcasted_iota(jnp.int32, (128, 128), 0)
    return jnp.where(ids == jnp.broadcast_to(row, (128, 128)), 1.0, 0.0).astype(BF16)


def water_tile(pos, vel, mass, count, col, field):
    if field < 3:
        return pos[pl.ds(field * 32 + col, 8, stride=4), :]
    if field > 3:
        return vel[pl.ds((field - 4) * 32 + col, 8, stride=4), :]
    value = mass[pl.ds(col, 8, stride=4), :]
    return jnp.where(subs() < spread(count[pl.ds(col, 1), :]), value, 0.0)


def grain_tile(gpos, gvel, grad, field):
    if field < 3:
        return gpos[pl.ds(field * 8, 8), :]
    if field < 6:
        return gvel[pl.ds((field - 3) * 8, 8), :]
    return grad[...]


def gather_kernel(pos, vel, mass, count, gpos, gvel, grad, own):
    for col in range(4):
        for field in range(7):
            own[col * 7 + field] = water_tile(pos, vel, mass, count, col, field)
    for field in range(7):
        own[Y_GRAIN + field] = grain_tile(gpos, gvel, grad, field)
    for side in range(2):
        own[Y_RIM + side] = jnp.zeros((8, 128), F32)


def pack_kernel(counts, *refs):
    sources, send, buffers, sems = refs[:9], refs[9], refs[10:19], refs[19]
    layer_here = lax.axis_index("gz")
    copies = [
        pltpu.make_async_copy(source, buffer, sems.at[k])
        for k, (source, buffer) in enumerate(zip(sources, buffers))
    ]
    for one in copies:
        one.start()
    for one in copies:
        one.wait()
    pos, vel, mass, count, gpos, gvel, grad, grain, offset = buffers
    lane = lanes()
    sub = subs()
    low = jnp.zeros((8, 128), F32)
    high = jnp.zeros((8, 128), F32)
    for col in range(4):
        for field in range(7):
            value = water_tile(pos, vel, mass, count, col, field)
            for layer in range(2):
                at = rim_lane(field, layer, col)
                low = jnp.where(lane == at, roll(value, at - layer), low)
                high = jnp.where(lane == at, roll(value, at - 126 - layer), high)
    for field in range(7):
        value = grain_tile(gpos, gvel, grad, field)
        at = GRAIN_LANE + field
        low = jnp.where(lane == at, roll(value, at), low)
        high = jnp.where(lane == at, roll(value, at - 127), high)
    radius = grad[...]
    volume = VOLUME_FACTOR * radius * radius * radius
    tables = [gvel[pl.ds(field * 8, 8), :] for field in range(3)] + [volume]
    for group in range(2):
        index = grain[pl.ds(group * 8, 8), :]
        row = index >> 7
        at = index & 127
        found = [jnp.zeros((8, 128), F32) for _ in range(4)]
        for place_row in range(8):
            here = row == place_row
            for field in range(4):
                got = lane_gather(spread(tables[field][place_row : place_row + 1]), at)
                found[field] = jnp.where(here, got, found[field])
        alive = jnp.zeros((8, 128), jnp.int32)
        for peer in range(8):
            alive = jnp.where(sub == peer, counts[group * 8 + peer], alive)
        found[3] = jnp.where(lane < alive, found[3], 0.0)
        for field in range(3):
            send[pl.ds(group * 96 + field, 8, stride=12), :] = offset[
                pl.ds(field * 16 + group * 8, 8), :
            ]
        for field in range(4):
            send[pl.ds(group * 96 + 3 + field, 8, stride=12), :] = found[field]
        send[pl.ds(group * 96 + 7, 8, stride=12), :] = jnp.zeros((8, 128), F32)
    low, high = [
        jnp.where(lane < 64, one, pltpu.roll(roll(one, 64), 4, 0))[0:4] for one in (low, high)
    ]
    for peer in range(16):
        send[pl.ds(peer * 12 + 8, 4), :] = jnp.where(peer < layer_here, low, high)


def rim_kernel(place, arrived, own_in, own):
    step = pl.program_id(0)
    layer = place[2]
    other = jnp.where(step == 0, layer - 1, layer + 1)
    inside = jnp.logical_and(other >= 0, other <= 15)
    rows = jnp.where(inside, arrived[jnp.clip(other, 0, 15) * 3 + 2], 0.0)
    own[0] = jnp.concatenate([rows, pltpu.roll(rows, 64, 1)], axis=0)


def widen_kernel(own, ahead, behind, up, down):
    for send, a in ((up, 1), (down, 0)):
        for y in range(6):
            source = (ahead, own, behind)[y // 2]
            col = a * 2 + y % 2
            for field in range(4):
                send[y * 4 + field] = source[col * 7 + field]
        for y in range(4):
            source = (ahead, own, own, behind)[y]
            col = a * 2 + (1, 0, 1, 0)[y]
            for field in range(3):
                send[X_VEL + y * 3 + field] = source[col * 7 + 4 + field]
            for field in range(7):
                for slot in range(2):
                    send[X_GRAIN + field, pl.ds(slot * 4 + y, 1), :] = source[
                        Y_GRAIN + field, pl.ds(slot * 4 + col, 1), :
                    ]
        for part, source in enumerate((own, ahead, behind)):
            for side in range(2):
                send[X_RIM + part * 2 + side] = source[Y_RIM + side]


class Near:
    def __init__(self, own, ahead, behind, left, right):
        self.own, self.ahead, self.behind = own, ahead, behind
        self.left, self.right = left, right

    def main(self, field, x, y):
        if x in (1, 2):
            source = (self.ahead, self.own, self.behind)[y // 2]
            return source[((x - 1) * 2 + y % 2) * 7 + field]
        source = self.left if x == 0 else self.right
        if field < 4:
            return source[y * 4 + field]
        return source[X_VEL + (y - 1) * 3 + field - 4]

    def rim(self, side, x, y):
        part = (1, 0, 2)[y // 2]
        if x in (1, 2):
            return (self.own, self.ahead, self.behind)[part][Y_RIM + side]
        source = self.left if x == 0 else self.right
        return source[X_RIM + part * 2 + side]

    def rim_col(self, x, y):
        return (1, 0, 1, 0)[x] * 2 + y % 2


class Columns:
    def __init__(self, data, near, has_left=None, has_right=None):
        self.data, self.near = data, near
        self.there = {0: has_left, 3: has_right}
        self.lane = lanes()
        self.packed = None

    def open_rim(self):
        self.packed = [[jnp.zeros((8, 128), F32) for _ in range(4)] for _ in range(3)]

    def put(self, at, x, y, rim):
        data, lane, packed = self.data, self.lane, self.packed
        col = data.rim_col(x, y)
        rims = [data.rim(side, x, y) for side in range(2)]
        for field in range(4):
            value = data.main(field, x, y)
            edge = [rims[0], rims[1]]
            if field == 3 and x in (0, 3):
                value = jnp.where(self.there[x], value, 0.0)
                edge = [jnp.where(self.there[x], one, 0.0) for one in edge]
            shift = float(x - 1) if field == 0 else float(y - 2) if field == 1 else 0.0
            if shift:
                value = value + shift
                edge = [one + shift for one in edge]
            back = jnp.where(
                lane == 0, roll(edge[0], -rim_lane(field, 1, col)), roll(value, 1)
            )
            fore = jnp.where(
                lane == 127, roll(edge[1], 127 - rim_lane(field, 0, col)), roll(value, 127)
            )
            if field == 2:
                back = back - 1.0
                fore = fore + 1.0
            self.near[at * 12 + field] = back
            self.near[at * 12 + 4 + field] = value
            self.near[at * 12 + 8 + field] = fore
            if not rim:
                continue
            for side in range(2):
                spot = side * 64 + x * 8 + y
                here = lane == spot
                outer = rim_lane(field, 0 if side == 0 else 1, col)
                inner = rim_lane(field, 1 if side == 0 else 0, col)
                packed[0][field] = jnp.where(here, roll(edge[side], spot - outer), packed[0][field])
                packed[1][field] = jnp.where(here, roll(edge[side], spot - inner), packed[1][field])
                packed[2][field] = jnp.where(
                    here, roll(value, spot - (0 if side == 0 else 127)), packed[2][field]
                )

    def close_rim(self):
        sign = jnp.where(self.lane < 64, -1.0, 1.0)
        self.packed[0][2] = self.packed[0][2] + sign
        self.packed[2][2] = self.packed[2][2] - sign

    def put_rim(self, at, moved):
        for level in range(3):
            for field in range(4):
                self.near[at * 12 + level * 4 + field] = moved(self.packed[level][field])


def place_of(data, x, y):
    value = [data.main(field, x, y) for field in range(4)]
    if x != 1:
        value[0] = value[0] + float(x - 1)
    if y != 2:
        value[1] = value[1] + float(y - 2)
    return value


def add_columns(near, table, start, targets, width, center_ref, total_ref):
    def one_column(number, carry):
        target = table[start + number * (width + 1)]
        center = [center_ref[target * 4 + field] for field in range(3)]

        def one_neighbour(step, total):
            base = table[start + number * (width + 1) + 1 + step] * 12
            for level in range(3):
                for slot in range(8):
                    row = [
                        spread(near[base + level * 4 + field, pl.ds(slot, 1), :])
                        for field in range(4)
                    ]
                    dx = center[0] - row[0]
                    dy = center[1] - row[1]
                    dz = center[2] - row[2]
                    square = jnp.maximum(dx * dx + dy * dy + dz * dz, TINY)
                    radius = square * lax.rsqrt(square)
                    reach = jnp.maximum(1.0 - radius, 0.0)
                    squared = reach * reach
                    total = total + (squared * squared) * ((1.25 - reach) * row[3])
            return total

        total_ref[target] = lax.fori_loop(
            0, width, one_neighbour, total_ref[target], unroll=True
        )
        return carry

    lax.fori_loop(0, targets, one_column, 0)


def fill(table, start, rows):
    at = start
    for row in rows:
        for value in row:
            table[at] = value
            at += 1
    return at


def own_density_kernel(own, total, near, center, table):
    data = Near(own, own, own, own, own)
    cols = Columns(data, near)
    rows = []
    for x in range(2):
        for y in range(2):
            cols.put(x * 2 + y, x + 1, y + 2, False)
            target = x * 4 + y + 1
            rows.append([target, 0, 1, 2, 3])
            for field, value in enumerate(place_of(data, x + 1, y + 2)):
                center[target * 4 + field] = value
    fill(table, 0, rows)
    total[...] = jnp.zeros((9, 8, 128), F32)
    add_columns(near, table, 0, 4, 4, center, total)


def mid_density_kernel(own, ahead, behind, start, total, rim_center, near, center, table):
    data = Near(own, ahead, behind, own, own)
    cols = Columns(data, near)
    cols.open_rim()
    for x in range(2):
        for y in range(6):
            cols.put(x * 6 + y, x + 1, y, True)
    cols.close_rim()
    lane = lanes()
    in_first = (lane & 63) < 16
    for step in range(3):
        cols.put_rim(12 + step, lambda v: roll(v, 1 - step))
        cols.put_rim(
            15 + step,
            lambda v: jnp.where(in_first, roll(v, 1 - step - 8), roll(v, 1 - step + 8)),
        )
    for field in range(4):
        center[8 * 4 + field] = cols.packed[1][field]
        rim_center[field] = cols.packed[1][field]
    outer, inner = [], []
    for x in range(2):
        for y in range(4):
            target = x * 4 + y
            for field, value in enumerate(place_of(data, x + 1, y + 1)):
                center[target * 4 + field] = value
            if y in (0, 3):
                outer.append([target] + [sx * 6 + y + dy for sx in range(2) for dy in range(3)])
            else:
                far = 1 if y == 1 else 4
                inner.append([target] + [sx * 6 + far for sx in range(2)])
    outer.append([8] + [12 + k for k in range(6)])
    total[...] = start[...]
    at = fill(table, 0, outer)
    fill(table, at, inner)
    add_columns(near, table, 0, 5, 6, center, total)
    add_columns(near, table, at, 4, 2, center, total)


def far_own_kernel(place, own, ahead, behind, left, right, start, out, near, center, table, total):
    data = Near(own, ahead, behind, left, right)
    cols = Columns(data, near, place[0] > 0, place[0] < 7)
    for x in range(2):
        for y in range(4):
            cols.put(x * 4 + y, x * 3, y + 1, False)
    rows = []
    for x in range(2):
        for y in (1, 2):
            target = x * 4 + y
            for field, value in enumerate(place_of(data, x + 1, y + 1)):
                center[target * 4 + field] = value
            rows.append([target] + [x * 4 + y - 1 + dy for dy in range(3)])
            total[target] = start[target]
    fill(table, 0, rows)
    add_columns(near, table, 0, 4, 3, center, total)
    for x in range(2):
        for y in (1, 2):
            press, inverse, pressure = finish(total[x * 4 + y], center[(x * 4 + y) * 4 + 3])
            at = (x * 2 + y - 1) * 3
            out[at] = press
            out[at + 1] = inverse
            out[at + 2] = pressure


def far_rest_kernel(
    place, own, ahead, behind, left, right, start, rim_center, own_fields, out, near, center, table, total
):
    data = Near(own, ahead, behind, left, right)
    cols = Columns(data, near, place[0] > 0, place[0] < 7)
    cols.open_rim()
    for x in range(2):
        for y in range(6):
            cols.put(x * 6 + y, x * 3, y, True)
    cols.close_rim()
    in_first = (lanes() & 63) < 16
    for step in range(3):
        cols.put_rim(
            12 + step,
            lambda v: jnp.where(in_first, roll(v, 1 - step + 8), roll(v, 1 - step - 8)),
        )
    rows = []
    for x in range(2):
        for y in (0, 3):
            target = x * 4 + y
            for field, value in enumerate(place_of(data, x + 1, y + 1)):
                center[target * 4 + field] = value
            rows.append([target] + [x * 6 + y + dy for dy in range(3)])
            total[target] = start[target]
    for field in range(4):
        center[8 * 4 + field] = rim_center[field]
    total[8] = start[8]
    rows.append([8, 12, 13, 14])
    fill(table, 0, rows)
    add_columns(near, table, 0, 5, 3, center, total)
    for target in (0, 3, 4, 7, 8):
        press, inverse, _ = finish(total[target], center[target * 4 + 3])
        out[target * 2] = press
        out[target * 2 + 1] = inverse
    for x in range(2):
        for y in range(2):
            for k in range(2):
                out[(x * 4 + y + 1) * 2 + k] = own_fields[(x * 2 + y) * 3 + k]


def finish(total, mass):
    density = (4.0 * NORMING) * total
    alive = mass > 0.0
    live = jnp.where(alive, 1.0, 0.0)
    safe = jnp.where(alive, density, 1.0)
    pressure = (density - REST_DENSITY) * live
    return pressure / (safe * safe), live / safe, pressure


def force_kernel(place, own, ahead, behind, left, right, fields, fleft, fright, reaction, out, near):
    lane = lanes()
    first = lane == 0
    last = lane == 127
    data = Near(own, ahead, behind, left, right)
    has_left = place[0] > 0
    has_right = place[0] < 7
    for x in range(4):
        for y in range(1, 5):
            col = data.rim_col(x, y)
            rims = [data.rim(side, x, y) for side in range(2)]
            source = fields if x in (1, 2) else fleft if x == 0 else fright
            far_x = (1, 0, 1, 0)[x]
            target = far_x * 4 + y - 1
            extra = []
            for which in range(2):
                value = source[target * 2 + which]
                halo = source[16 + which]
                extra.append((value, halo))
            levels = [[], [], []]
            for field in range(7):
                value = data.main(field, x, y)
                edge = [rims[0], rims[1]]
                if field == 3 and x in (0, 3):
                    there = has_left if x == 0 else has_right
                    value = jnp.where(there, value, 0.0)
                    edge = [jnp.where(there, one, 0.0) for one in edge]
                back = jnp.where(first, roll(edge[0], -rim_lane(field, 1, col)), roll(value, 1))
                fore = jnp.where(last, roll(edge[1], 127 - rim_lane(field, 0, col)), roll(value, 127))
                shift = float(x - 1) if field == 0 else float(y - 2) if field == 1 else 0.0
                if shift:
                    value, back, fore = value + shift, back + shift, fore + shift
                if field == 2:
                    back = back - 1.0
                    fore = fore + 1.0
                for level, one in enumerate((back, value, fore)):
                    levels[level].append(one)
            spot = (far_x + 1) * 8 + y
            for value, halo in extra:
                back = jnp.where(first, roll(halo, -spot), roll(value, 1))
                fore = jnp.where(last, roll(halo, 127 - 64 - spot), roll(value, 127))
                for level, one in enumerate((back, value, fore)):
                    levels[level].append(one)
            for level in range(3):
                px, py, pz, m, vx, vy, vz, press, inverse = levels[level]
                at = ((x * 4 + y - 1) * 3 + level) * 9
                for k, one in enumerate((px, py, pz, m, m * press, m * inverse, vx, vy, vz)):
                    near[at + k] = one

    def one_column(target, carry):
        a = target // 2
        b = target % 2
        middle = (((a + 1) * 4 + b + 1) * 3 + 1) * 9
        center = [near[middle + k] for k in range(3)]
        press = fields[(a * 4 + b + 1) * 2]
        inverse = fields[(a * 4 + b + 1) * 2 + 1]

        def one_neighbour(step, total):
            base = (((a + step // 3) * 4 + b + step % 3) * 3) * 9
            total = list(total)
            for level in range(3):
                for slot in range(8):
                    row = [
                        spread(near[base + level * 9 + k, pl.ds(slot, 1), :]) for k in range(9)
                    ]
                    dx = center[0] - row[0]
                    dy = center[1] - row[1]
                    dz = center[2] - row[2]
                    square = dx * dx + dy * dy + dz * dz
                    guarded = jnp.maximum(square, TINY)
                    radius = guarded * lax.rsqrt(guarded)
                    reach = jnp.maximum(1.0 - radius, 0.0)
                    cubed = reach * reach * reach
                    push = cubed * (row[3] * press + row[4])
                    soft = pltpu.reciprocal(square + SOFTENING, approx=True)
                    drag = (cubed * row[5]) * (square * soft)
                    total[0] = total[0] + push * dx
                    total[1] = total[1] + push * dy
                    total[2] = total[2] + push * dz
                    total[3] = total[3] + drag
                    total[4] = total[4] + drag * row[6]
                    total[5] = total[5] + drag * row[7]
                    total[6] = total[6] + drag * row[8]
            return tuple(total)

        zero = jnp.zeros((8, 128), F32)
        total = lax.fori_loop(0, 9, one_neighbour, (zero,) * 7, unroll=True)
        live = jnp.where(near[middle + 3] > 0.0, 1.0, 0.0)
        for d in range(3):
            slow = inverse * (near[middle + 6 + d] * total[3] - total[4 + d])
            force = 20.0 * NORMING * (total[d] - slow)
            if d == 2:
                force = force - GRAVITY
            out[pl.ds(d * 32 + target, 8, stride=4), :] = live * force + reaction[d * 4 + target]
        return carry

    lax.fori_loop(0, 4, one_column, 0)


def pair_kernel(own, fields, arrived, cells, send, reaction, left, hot):
    for peer in range(16):
        index = cells[pl.ds(peer, 1), :]
        at_row = index & 127
        at = spread(at_row)
        col_of = spread(index >> 7)
        found = None
        for col in range(4):
            mid = col * 3
            inverse = fields[mid + 1]
            tables = [own[col * 7 + k] for k in (0, 1, 2, 4, 5, 6)]
            tables += [own[col * 7 + 3] * inverse, fields[mid + 2], inverse]
            got = [lane_gather(one, at) for one in tables]
            if found is None:
                found = got
            else:
                here = col_of == col
                found = [jnp.where(here, new, old) for new, old in zip(got, found)]
        row = [spread(arrived[peer * 3 + k // 4, pl.ds(k % 4, 1), :]) for k in range(7)]
        delta = [row[d] - found[d] for d in range(3)]
        square = jnp.maximum(delta[0] * delta[0] + delta[1] * delta[1] + delta[2] * delta[2], TINY)
        radius = square * lax.rsqrt(square)
        reach = jnp.maximum(1.0 - radius, 0.0)
        cubed = reach * reach * reach
        weight = (DRAG_RATE * NORMING) * cubed * reach * (4.0 * radius + 1.0)
        push = (20.0 * NORMING) * found[7] * cubed
        hot[:, peer * 128 : peer * 128 + 128] = hot_rows(at_row)
        for d in range(3):
            bracket = row[6] * (push * delta[d] + weight * (found[3 + d] - row[3 + d]))
            send[peer, pl.ds(d, 1), :] = jnp.sum(found[6] * bracket, axis=0, keepdims=True)
            both = split_rows(-found[8] * bracket)
            col_both = jnp.concatenate([col_of, col_of], axis=0)
            for col in range(4):
                at16 = (d * 4 + col) * 16
                left[at16 : at16 + 16, peer * 128 : peer * 128 + 128] = jnp.where(
                    col_both == col, both, 0.0
                ).astype(BF16)
        send[peer, pl.ds(3, 1), :] = jnp.zeros((1, 128), F32)
    sums = scatter_dot(left[...], hot[...])
    for k in range(12):
        reaction[k] = sums[k * 16 : k * 16 + 8] + sums[k * 16 + 8 : k * 16 + 16]


def contact_kernel(place, live_count, own, ahead, behind, left, right, listed, out, rims, turned, rows, lhs, hot):
    lane = lanes()
    sub = subs()
    has_left = place[0] > 0
    has_right = place[0] < 7
    def far_line(field, row):
        slot, x, y = row // 16, row // 4 % 4, row % 4
        if x in (1, 2):
            source = (ahead, own, own, behind)[y]
            at = slot * 4 + (x - 1) * 2 + (1, 0, 1, 0)[y]
            return source[Y_GRAIN + field, pl.ds(at, 1), :]
        source = left if x == 0 else right
        return source[X_GRAIN + field, pl.ds(slot * 4 + y, 1), :]

    for side in range(2):
        rims[...] = jnp.zeros((128, 128), F32)
        for part, source in enumerate((own, ahead, behind)):
            rims[pl.ds(part * 8, 8), :] = source[Y_RIM + side]
            rims[pl.ds((3 + part) * 8, 8), :] = jnp.where(
                has_left, left[X_RIM + part * 2 + side], 0.0
            )
            rims[pl.ds((6 + part) * 8, 8), :] = jnp.where(
                has_right, right[X_RIM + part * 2 + side], 0.0
            )
        turned[side] = jnp.transpose(rims[...])

    def one_group(group):
        start = group * 8
        one = listed[pl.ds(start, 8), :]
        two = listed[pl.ds(start + 48, 8), :]
        own_row = one >> 7
        own_c = one & 127
        far_row = (two * 4033) >> 19
        far_c = two - far_row * 130
        far_slot = far_row >> 4
        far_x = (far_row >> 2) & 3
        far_y = far_row & 3
        far_at = jnp.clip(far_c - 1, 0, 127)
        x_part = jnp.where(far_x == 0, 1, jnp.where(far_x == 3, 2, 0))
        y_part = jnp.where(far_y == 0, 1, jnp.where(far_y == 3, 2, 0))
        rim_a = jnp.where(far_x == 0, 1, jnp.where(far_x == 3, 0, far_x - 1))
        rim_b = jnp.where(far_y == 0, 1, jnp.where(far_y == 3, 0, far_y - 1))
        rim_at = (x_part * 3 + y_part) * 8 + far_slot * 4 + rim_a * 2 + rim_b
        own_found = [jnp.zeros((8, 128), F32) for _ in range(7)]
        for row in range(8):
            here = own_row == row
            for field in range(7):
                got = lane_gather(spread(own[Y_GRAIN + field, pl.ds(row, 1), :]), own_c)
                own_found[field] = jnp.where(here, got, own_found[field])
        far_found = [jnp.zeros((8, 128), F32) for _ in range(7)]
        for row in range(32):
            here = far_row == row
            if row // 4 % 4 in (0, 3):
                here = jnp.logical_and(here, has_left if row // 4 % 4 == 0 else has_right)
            for field in range(7):
                got = lane_gather(spread(far_line(field, row)), far_at)
                far_found[field] = jnp.where(here, got, far_found[field])
        for side, edge in ((0, 0), (1, 129)):
            here = far_c == edge
            for field in range(7):
                got = lane_gather(
                    spread(turned[side, pl.ds(GRAIN_LANE + field, 1), :]), rim_at
                )
                far_found[field] = jnp.where(here, got, far_found[field])
        shift = [
            (((own_row >> 1) & 1) - far_x + 1).astype(F32),
            ((own_row & 1) - far_y + 1).astype(F32),
            (own_c - far_c + 1).astype(F32),
        ]
        delta = [own_found[d] - far_found[d] + shift[d] for d in range(3)]
        distance = jnp.sqrt(
            delta[0] * delta[0] + delta[1] * delta[1] + delta[2] * delta[2] + SOFTENING
        )
        normal = [one_delta / distance for one_delta in delta]
        both = own_found[6] + far_found[6]
        overlap = (both - distance) / SOFT_WIDTH
        stiff = SPRING * own_found[6] * far_found[6] / both
        closing = sum((own_found[3 + d] - far_found[3 + d]) * normal[d] for d in range(3))
        soft = jnp.maximum(overlap, 0.0) + jnp.log1p(jnp.exp(-jnp.abs(overlap)))
        number = group * 1024 + sub * 128 + lane
        magnitude = jnp.where(
            number < live_count[0], stiff * (SOFT_WIDTH * soft - DAMPING * closing), 0.0
        )
        force = [magnitude * normal[d] for d in range(3)]
        values = force + [
            force[0] * normal[0],
            force[1] * normal[1],
            force[2] * normal[2],
            force[0] * normal[1],
            force[0] * normal[2],
            force[1] * normal[2],
        ]
        for k in range(9):
            high = values[k].astype(BF16).astype(F32)
            rows[group, pl.ds(k * 16, 8), :] = high
            rows[group, pl.ds(k * 16 + 8, 8), :] = values[k] - high
        for s in range(8):
            at = pl.ds((group * 8 + s) * 128, 128)
            mine = spread(own_row[s : s + 1]) == sub
            hot[:, at] = hot_rows(own_c[s : s + 1])
            for k in range(9):
                high = spread(rows[group, pl.ds(k * 16 + s, 1), :])
                low = spread(rows[group, pl.ds(k * 16 + 8 + s, 1), :])
                pair = jnp.concatenate(
                    [jnp.where(mine, high, 0.0), jnp.where(mine, low, 0.0)], axis=0
                )
                lhs[k * 16 : k * 16 + 16, at] = pair.astype(BF16)

    for group in range(6):
        one_group(group)
    sums = scatter_dot(lhs[...], hot[...])
    for k in range(9):
        out[k] = sums[k * 16 : k * 16 + 8] + sums[k * 16 + 8 : k * 16 + 16]


def grain_kernel(back, grain, contact, radius_ref, force_out, stress_out, lhs, hot):
    sub = subs()
    for peer in range(16):
        index = grain[pl.ds(peer, 1), :]
        mine = spread(index >> 7) == sub
        hot[:, peer * 128 : peer * 128 + 128] = hot_rows(index & 127)
        for d in range(3):
            value = jnp.where(mine, spread(back[peer, pl.ds(d, 1), :]), 0.0)
            lhs[d * 16 : d * 16 + 16, peer * 128 : peer * 128 + 128] = split_rows(value).astype(BF16)
    sums = scatter_dot(lhs[...], hot[...])
    radius = radius_ref[...]
    volume = VOLUME_FACTOR * radius * radius * radius
    for d in range(3):
        value = contact[d] + (sums[d * 16 : d * 16 + 8] + sums[d * 16 + 8 : d * 16 + 16])
        if d == 2:
            value = value - GRAIN_WEIGHT * volume
        force_out[pl.ds(d * 8, 8), :] = value
    scale = radius / volume
    for k in range(6):
        stress_out[pl.ds(k * 8, 8), :] = -contact[3 + k] * scale


def density_scratch(columns):
    return [
        pltpu.VMEM((columns * 12, 8, 128), F32),
        pltpu.VMEM((36, 8, 128), F32),
        pltpu.SMEM((64,), jnp.int32),
    ]


def along_y(value, step):
    count = lax.axis_size("gy")
    pairs = [(i, i + step) for i in range(count) if 0 <= i + step < count]
    return lax.ppermute(value, "gy", pairs)


def along_x(value, step):
    count = lax.axis_size("gx")
    return lax.ppermute(value, "gx", [(i, (i + step) % count) for i in range(count)])


def body(
    sph_pos,
    sph_vel,
    sph_mass,
    cell_count,
    grain_pos,
    grain_vel,
    grain_radius,
    contact_pairs,
    contact_count,
    iface_grain,
    iface_offset,
    pair_count,
    iface_cell,
):
    place = jnp.stack(
        [lax.axis_index("gx"), lax.axis_index("gy"), lax.axis_index("gz")]
    ).astype(jnp.int32)
    radius = grain_radius.reshape(8, 128)
    route_grain = iface_grain.reshape(16, 128)
    bricks = (
        sph_pos.reshape(96, 128),
        sph_vel.reshape(96, 128),
        sph_mass.reshape(32, 128),
        cell_count.reshape(4, 128),
        grain_pos.reshape(24, 128),
        grain_vel.reshape(24, 128),
        radius,
    )
    send = call(
        pack_kernel,
        shape(192, 128),
        ins=[S] + [pl.BlockSpec(memory_space=pltpu.HBM)] * 9,
        scratch=[pltpu.VMEM((rows, 128), F32) for rows in (96, 96, 32)]
        + [pltpu.VMEM((4, 128), jnp.int32)]
        + [pltpu.VMEM((rows, 128), F32) for rows in (24, 24, 8)]
        + [pltpu.VMEM((16, 128), jnp.int32), pltpu.VMEM((48, 128), F32)]
        + [pltpu.SemaphoreType.DMA((9,))],
        cost=cost(3),
        limit=None,
    )(pair_count.reshape(16), *bricks, route_grain, iface_offset.reshape(48, 128))
    later = lax.optimization_barrier((send,) + bricks)
    send, bricks = later[0], later[1:]
    own = call(gather_kernel, shape(Y_TILES, 8, 128), ins=[V] * 7, cost=cost(1))(*bricks)
    arrived = lax.all_to_all(
        send.reshape(16, 3, 4, 128), "gz", split_axis=0, concat_axis=0, tiled=True
    ).reshape(48, 4, 128)
    own = call(
        rim_kernel,
        shape(Y_TILES, 8, 128),
        ins=[S, V, pl.BlockSpec(memory_space=pl.ANY)],
        alias={2: 0},
        grid=(2,),
        out_specs=[pl.BlockSpec((1, 8, 128), lambda i: (Y_RIM + i, 0, 0))],
        cost=cost(1),
    )(place, arrived, own)
    ahead = along_y(own, 1)
    behind = along_y(own, -1)
    own_total = call(
        own_density_kernel,
        shape(9, 8, 128),
        ins=[V],
        scratch=density_scratch(4),
        cost=cost(3),
    )(own)
    ahead, behind, own_total = lax.optimization_barrier((ahead, behind, own_total))
    up, down = call(
        widen_kernel,
        [shape(X_TILES, 8, 128)] * 2,
        ins=[V] * 3,
        cost=cost(1),
    )(own, ahead, behind)
    left = along_x(up, 1)
    right = along_x(down, -1)
    mid_total, rim_center = call(
        mid_density_kernel,
        [shape(9, 8, 128), shape(4, 8, 128)],
        ins=[V] * 4,
        scratch=density_scratch(18),
        cost=cost(6),
    )(own, ahead, behind, own_total)
    own_fields = call(
        far_own_kernel,
        shape(12, 8, 128),
        ins=[S] + [V] * 6,
        scratch=density_scratch(8) + [pltpu.VMEM((9, 8, 128), F32)],
        cost=cost(2),
    )(place, own, ahead, behind, left, right, mid_total)
    send_back, reaction = call(
        pair_kernel,
        [shape(16, 4, 128), shape(12, 8, 128)],
        ins=[V] * 4,
        scratch=[pltpu.VMEM((192, 2048), BF16), pltpu.VMEM((128, 2048), BF16)],
        cost=cost(3),
    )(own, own_fields, arrived, iface_cell.reshape(16, 128))
    fields = call(
        far_rest_kernel,
        shape(18, 8, 128),
        ins=[S] + [V] * 8,
        scratch=density_scratch(15) + [pltpu.VMEM((9, 8, 128), F32)],
        cost=cost(3),
    )(place, own, ahead, behind, left, right, mid_total, rim_center, own_fields)
    fields_left = along_x(fields, 1)
    fields_right = along_x(fields, -1)
    back = lax.all_to_all(send_back, "gz", split_axis=0, concat_axis=0, tiled=True)
    contact = call(
        contact_kernel,
        shape(9, 8, 128),
        ins=[S, S] + [V] * 6,
        scratch=[
            pltpu.VMEM((128, 128), F32),
            pltpu.VMEM((2, 128, 128), F32),
            pltpu.VMEM((6, 144, 128), F32),
            pltpu.VMEM((144, 6144), BF16),
            pltpu.VMEM((128, 6144), BF16),
        ],
        cost=cost(6),
    )(
        place,
        contact_count.reshape(1),
        own,
        ahead,
        behind,
        left,
        right,
        contact_pairs.reshape(96, 128),
    )
    accel = call(
        force_kernel,
        shape(96, 128),
        ins=[S] + [V] * 9,
        scratch=[pltpu.VMEM((16 * 27, 8, 128), F32)],
        cost=cost(6),
    )(place, own, ahead, behind, left, right, fields, fields_left, fields_right, reaction)
    grain_force, grain_stress = call(
        grain_kernel,
        [shape(24, 128), shape(48, 128)],
        ins=[V] * 4,
        scratch=[pltpu.VMEM((48, 2048), BF16), pltpu.VMEM((128, 2048), BF16)],
        cost=cost(2),
    )(back, route_grain, contact, radius)
    return (
        accel.reshape(sph_pos.shape),
        grain_force.reshape(grain_pos.shape),
        grain_stress.reshape((6,) + grain_radius.shape),
    )


def solution(mesh):
    return jax.shard_map(
        body,
        mesh=mesh,
        in_specs=(
            P(None, None, "gx", "gy", "gz"),
            P(None, None, "gx", "gy", "gz"),
            P(None, "gx", "gy", "gz"),
            P("gx", "gy", "gz"),
            P(None, None, "gx", "gy", "gz"),
            P(None, None, "gx", "gy", "gz"),
            P(None, "gx", "gy", "gz"),
            P(None, "gx", "gy", "gz"),
            P("gx", "gy", "gz"),
            P("gx", "gy", "gz", None),
            P(None, "gx", "gy", "gz", None),
            P("gx", "gy", "gz"),
            P("gx", "gy", "gz", None),
        ),
        out_specs=(
            P(None, None, "gx", "gy", "gz"),
            P(None, None, "gx", "gy", "gz"),
            P(None, None, "gx", "gy", "gz"),
        ),
        check_vma=False,
    )
```
